32 devices in a mesh: head: 2 (over x), ctx: 16 (over z, y, core).
Axes of the slice: x: 2, y: 2, z: 4, core: 2. Of those that a mesh axis runs over, the one named last changes fastest.
Arguments:
- queries: bfloat16 [2, 16, 1024, 128], P('head', 'ctx'), may hold values from -72 to 72
- keys: bfloat16 [2, 65536, 128], P('head', 'ctx'), may hold values from -24 to 24
- values: bfloat16 [2, 65536, 128], P('head', 'ctx'), may hold values from -6 to 6
- kept: int32 [2, 512], P('head'), may hold values from 0 to 65535, as said below
- roots: int32 [2], P('head'), may hold values from 0 to 15
Outputs:
- compact: float32 [2, 512, 128], P('head')
- fit_error: float32 [], replicated
The draws below stay inside these ranges and needn't reach their ends.
Inputs may be any that keep to these rules, and one draw needn't show every extreme that they name: `kept`: per head: 512 distinct increasing positions; at most 128 of them lie within one context device's 4096 positions, and exactly 128 within at least one such device.
All inputs are finite; a program needn't handle non-finite values.
Results may differ from the reference program's by a relative error of at most 0.0003.
Values may be sent and summed in bfloat16 or wider, within the bound.
No kernel may reach another device: no remote copies, remote signals or barrier semaphores. Data moves between devices by JAX's collectives and lax.ppermute only.
A program may use at most 64 MiB of HBM per device.

```python
import math
import jax
import jax.numpy as jnp
from jax import lax

HD = 128
R = 1024
SLAB = 4096
KBLK = 1024
M = 512
HEADS = 2
S = 65536
CAP = 128
N_CTX = 16


def kept_positions(base):
    keyring = jax.random.split(jax.random.fold_in(base, 11), 4)
    candidates = N_CTX * CAP
    noise = jax.random.randint(keyring[0], (HEADS, candidates), 0, 4096)
    weight = jax.random.randint(keyring[1], (HEADS, N_CTX), 1, 5)
    busiest = jax.random.randint(keyring[2], (HEADS, 1), 0, N_CTX)
    shard_of = jnp.arange(candidates, dtype=jnp.int32) // CAP
    score = noise * jnp.take(weight, shard_of, axis=1) + jnp.where(shard_of[None, :] == busiest, 65536, 0)
    score = score * candidates + jnp.arange(candidates, dtype=jnp.int32)[None, :]
    chosen = lax.top_k(score, M)[1].astype(jnp.int32)
    shuffles = jax.vmap(lambda subkey: jax.random.permutation(subkey, SLAB)[:CAP])(jax.random.split(keyring[3], HEADS * N_CTX))
    offsets = shuffles.reshape(HEADS, candidates).astype(jnp.int32)
    positions = chosen // CAP * SLAB + jnp.take_along_axis(offsets, chosen, axis=1)
    return jnp.sort(positions, axis=1).astype(jnp.int32)


def make_keys(base):
    raw = jax.random.normal(jax.random.fold_in(base, 23), (HEADS, S, HD), jnp.float32)
    spread = 2.5 * 1.6 ** (jnp.arange(HEADS, dtype=jnp.float32) / max(HEADS - 1, 1))
    result = (jnp.clip(raw, -6.0, 6.0) * spread[:, None, None]).astype(jnp.bfloat16).astype(jnp.float32)
    return result


def draw_keys(key, part):
    return make_keys(key).astype(jnp.bfloat16)


def draw_queries(key, part):
    raw = jax.random.normal(jax.random.fold_in(key, 37), (HEADS, N_CTX, R, HD), jnp.float32)
    result = jnp.clip(raw, -6.0, 6.0)
    return result.astype(jnp.bfloat16)


def draw_kept(key, part):
    return kept_positions(key)


def levels(key, shape, cuts, least, high):
    level, own = 1.0, jax.random.fold_in(key, 6)
    for dim, shards_of in cuts:
        steps = jnp.exp(jax.random.uniform(jax.random.fold_in(own, dim), (shards_of,), jnp.float32, least / len(cuts), high / len(cuts)))
        level = level * jnp.repeat(steps, shape[dim] // shards_of).reshape([-1 if axis == dim else 1 for axis in range(len(shape))])
    return level


def gaussian(own_key, dims, width, limit, cuts=(), kind=jnp.bfloat16):
    entries = jax.random.normal(own_key, dims, jnp.float32) * width
    if len(cuts) > 0:
        entries = levels(own_key, dims, cuts, -0.22, 0.18) * entries
    return jnp.clip(entries, min=-limit, max=limit).astype(kind)


def setup_inputs(seed: int = 0) -> dict:
    streams_of = jax.random.split(jax.random.key(seed), 6)
    queries = draw_queries(jax.random.fold_in(streams_of[5], 71), 0)
    keys = draw_keys(jax.random.fold_in(streams_of[5], 71), 0)
    values = gaussian(streams_of[2], (HEADS, S, HD), 1.0, 6.0, ((0, 2), (1, 16)))
    kept = draw_kept(jax.random.fold_in(streams_of[5], 71), 0)
    roots = jax.random.randint(streams_of[4], (HEADS,), 0, N_CTX).astype(jnp.int32)
    return {"queries": queries, "keys": keys, "values": values, "kept": kept, "roots": roots}


ridge_share = 0.01

def merge_parts(first, second):
    first_max, first_sum, first_out = first
    second_max, second_sum, second_out = second
    joint = jnp.maximum(first_max, second_max)
    first_scale = jnp.exp(first_max - joint)
    second_scale = jnp.exp(second_max - joint)
    return (joint, first_sum * first_scale + second_sum * second_scale, first_out * first_scale[:, None] + second_out * second_scale[:, None])

def block_partials(queries_ref, key_all, value_all, score_scale):
    blocks = key_all.shape[0] // KBLK
    key_blocks = key_all.reshape(blocks, KBLK, HD)
    value_blocks = value_all.reshape(blocks, KBLK, HD)
    rows = queries_ref.shape[0]

    def visit(carry, pieces):
        key_block, value_block = pieces
        scores = jnp.einsum('rd,kd->rk', queries_ref.astype(jnp.float32), key_block.astype(jnp.float32), preferred_element_type=jnp.float32) * score_scale
        block_max = lax.optimization_barrier(jnp.max(scores, axis=1))
        weights = jnp.exp(scores - block_max[:, None]).astype(jnp.bfloat16)
        block_sum = lax.optimization_barrier(jnp.sum(weights.astype(jnp.float32), axis=1))
        block_out = jnp.dot(weights.astype(jnp.float32), value_block.astype(jnp.float32), preferred_element_type=jnp.float32)
        return (merge_parts(carry, (block_max, block_sum, block_out)), None)
    start = (jnp.full((rows,), -jnp.inf, jnp.float32), jnp.zeros((rows,), jnp.float32), jnp.zeros((rows, HD), jnp.float32))
    return lax.scan(visit, start, (key_blocks, value_blocks))[0]

def compact_softmax(queries_ref, compact_keys, score_scale):
    scores = jnp.einsum('rd,md->rm', queries_ref.astype(jnp.float32), compact_keys.astype(jnp.float32), preferred_element_type=jnp.float32) * score_scale
    return jax.nn.softmax(scores, axis=1)

def inner_left(left, right):
    return lax.dot_general(left.astype(jnp.float32), right.astype(jnp.float32), (((0,), (0,)), ((), ())), precision=lax.Precision.HIGHEST, preferred_element_type=jnp.float32)

def one_head(inputs):
    query_sets, key_all, value_all, kept_rows, root_row = inputs
    score_scale = 1.0 / math.sqrt(HD)
    queries_ref = lax.dynamic_index_in_dim(query_sets, root_row.astype(jnp.int32), 0, keepdims=False)
    run_max, run_sum, run_out = block_partials(queries_ref, key_all, value_all, score_scale)
    target = run_out / run_sum[:, None]
    compact_keys = jnp.take(key_all, kept_rows.astype(jnp.int32), axis=0)
    attend = compact_softmax(queries_ref, compact_keys, score_scale)
    gram = inner_left(attend, attend)
    cross = inner_left(attend, target)
    ridge = ridge_share * jnp.trace(gram) / M
    system = gram + ridge * jnp.eye(M, dtype=jnp.float32)
    factor_low = jnp.linalg.cholesky(system)
    halfway = lax.linalg.triangular_solve(factor_low, cross, left_side=True, lower=True)
    compact = lax.linalg.triangular_solve(factor_low, halfway, left_side=True, lower=True, transpose_a=True)
    fitted = jnp.dot(attend.astype(jnp.float32), compact.astype(jnp.float32), precision=lax.Precision.HIGHEST, preferred_element_type=jnp.float32)
    misfit = fitted - target
    head_error = jnp.sum(misfit * misfit) / jnp.sum(target * target)
    return (compact, head_error)

def reference(queries, keys, values, kept, roots):
    compact, errors = lax.map(one_head, (queries, keys, values, kept, roots))
    return (compact, jnp.mean(errors))
```

```python
import functools
import math

import jax
import jax.numpy as jnp
from jax import lax
from jax.experimental import pallas as pl
from jax.experimental.pallas import tpu as pltpu
from jax.sharding import PartitionSpec as P

KBLK = 1024
PANEL = 128
SUB = 8
RIDGE_SHARE = 0.01
F32 = jnp.float32
BF16 = jnp.bfloat16
HIGH = lax.Precision.HIGHEST
VMEM_LIMIT = 48 * 1024 * 1024
VMEM = pl.BlockSpec(memory_space=pltpu.VMEM)
SMEM = pl.BlockSpec(memory_space=pltpu.SMEM)
NT = (((1,), (1,)), ((), ()))
TN = (((0,), (0,)), ((), ()))
NN = (((1,), (0,)), ((), ()))


def params(**extra):
    return pltpu.CompilerParams(vmem_limit_bytes=VMEM_LIMIT, **extra)


def swap(array, axis, step):
    size = lax.axis_size(axis)
    return lax.ppermute(array, axis, [(i, i ^ step) for i in range(size)])


def swaps(arrays, axis, stride):
    return [arrays[0]] + [swap(x, axis, t * stride) for t, x in enumerate(arrays) if t]


def choose(arrays, which):
    result = arrays[0]
    for t, array in enumerate(arrays[1:], 1):
        result = jnp.where(which == t, array, result)
    return result


def attention_kernel(pieces, score_scale, *refs):
    q_refs, (k_ref, v_ref), o_refs = refs[:pieces], refs[pieces : pieces + 2], refs[pieces + 2 : 2 * pieces + 2]
    vt_ref = refs[-1]
    step = pl.program_id(0)
    dims = v_ref.shape[1]
    keys = k_ref.shape[0]
    vt_ref[:dims, :] = v_ref[...].T
    vt_ref[dims:, :] = jnp.ones((vt_ref.shape[0] - dims, keys), BF16)
    factor = score_scale * math.log2(math.e)

    @pl.when(step == 0)
    def _():
        for o_ref in o_refs:
            o_ref[...] = jnp.zeros_like(o_ref)
            o_ref[dims : dims + 1, :] = jnp.full((1, o_ref.shape[1]), -jnp.inf, F32)

    for q_ref, o_ref in zip(q_refs, o_refs):
        s = lax.dot_general(k_ref[...], q_ref[...], NT, preferred_element_type=F32)
        top = jnp.max(s, axis=0, keepdims=True)
        e = jnp.exp2((s - top) * factor).astype(BF16)
        out = lax.dot_general(vt_ref[...], e, NN, preferred_element_type=F32)
        block_sum = out[dims : dims + 1, :]
        top = top * factor
        old_top = o_ref[dims : dims + 1, :]
        joint = jnp.maximum(old_top, top)
        old_scale = jnp.exp2(old_top - joint)
        new_scale = jnp.exp2(top - joint)
        o_ref[:dims, :] = o_ref[:dims, :] * old_scale + out[:dims, :] * new_scale
        o_ref[dims + 1 : dims + 2, :] = o_ref[dims + 1 : dims + 2, :] * old_scale + block_sum * new_scale
        o_ref[dims : dims + 1, :] = joint


def attention(q_pieces, keys, values, score_scale):
    pieces = len(q_pieces)
    rows, dims = q_pieces[0].shape
    slab = keys.shape[0]
    block = min(KBLK, slab)
    full = lambda shape: pl.BlockSpec(shape, lambda b: (0, 0))
    return pl.pallas_call(
        functools.partial(attention_kernel, pieces, score_scale),
        grid=(slab // block,),
        in_specs=[full((rows, dims))] * pieces + [pl.BlockSpec((block, dims), lambda b: (b, 0))] * 2,
        out_specs=[full((dims + SUB, rows))] * pieces,
        out_shape=[jax.ShapeDtypeStruct((dims + SUB, rows), F32)] * pieces,
        scratch_shapes=[pltpu.VMEM((dims + 16, block), BF16)],
        compiler_params=params(),
        cost_estimate=pl.CostEstimate(
            flops=4 * pieces * rows * slab * dims, bytes_accessed=4 * slab * dims, transcendentals=pieces * rows * slab
        ),
        name="attention",
    )(*q_pieces, keys, values)


def joined(refs, dims):
    tops = [ref[dims : dims + 1, :] for ref in refs]
    top = functools.reduce(jnp.maximum, tops)
    scales = [jnp.exp2(t - top) for t in tops]
    total = sum(ref[dims + 1 : dims + 2, :] * w for ref, w in zip(refs, scales))
    return top, total, scales


def merge_kernel(ways, place_ref, *refs):
    ins, outs = refs[:ways], refs[ways:-1]
    acc = refs[-1]
    dims = ins[0].shape[0] - SUB
    top, total, scales = joined(ins, dims)
    acc[...] = sum(ref[:dims, :] * w for ref, w in zip(ins, scales))
    rows = dims // len(outs)
    for t, out in enumerate(outs):
        start = pl.multiple_of((place_ref[0] ^ t) * rows, SUB)
        out[:rows, :] = acc[pl.ds(start, rows), :]
        out[rows:, :] = jnp.zeros((SUB, out.shape[1]), F32)
        out[rows : rows + 1, :] = top
        out[rows + 1 : rows + 2, :] = total


def merge(parts, place, groups):
    dims, rows = parts[0].shape[0] - SUB, parts[0].shape[1]
    return pl.pallas_call(
        functools.partial(merge_kernel, len(parts)),
        in_specs=[SMEM] + [VMEM] * len(parts),
        out_specs=[VMEM] * groups,
        out_shape=[jax.ShapeDtypeStruct((dims // groups + SUB, rows), F32)] * groups,
        scratch_shapes=[pltpu.VMEM((dims, rows), F32)],
        compiler_params=params(),
        cost_estimate=pl.CostEstimate(flops=10**6, bytes_accessed=10**6, transcendentals=0),
        name="merge",
    )(place, *parts)


def finish_kernel(*refs):
    ins, out = refs[:-1], refs[-1]
    dims = out.shape[0]
    _, total, scales = joined(ins, dims)
    out[...] = sum(ref[:dims, :] * (w / total) for ref, w in zip(ins, scales))


def finish(parts):
    dims, rows = parts[0].shape[0] - SUB, parts[0].shape[1]
    return pl.pallas_call(
        finish_kernel,
        in_specs=[VMEM] * len(parts),
        out_specs=VMEM,
        out_shape=jax.ShapeDtypeStruct((dims, rows), F32),
        compiler_params=params(),
        cost_estimate=pl.CostEstimate(flops=10**6, bytes_accessed=10**6, transcendentals=0),
        name="finish",
    )(*parts)


def stack_kernel(place_ref, *refs):
    ins, out = refs[:-1], refs[-1]
    rows = ins[0].shape[0]
    for t, ref in enumerate(ins):
        start = pl.multiple_of((place_ref[0] ^ t) * rows, SUB)
        out[pl.ds(start, rows), :] = ref[...]


def stack(parts, place):
    rows, cols = parts[0].shape
    return pl.pallas_call(
        stack_kernel,
        in_specs=[SMEM] + [VMEM] * len(parts),
        out_specs=VMEM,
        out_shape=jax.ShapeDtypeStruct((rows * len(parts), cols), parts[0].dtype),
        compiler_params=params(),
        cost_estimate=pl.CostEstimate(flops=10**6, bytes_accessed=10**6, transcendentals=0),
        name="stack",
    )(place, *parts)


def gram_kernel(lo, score_scale, place_ref, *refs):
    q_refs, c_refs = refs[:lo], refs[lo : 2 * lo]
    at_ref, h_ref = refs[2 * lo :  2 * lo + 2]
    c_all = refs[-1]
    part = c_refs[0].shape[0]
    for s, c_ref in enumerate(c_refs):
        c_all[pl.ds(pl.multiple_of((place_ref[0] ^ s) * part, 16), part), :] = c_ref[...]
    rows = q_refs[0].shape[0]
    for s, q_ref in enumerate(q_refs):
        scores = lax.dot_general(c_all[...], q_ref[...], NT, preferred_element_type=F32) * score_scale
        weights = jnp.exp(scores - jnp.max(scores, axis=0, keepdims=True))
        weights = weights / jnp.sum(weights, axis=0, keepdims=True)
        at_ref[:, pl.ds(pl.multiple_of((place_ref[0] ^ s) * rows, rows), rows)] = weights
    gram = lax.dot_general(at_ref[...], at_ref[...], NT, precision=HIGH, preferred_element_type=F32)
    kept = gram.shape[0]
    diagonal = lax.broadcasted_iota(jnp.int32, gram.shape, 0) == lax.broadcasted_iota(jnp.int32, gram.shape, 1)
    trace = jnp.sum(jnp.where(diagonal, gram, 0.0))
    h_ref[...] = gram + jnp.where(diagonal, RIDGE_SHARE * trace / kept, 0.0)


def gram_system(q_pieces, c_pieces, place, score_scale):
    lo = len(q_pieces)
    rows = sum(q.shape[0] for q in q_pieces)
    kept = sum(c.shape[0] for c in c_pieces)
    dims = q_pieces[0].shape[1]
    return pl.pallas_call(
        functools.partial(gram_kernel, lo, score_scale),
        in_specs=[SMEM] + [VMEM] * (2 * lo),
        out_specs=[VMEM] * 2,
        out_shape=[jax.ShapeDtypeStruct((kept, rows), F32), jax.ShapeDtypeStruct((kept, kept), F32)],
        scratch_shapes=[pltpu.VMEM((kept, dims), BF16)],
        compiler_params=params(),
        cost_estimate=pl.CostEstimate(flops=12 * rows * kept * kept, bytes_accessed=10**6, transcendentals=rows * kept),
        name="gram",
    )(place, *q_pieces, *c_pieces)


def invert_block(rows):
    count = len(rows)
    size = count * SUB
    lane = lax.broadcasted_iota(jnp.int32, (SUB, size), 1)
    sub = lax.broadcasted_iota(jnp.int32, (SUB, size), 0)
    spread = lambda array, column: jnp.broadcast_to(array[:, column : column + 1], (SUB, size))
    line = lambda array, row: jnp.broadcast_to(array[row : row + 1, :], (SUB, size))
    for k in range(count):
        base = k * SUB
        inside = (lane >= base) & (lane < base + SUB)
        columns = [spread(rows[k], base + j) for j in range(SUB)]
        work = jnp.where(inside, jnp.where(lane - base == sub, 1.0, 0.0), rows[k])
        for j in range(SUB):
            here = sub == j
            inverse = 1.0 / line(columns[j], j)
            step = lambda v: (lambda t: jnp.where(here, t, v - columns[j] * t))(line(v, j) * inverse)
            for i in range(j + 1, SUB):
                columns[i] = step(columns[i])
            work = step(work)
        lines = [line(work, j) for j in range(SUB)]
        updated = []
        for i in range(count):
            if i == k:
                updated.append(work)
                continue
            fresh = jnp.where(inside, 0.0, rows[i])
            for j in range(SUB):
                fresh = fresh - spread(rows[i], base + j) * lines[j]
            updated.append(fresh)
        rows = updated
    return rows


def sweep_kernel(panel, h_ref, out_ref):
    size = h_ref.shape[0]
    at = pl.ds(panel * PANEL, PANEL)
    across = h_ref[at, :]
    block = across[:, panel * PANEL : (panel + 1) * PANEL]
    inverse = jnp.concatenate(
        invert_block([block[i * SUB : (i + 1) * SUB, :] for i in range(PANEL // SUB)]), axis=0
    )
    turned = lax.dot_general(inverse, across, NN, precision=HIGH, preferred_element_type=F32)
    out_ref[...] = h_ref[...] - lax.dot_general(across, turned, TN, precision=HIGH, preferred_element_type=F32)
    out_ref[:, at] = turned.T
    out_ref[at, :] = turned
    out_ref[at, at] = -inverse


def sweep(system, panel):
    size = system.shape[0]
    return pl.pallas_call(
        functools.partial(sweep_kernel, panel),
        in_specs=[VMEM],
        out_specs=VMEM,
        out_shape=jax.ShapeDtypeStruct(system.shape, F32),
        compiler_params=params(),
        cost_estimate=pl.CostEstimate(flops=5 * 10**9, bytes_accessed=4 * size * size, transcendentals=0),
        name="sweep",
    )(system)


def fit_kernel(lo, place_ref, minus_ref, at_ref, *refs):
    y_refs = refs[:lo]
    x_ref, err_ref = refs[lo : lo + 2]
    yt = refs[-1]
    rows = y_refs[0].shape[1]
    for s, y_ref in enumerate(y_refs):
        yt[:, pl.ds(pl.multiple_of((place_ref[0] ^ s) * rows, rows), rows)] = y_ref[...]
    target = yt[...]
    attend = at_ref[...]
    cross = lax.dot_general(target, attend, NT, precision=HIGH, preferred_element_type=F32)
    fitted = -lax.dot_general(cross, minus_ref[...], NN, precision=HIGH, preferred_element_type=F32)
    x_ref[...] = fitted.T
    misfit = lax.dot_general(fitted, attend, NN, precision=HIGH, preferred_element_type=F32) - target
    error = jnp.sum(misfit * misfit) / jnp.sum(target * target)
    err_ref[...] = jnp.full(err_ref.shape, error, F32)


def fit(minus_inverse, attend, y_pieces, place):
    kept, rows = attend.shape
    dims = y_pieces[0].shape[0]
    lo = len(y_pieces)
    return pl.pallas_call(
        functools.partial(fit_kernel, lo),
        in_specs=[SMEM] + [VMEM] * (2 + lo),
        out_specs=[VMEM] * 2,
        out_shape=[jax.ShapeDtypeStruct((kept, dims), F32), jax.ShapeDtypeStruct((SUB, 128), F32)],
        scratch_shapes=[pltpu.VMEM((dims, rows), F32)],
        compiler_params=params(),
        cost_estimate=pl.CostEstimate(flops=24 * rows * kept * dims, bytes_accessed=10**6, transcendentals=0),
        name="fit",
    )(place, minus_inverse, attend, *y_pieces)


def per_device(queries, keys, values, kept, roots):
    dims = queries.shape[3]
    score_scale = 1.0 / math.sqrt(dims)
    count = lax.axis_size("ctx")
    lo = math.gcd(count, 4)
    hi = count // lo
    shard = lax.axis_index("ctx")
    my_lo, my_hi = shard % lo, shard // lo
    root_lo, root_hi = roots[0] % lo, roots[0] // lo
    place_lo = my_lo.reshape(1).astype(jnp.int32)
    place_hi = my_hi.reshape(1).astype(jnp.int32)
    part = lambda array, step: lax.dynamic_index_in_dim(array, my_lo ^ step, 0, keepdims=False)

    own = queries[0, 0].reshape(lo, -1, dims)
    quarter = choose(swaps([part(own, s) for s in range(lo)], "ctx", 1), my_lo ^ root_lo)
    quarter = choose(swaps([quarter] * hi, "ctx", lo), my_hi ^ root_hi)
    q_pieces = swaps([quarter] * lo, "ctx", 1)

    slab = keys.shape[1]
    local = kept[0] - shard * slab
    held = (local >= 0) & (local < slab)
    mine = jnp.where(held[:, None], jnp.take(keys[0], jnp.clip(local, 0, slab - 1), axis=0), jnp.zeros((), keys.dtype))
    mine = mine.reshape(lo, -1, dims)
    chunk = sum(swaps([part(mine, s) for s in range(lo)], "ctx", 1))
    chunk = sum(swaps([chunk] * hi, "ctx", lo))
    c_pieces = swaps([chunk] * lo, "ctx", 1)

    parts = attention(q_pieces[:1], keys[0], values[0], score_scale)
    parts += attention(q_pieces[1:], keys[0], values[0], score_scale)
    parts = swaps(parts, "ctx", 1)

    attend, system = gram_system(q_pieces, c_pieces, place_lo, score_scale)
    panels = system.shape[0] // PANEL
    work = [lambda x, p=p: sweep(x, p) for p in range(panels)]

    def run(x):
        return work.pop(0)(x) if work else x

    def after(x, y):
        return lax.optimization_barrier((x, y))

    system = run(system)
    parts, system = after(parts, system)
    parts = swaps(merge(parts, place_hi, hi), "ctx", lo)
    system = run(system)
    parts, system = after(parts, system)
    done = finish(parts)
    blocks = swaps([done] * hi, "ctx", lo)
    system = run(system)
    blocks, system = after(blocks, system)
    y_pieces = swaps([stack(blocks, place_hi)] * lo, "ctx", 1)
    while work:
        system = run(system)

    compact, error = fit(system, attend, y_pieces, place_lo)
    error = error[0, 0]
    heads = lax.axis_size("head")
    step = 1
    while step < heads:
        error = error + swap(error, "head", step)
        step *= 2
    return (compact[None], error / heads)


def solution(mesh):
    placed = (
        P("head", "ctx", None, None),
        P("head", "ctx", None),
        P("head", "ctx", None),
        P("head", None),
        P("head"),
    )
    return jax.shard_map(
        per_device,
        mesh=mesh,
        in_specs=placed,
        out_specs=(P("head", None, None), P()),
        check_vma=False,
    )
```

```python
import functools
import math

import jax
import jax.numpy as jnp
from jax import lax
from jax.experimental import pallas as pl
from jax.experimental.pallas import tpu as pltpu
from jax.sharding import PartitionSpec as P

KBLK = 1024
PANEL = 128
SUB = 8
RIDGE_SHARE = 0.01
F32 = jnp.float32
BF16 = jnp.bfloat16
HIGH = lax.Precision.HIGHEST
VMEM_LIMIT = 48 * 1024 * 1024
VMEM = pl.BlockSpec(memory_space=pltpu.VMEM)
NT = (((1,), (1,)), ((), ()))
TN = (((0,), (0,)), ((), ()))
NN = (((1,), (0,)), ((), ()))


def params(**extra):
    return pltpu.CompilerParams(vmem_limit_bytes=VMEM_LIMIT, **extra)


def swap(array, axis, step):
    size = lax.axis_size(axis)
    return lax.ppermute(array, axis, [(i, i ^ step) for i in range(size)])


def exchange(array):
    return lax.all_to_all(array, "ctx", 0, 0, tiled=True)


def gathered(array):
    return exchange(jnp.broadcast_to(array[None], (lax.axis_size("ctx"),) + array.shape))


def attention_kernel(lanes, blocks, score_scale, q_ref, k_ref, v_ref, out_ref, vt_ref, acc_ref, top_ref, sum_ref):
    step = pl.program_id(0)
    dims = v_ref.shape[1]
    keys = k_ref.shape[0] // blocks
    chunks = q_ref.shape[0] // lanes
    factor = score_scale * math.log2(math.e)
    vt_ref[:dims, :] = v_ref[...].T
    vt_ref[dims:, :] = jnp.ones((vt_ref.shape[0] - dims, v_ref.shape[0]), BF16)

    @pl.when(step == 0)
    def _():
        acc_ref[...] = jnp.zeros_like(acc_ref)
        sum_ref[...] = jnp.zeros_like(sum_ref)
        top_ref[...] = jnp.full(top_ref.shape, -jnp.inf, F32)

    def scores(b, c):
        return lax.dot_general(
            k_ref[b * keys : (b + 1) * keys, :],
            q_ref[c * lanes : (c + 1) * lanes, :],
            NT,
            preferred_element_type=F32,
        )

    stages = [(b, c) for b in range(blocks) for c in range(chunks)]
    ahead = scores(*stages[0])
    for n, (b, c) in enumerate(stages):
        s = ahead
        if n + 1 < len(stages):
            ahead = scores(*stages[n + 1])
        at = slice(c * lanes, (c + 1) * lanes)
        top = jnp.max(s, axis=0, keepdims=True)
        e = jnp.exp2((s - top) * factor).astype(BF16)
        out = lax.dot_general(vt_ref[:, b * keys : (b + 1) * keys], e, NN, preferred_element_type=F32)
        top = top * factor
        old_top = top_ref[:, at]
        joint = jnp.maximum(old_top, top)
        old_scale = jnp.exp2(old_top - joint)
        new_scale = jnp.exp2(top - joint)
        acc_ref[:, at] = acc_ref[:, at] * old_scale + out[:dims, :] * new_scale
        sum_ref[:, at] = sum_ref[:, at] * old_scale + out[dims : dims + 1, :] * new_scale
        top_ref[:, at] = joint

    @pl.when(step == pl.num_programs(0) - 1)
    def _():
        rows = out_ref.shape[1] - SUB
        for j in range(out_ref.shape[0]):
            h, c = divmod(j, chunks)
            at = slice(c * lanes, (c + 1) * lanes)
            out_ref[j, :rows, :] = acc_ref[h * rows : (h + 1) * rows, at]
            out_ref[j, rows:, :] = jnp.concatenate(
                [top_ref[:, at], sum_ref[:, at], jnp.zeros((SUB - 2, lanes), F32)], axis=0
            )


def attention(queries, keys, values, score_scale, groups, chunks):
    rows, dims = queries.shape
    slab = keys.shape[0]
    block = min(KBLK, slab)
    blocks = 2 if slab % (2 * block) == 0 else 1
    lanes = rows // chunks
    shape = (groups * chunks, dims // groups + SUB, lanes)
    return pl.pallas_call(
        functools.partial(attention_kernel, lanes, blocks, score_scale),
        grid=(slab // (block * blocks),),
        in_specs=[pl.BlockSpec((rows, dims), lambda b: (0, 0))]
        + [pl.BlockSpec((block * blocks, dims), lambda b: (b, 0))] * 2,
        out_specs=pl.BlockSpec(shape, lambda b: (0, 0, 0)),
        out_shape=jax.ShapeDtypeStruct(shape, F32),
        scratch_shapes=[
            pltpu.VMEM((dims + 16, block * blocks), BF16),
            pltpu.VMEM((dims, rows), F32),
            pltpu.VMEM((1, rows), F32),
            pltpu.VMEM((1, rows), F32),
        ],
        compiler_params=params(),
        cost_estimate=pl.CostEstimate(
            flops=4 * rows * slab * dims, bytes_accessed=4 * slab * dims, transcendentals=rows * slab
        ),
        name="attention",
    )(queries, keys, values)


def merge_kernel(part_ref, out_ref):
    count, rows = part_ref.shape[0], out_ref.shape[1]
    tops = [part_ref[i, rows : rows + 1, :] for i in range(count)]
    top = functools.reduce(jnp.maximum, tops)
    scales = [jnp.exp2(t - top) for t in tops]
    total = sum(part_ref[i, rows + 1 : rows + 2, :] * scales[i] for i in range(count))
    merged = sum(part_ref[i, :rows, :] * scales[i] for i in range(count)) / total
    for i in range(count):
        out_ref[i] = merged


def merge(parts):
    count, rows, lanes = parts.shape
    return pl.pallas_call(
        merge_kernel,
        in_specs=[VMEM],
        out_specs=VMEM,
        out_shape=jax.ShapeDtypeStruct((count, rows - SUB, lanes), F32),
        compiler_params=params(),
        cost_estimate=pl.CostEstimate(flops=10**6, bytes_accessed=10**6, transcendentals=0),
        name="merge",
    )(parts)


def gram_kernel(score_scale, q_ref, c_ref, at_ref, h_ref):
    scores = lax.dot_general(c_ref[...], q_ref[...], NT, preferred_element_type=F32) * score_scale
    weights = jnp.exp(scores - jnp.max(scores, axis=0, keepdims=True))
    at_ref[...] = weights / jnp.sum(weights, axis=0, keepdims=True)
    gram = lax.dot_general(at_ref[...], at_ref[...], NT, precision=HIGH, preferred_element_type=F32)
    kept = gram.shape[0]
    diagonal = lax.broadcasted_iota(jnp.int32, gram.shape, 0) == lax.broadcasted_iota(jnp.int32, gram.shape, 1)
    trace = jnp.sum(jnp.where(diagonal, gram, 0.0))
    h_ref[...] = gram + jnp.where(diagonal, RIDGE_SHARE * trace / kept, 0.0)


def gram_system(queries, kept_keys, score_scale):
    rows, kept = queries.shape[0], kept_keys.shape[0]
    return pl.pallas_call(
        functools.partial(gram_kernel, score_scale),
        in_specs=[VMEM] * 2,
        out_specs=[VMEM] * 2,
        out_shape=[jax.ShapeDtypeStruct((kept, rows), F32), jax.ShapeDtypeStruct((kept, kept), F32)],
        compiler_params=params(),
        cost_estimate=pl.CostEstimate(flops=12 * rows * kept * kept, bytes_accessed=10**6, transcendentals=rows * kept),
        name="gram",
    )(queries, kept_keys)


def invert_block(rows):
    count = len(rows)
    size = count * SUB
    lane = lax.broadcasted_iota(jnp.int32, (SUB, size), 1)
    sub = lax.broadcasted_iota(jnp.int32, (SUB, size), 0)
    spread = lambda array, column: jnp.broadcast_to(array[:, column : column + 1], (SUB, size))
    line = lambda array, row: jnp.broadcast_to(array[row : row + 1, :], (SUB, size))
    for k in range(count):
        base = k * SUB
        inside = (lane >= base) & (lane < base + SUB)
        columns = [spread(rows[k], base + j) for j in range(SUB)]
        work = jnp.where(inside, jnp.where(lane - base == sub, 1.0, 0.0), rows[k])
        for j in range(SUB):
            here = sub == j
            inverse = 1.0 / line(columns[j], j)
            step = lambda v: (lambda t: jnp.where(here, t, v - columns[j] * t))(line(v, j) * inverse)
            for i in range(j + 1, SUB):
                columns[i] = step(columns[i])
            work = step(work)
        lines = [line(work, j) for j in range(SUB)]
        updated = []
        for i in range(count):
            if i == k:
                updated.append(work)
                continue
            fresh = jnp.where(inside, 0.0, rows[i])
            for j in range(SUB):
                fresh = fresh - spread(rows[i], base + j) * lines[j]
            updated.append(fresh)
        rows = updated
    return rows


def sweep_kernel(panel, h_ref, out_ref):
    size = h_ref.shape[0]
    at = pl.ds(panel * PANEL, PANEL)
    across = h_ref[at, :]
    block = across[:, panel * PANEL : (panel + 1) * PANEL]
    inverse = jnp.concatenate(
        invert_block([block[i * SUB : (i + 1) * SUB, :] for i in range(PANEL // SUB)]), axis=0
    )
    turned = lax.dot_general(inverse, across, NN, precision=HIGH, preferred_element_type=F32)
    out_ref[...] = h_ref[...] - lax.dot_general(across, turned, TN, precision=HIGH, preferred_element_type=F32)
    out_ref[:, at] = turned.T
    out_ref[at, :] = turned
    out_ref[at, at] = -inverse


def sweep(system, panel):
    size = system.shape[0]
    return pl.pallas_call(
        functools.partial(sweep_kernel, panel),
        in_specs=[VMEM],
        out_specs=VMEM,
        out_shape=jax.ShapeDtypeStruct(system.shape, F32),
        compiler_params=params(),
        cost_estimate=pl.CostEstimate(flops=5 * 10**9, bytes_accessed=4 * size * size, transcendentals=0),
        name="sweep",
    )(system)


def fit_kernel(minus_ref, at_ref, y_ref, x_ref, err_ref, yt):
    count, high, wide = y_ref.shape
    chunks = at_ref.shape[1] // wide
    for j in range(count):
        h, c = divmod(j, chunks)
        yt[h * high : (h + 1) * high, c * wide : (c + 1) * wide] = y_ref[j]
    target = yt[...]
    attend = at_ref[...]
    cross = lax.dot_general(target, attend, NT, precision=HIGH, preferred_element_type=F32)
    fitted = -lax.dot_general(cross, minus_ref[...], NN, precision=HIGH, preferred_element_type=F32)
    x_ref[...] = fitted.T
    misfit = lax.dot_general(fitted, attend, NN, precision=HIGH, preferred_element_type=F32) - target
    error = jnp.sum(misfit * misfit) / jnp.sum(target * target)
    err_ref[...] = jnp.full(err_ref.shape, error, F32)


def fit(minus_inverse, attend, blocks):
    kept, rows = attend.shape
    dims = blocks.size // rows
    return pl.pallas_call(
        fit_kernel,
        in_specs=[VMEM] * 3,
        out_specs=[VMEM] * 2,
        out_shape=[jax.ShapeDtypeStruct((kept, dims), F32), jax.ShapeDtypeStruct((SUB, 128), F32)],
        scratch_shapes=[pltpu.VMEM((dims, rows), F32)],
        compiler_params=params(),
        cost_estimate=pl.CostEstimate(flops=24 * rows * kept * dims, bytes_accessed=10**6, transcendentals=0),
        name="fit",
    )(minus_inverse, attend, blocks)


def per_device(queries, keys, values, kept, roots):
    rows, dims = queries.shape[2:]
    score_scale = 1.0 / math.sqrt(dims)
    count = lax.axis_size("ctx")
    chunks = math.gcd(count, 4)
    groups = count // chunks
    shard = lax.axis_index("ctx")

    share = exchange(queries[0, 0].reshape(count, -1, dims))
    share = lax.dynamic_index_in_dim(share, roots[0], 0, keepdims=False)
    reference = gathered(share).reshape(rows, dims)

    slab = keys.shape[1]
    local = kept[0] - shard * slab
    held = (local >= 0) & (local < slab)
    mine = jnp.where(held[:, None], jnp.take(keys[0], jnp.clip(local, 0, slab - 1), axis=0), jnp.zeros((), keys.dtype))
    share = jnp.sum(exchange(mine.reshape(count, -1, dims)), axis=0, dtype=keys.dtype)
    kept_keys = gathered(share).reshape(-1, dims)

    parts = exchange(attention(reference, keys[0], values[0], score_scale, groups, chunks))

    attend, system = gram_system(reference, kept_keys, score_scale)
    panels = system.shape[0] // PANEL
    before = panels // 2
    for panel in range(before):
        system = sweep(system, panel)
    parts, system = lax.optimization_barrier((parts, system))
    blocks = exchange(merge(parts))
    for panel in range(before, panels):
        system = sweep(system, panel)

    compact, error = fit(system, attend, blocks)
    error = error[0, 0]
    heads = lax.axis_size("head")
    step = 1
    while step < heads:
        error = error + swap(error, "head", step)
        step *= 2
    return (compact[None], error / heads)


def solution(mesh):
    placed = (
        P("head", "ctx", None, None),
        P("head", "ctx", None),
        P("head", "ctx", None),
        P("head", None),
        P("head"),
    )
    return jax.shard_map(
        per_device,
        mesh=mesh,
        in_specs=placed,
        out_specs=(P("head", None, None), P()),
        check_vma=False,
    )
```

```python
import functools
import math

import jax
import jax.numpy as jnp
from jax import lax
from jax.experimental import pallas as pl
from jax.experimental.pallas import tpu as pltpu
from jax.sharding import PartitionSpec as P

KBLK = 1024
PANEL = 128
SUB = 8
RIDGE_SHARE = 0.01
F32 = jnp.float32
BF16 = jnp.bfloat16
HIGH = lax.Precision.HIGHEST
VMEM_LIMIT = 48 * 1024 * 1024
VMEM = pl.BlockSpec(memory_space=pltpu.VMEM)
SMEM = pl.BlockSpec(memory_space=pltpu.SMEM)
NT = (((1,), (1,)), ((), ()))
TN = (((0,), (0,)), ((), ()))
NN = (((1,), (0,)), ((), ()))


def swap(array, axis, step):
    size = lax.axis_size(axis)
    return lax.ppermute(array, axis, [(i, i ^ step) for i in range(size)])


def call(kernel, ins, outs, cost=0, scratch=(), name=None):
    shapes = [jax.ShapeDtypeStruct(shape, kind) for shape, kind in outs]
    return pl.pallas_call(
        kernel,
        in_specs=[SMEM] + [VMEM] * (len(ins) - 1),
        out_specs=[VMEM] * len(outs),
        out_shape=shapes,
        scratch_shapes=list(scratch),
        compiler_params=pltpu.CompilerParams(vmem_limit_bytes=VMEM_LIMIT),
        cost_estimate=pl.CostEstimate(flops=cost, bytes_accessed=10**5, transcendentals=0),
        name=name,
    )(*ins)


def aligned(value, unit):
    return pl.ds(pl.multiple_of(value * unit, unit), unit)


def prepare_kernel(window, place_ref, q_ref, kept_ref, k_ref, keep_ref, send_ref, spots, picked):
    slab, dims = k_ref.shape
    kept = kept_ref.shape[1]
    base = place_ref[3]
    positions = kept_ref[...]
    before = jnp.sum((positions < base).astype(jnp.int32))
    start = jnp.minimum(before // 16, (kept - window) // 16)
    local = (positions - base).astype(F32)
    for i in range(0, kept, 128):
        spots[i : i + 128, :] = jnp.broadcast_to(local[:, i : i + 128], (128, 128)).T
    mine = spots[pl.ds(pl.multiple_of(start * 16, 16), window), :]
    column = lax.broadcasted_iota(jnp.int32, (window, 128), 1).astype(F32)
    onehot = jnp.concatenate(
        [jnp.where(mine == column + float(i), 1.0, 0.0).astype(BF16) for i in range(0, slab, 128)], axis=1
    )
    rows = lax.dot_general(onehot, k_ref[...], NN, preferred_element_type=F32)
    picked[...] = jnp.zeros_like(picked)
    picked[pl.ds(pl.multiple_of(start * 16, 16), window), :] = rows.astype(BF16)
    share, part = q_ref.shape[0] // 4, kept // 4
    is_root = place_ref[2] == 1
    for out, core in ((keep_ref, place_ref[0]), (send_ref, 1 - place_ref[0])):
        for y in range(2):
            q = q_ref[aligned(2 * y + core, share), :]
            out[y, :share, :] = jnp.where(is_root, q, jnp.zeros_like(q))
            out[y, share:, :] = picked[aligned(2 * y + core, part), :]


def split_add_kernel(place_ref, a_ref, b_ref, keep_ref, send_ref):
    y = place_ref[1]
    keep_ref[...] = a_ref[y] + b_ref[y]
    send_ref[...] = a_ref[1 - y] + b_ref[1 - y]


def add_kernel(place_ref, a_ref, b_ref, out_ref):
    out_ref[...] = a_ref[...] + b_ref[...]


def pair_kernel(place_ref, a_ref, b_ref, out_ref):
    y = place_ref[1]
    out_ref[y] = a_ref[...]
    out_ref[1 - y] = b_ref[...]


def arrange_kernel(place_ref, a_ref, b_ref, q_ref, c_ref):
    share, part = q_ref.shape[0] // 4, c_ref.shape[0] // 4
    for ref, core in ((a_ref, place_ref[0]), (b_ref, 1 - place_ref[0])):
        for y in range(2):
            q_ref[aligned(2 * y + core, share), :] = ref[y, :share, :]
            c_ref[aligned(2 * y + core, part), :] = ref[y, share:, :]


def spread(place, queries, kept, keys):
    rows, dims = queries.shape
    count = kept.shape[1]
    window = 4 * count // lax.axis_size("ctx") + 16
    tall = (rows + count) // 4
    half, quarter = ((2, tall, dims), BF16), ((tall, dims), BF16)
    keep, send = call(
        functools.partial(prepare_kernel, window),
        (place, queries, kept, keys),
        [half, half],
        scratch=[pltpu.VMEM((count, 128), F32), pltpu.VMEM((count, dims), BF16)],
        name="prepare",
    )
    keep, send = call(split_add_kernel, (place, keep, swap(send, "ctx", 1)), [quarter] * 2, name="split")
    (share,) = call(add_kernel, (place, keep, swap(send, "ctx", 2)), [quarter], name="join")
    step = lax.axis_size("ctx") // 2
    while step >= 4:
        (share,) = call(add_kernel, (place, share, swap(share, "ctx", step)), [quarter], name="join")
        step //= 2
    (share,) = call(pair_kernel, (place, share, swap(share, "ctx", 2)), [half], name="pair")
    return call(
        arrange_kernel,
        (place, share, swap(share, "ctx", 1)),
        [((rows, dims), BF16), ((count, dims), BF16)],
        name="arrange",
    )


def attention_kernel(lanes, blocks, score_scale, place_ref, q_ref, k_ref, v_ref, keep_ref, send_ref, vt_ref, acc_ref, top_ref, sum_ref):
    step = pl.program_id(0)
    dims = v_ref.shape[1]
    keys = k_ref.shape[0] // blocks
    chunks = q_ref.shape[0] // lanes
    factor = score_scale * math.log2(math.e)
    vt_ref[:dims, :] = v_ref[...].T
    vt_ref[dims:, :] = jnp.ones((vt_ref.shape[0] - dims, v_ref.shape[0]), BF16)

    @pl.when(step == 0)
    def _():
        acc_ref[...] = jnp.zeros_like(acc_ref)
        sum_ref[...] = jnp.zeros_like(sum_ref)
        top_ref[...] = jnp.full(top_ref.shape, -jnp.inf, F32)

    def scores(b, c):
        return lax.dot_general(
            k_ref[b * keys : (b + 1) * keys, :],
            q_ref[c * lanes : (c + 1) * lanes, :],
            NT,
            preferred_element_type=F32,
        )

    stages = [(b, c) for b in range(blocks) for c in range(chunks)]
    ahead = scores(*stages[0])
    for n, (b, c) in enumerate(stages):
        s = ahead
        if n + 1 < len(stages):
            ahead = scores(*stages[n + 1])
        at = slice(c * lanes, (c + 1) * lanes)
        top = jnp.max(s, axis=0, keepdims=True)
        e = jnp.exp2((s - top) * factor).astype(BF16)
        out = lax.dot_general(vt_ref[:, b * keys : (b + 1) * keys], e, NN, preferred_element_type=F32)
        top = top * factor
        old_top = top_ref[:, at]
        joint = jnp.maximum(old_top, top)
        old_scale = jnp.exp2(old_top - joint)
        new_scale = jnp.exp2(top - joint)
        acc_ref[:, at] = acc_ref[:, at] * old_scale + out[:dims, :] * new_scale
        sum_ref[:, at] = sum_ref[:, at] * old_scale + out[dims : dims + 1, :] * new_scale
        top_ref[:, at] = joint

    @pl.when(step == pl.num_programs(0) - 1)
    def _():
        for out, core in ((keep_ref, place_ref[0]), (send_ref, 1 - place_ref[0])):
            for y in range(2):
                at, to = aligned(2 * y + core, lanes), slice(y * lanes, (y + 1) * lanes)
                out[:dims, to] = acc_ref[:, at]
                out[dims:, to] = jnp.concatenate(
                    [top_ref[:, at], sum_ref[:, at], jnp.zeros((SUB - 2, lanes), F32)], axis=0
                )


def attention(place, queries, keys, values, score_scale):
    rows, dims = queries.shape
    slab = keys.shape[0]
    block = min(KBLK, slab)
    blocks = 2 if slab % (2 * block) == 0 else 1
    lanes = rows // 4
    shape = (dims + SUB, rows // 2)
    return pl.pallas_call(
        functools.partial(attention_kernel, lanes, blocks, score_scale),
        grid=(slab // (block * blocks),),
        in_specs=[SMEM, pl.BlockSpec((rows, dims), lambda b: (0, 0))]
        + [pl.BlockSpec((block * blocks, dims), lambda b: (b, 0))] * 2,
        out_specs=[pl.BlockSpec(shape, lambda b: (0, 0))] * 2,
        out_shape=[jax.ShapeDtypeStruct(shape, F32)] * 2,
        scratch_shapes=[
            pltpu.VMEM((dims + 16, block * blocks), BF16),
            pltpu.VMEM((dims, rows), F32),
            pltpu.VMEM((1, rows), F32),
            pltpu.VMEM((1, rows), F32),
        ],
        compiler_params=pltpu.CompilerParams(vmem_limit_bytes=VMEM_LIMIT),
        cost_estimate=pl.CostEstimate(
            flops=4 * rows * slab * dims, bytes_accessed=4 * slab * dims, transcendentals=rows * slab
        ),
        name="attention",
    )(place, queries, keys, values)


def merged(a_ref, b_ref):
    dims = a_ref.shape[0] - SUB
    a_top, b_top = a_ref[dims : dims + 1, :], b_ref[dims : dims + 1, :]
    top = jnp.maximum(a_top, b_top)
    a_scale, b_scale = jnp.exp2(a_top - top), jnp.exp2(b_top - top)
    total = a_ref[dims + 1 : dims + 2, :] * a_scale + b_ref[dims + 1 : dims + 2, :] * b_scale
    out = a_ref[:dims, :] * a_scale + b_ref[:dims, :] * b_scale
    return out, top, total


def tail(top, total):
    return jnp.concatenate([top, total, jnp.zeros((SUB - 2, top.shape[1]), F32)], axis=0)


def merge_lanes_kernel(place_ref, a_ref, b_ref, keep_ref, send_ref, work):
    out, top, total = merged(a_ref, b_ref)
    dims, lanes = out.shape[0], keep_ref.shape[1]
    work[:dims, :] = out
    work[dims:, :] = tail(top, total)
    y = place_ref[1]
    keep_ref[...] = work[:, aligned(y, lanes)]
    send_ref[...] = work[:, aligned(1 - y, lanes)]


def merge_rows_kernel(step, place_ref, a_ref, b_ref, keep_ref, send_ref, work):
    out, top, total = merged(a_ref, b_ref)
    rows = keep_ref.shape[0] - SUB
    work[...] = out
    bit = (place_ref[4] // step) % 2
    for ref, which in ((keep_ref, bit), (send_ref, 1 - bit)):
        ref[:rows, :] = work[aligned(which, rows), :]
        ref[rows:, :] = tail(top, total)


def finish_kernel(place_ref, a_ref, b_ref, out_ref):
    out, _, total = merged(a_ref, b_ref)
    out_ref[...] = out / total


def stack_rows_kernel(step, place_ref, a_ref, b_ref, out_ref):
    rows = a_ref.shape[0]
    bit = (place_ref[4] // step) % 2
    out_ref[aligned(bit, rows), :] = a_ref[...]
    out_ref[aligned(1 - bit, rows), :] = b_ref[...]


def stack_lanes_kernel(place_ref, a_ref, b_ref, out_ref):
    lanes = a_ref.shape[1]
    y = place_ref[1]
    out_ref[:, aligned(y, lanes)] = a_ref[...]
    out_ref[:, aligned(1 - y, lanes)] = b_ref[...]


def target_rounds(place, keep, send):
    dims, lanes = keep.shape[0] - SUB, keep.shape[1] // 2
    came = yield swap(send, "ctx", 1)
    shape = ((dims + SUB, lanes), F32)
    keep, send = call(
        merge_lanes_kernel, (place, keep, came), [shape] * 2, scratch=[pltpu.VMEM((dims + SUB, 2 * lanes), F32)], name="merge"
    )
    came = yield swap(send, "ctx", 2)
    step, rows = lax.axis_size("ctx") // 2, dims
    while step >= 4:
        shape = ((rows // 2 + SUB, lanes), F32)
        kernel = functools.partial(merge_rows_kernel, step)
        keep, send = call(kernel, (place, keep, came), [shape] * 2, scratch=[pltpu.VMEM((rows, lanes), F32)], name="merge")
        came = yield swap(send, "ctx", step)
        rows //= 2
        step //= 2
    (block,) = call(finish_kernel, (place, keep, came), [((rows, lanes), F32)], name="finish")
    step = 4
    while step < lax.axis_size("ctx"):
        came = yield swap(block, "ctx", step)
        rows *= 2
        (block,) = call(functools.partial(stack_rows_kernel, step), (place, block, came), [((rows, lanes), F32)], name="stack")
        step *= 2
    came = yield swap(block, "ctx", 2)
    (block,) = call(stack_lanes_kernel, (place, block, came), [((dims, 2 * lanes), F32)], name="stack")
    came = yield swap(block, "ctx", 1)
    return block, came


def attend_kernel(score_scale, place_ref, q_ref, c_ref, at_ref):
    scores = lax.dot_general(c_ref[...], q_ref[...], NT, preferred_element_type=F32) * score_scale
    weights = jnp.exp(scores - jnp.max(scores, axis=0, keepdims=True))
    at_ref[...] = weights / jnp.sum(weights, axis=0, keepdims=True)


def gram_kernel(place_ref, at_ref, h_ref):
    gram = lax.dot_general(at_ref[...], at_ref[...], NT, precision=HIGH, preferred_element_type=F32)
    kept = gram.shape[0]
    diagonal = lax.broadcasted_iota(jnp.int32, gram.shape, 0) == lax.broadcasted_iota(jnp.int32, gram.shape, 1)
    trace = jnp.sum(jnp.where(diagonal, gram, 0.0))
    h_ref[...] = gram + jnp.where(diagonal, RIDGE_SHARE * trace / kept, 0.0)


def invert_block(rows):
    count = len(rows)
    size = count * SUB
    lane = lax.broadcasted_iota(jnp.int32, (SUB, size), 1)
    sub = lax.broadcasted_iota(jnp.int32, (SUB, size), 0)
    spread = lambda array, column: jnp.broadcast_to(array[:, column : column + 1], (SUB, size))
    line = lambda array, row: jnp.broadcast_to(array[row : row + 1, :], (SUB, size))
    for k in range(count):
        base = k * SUB
        inside = (lane >= base) & (lane < base + SUB)
        columns = [spread(rows[k], base + j) for j in range(SUB)]
        work = jnp.where(inside, jnp.where(lane - base == sub, 1.0, 0.0), rows[k])
        for j in range(SUB):
            here = sub == j
            inverse = 1.0 / line(columns[j], j)
            step = lambda v: (lambda t: jnp.where(here, t, v - columns[j] * t))(line(v, j) * inverse)
            for i in range(j + 1, SUB):
                columns[i] = step(columns[i])
            work = step(work)
        lines = [line(work, j) for j in range(SUB)]
        updated = []
        for i in range(count):
            if i == k:
                updated.append(work)
                continue
            fresh = jnp.where(inside, 0.0, rows[i])
            for j in range(SUB):
                fresh = fresh - spread(rows[i], base + j) * lines[j]
            updated.append(fresh)
        rows = updated
    return rows


def invert_kernel(panel, place_ref, h_ref, out_ref):
    at = slice(panel * PANEL, (panel + 1) * PANEL)
    block = h_ref[at, at]
    out_ref[...] = jnp.concatenate(
        invert_block([block[i * SUB : (i + 1) * SUB, :] for i in range(PANEL // SUB)]), axis=0
    )


def update_kernel(panel, place_ref, h_ref, inverse_ref, out_ref):
    at = slice(panel * PANEL, (panel + 1) * PANEL)
    across = h_ref[at, :]
    turned = lax.dot_general(inverse_ref[...], across, NN, precision=HIGH, preferred_element_type=F32)
    out_ref[...] = h_ref[...] - lax.dot_general(across, turned, TN, precision=HIGH, preferred_element_type=F32)
    out_ref[:, at] = turned.T
    out_ref[at, :] = turned
    out_ref[at, at] = -inverse_ref[...]


def fit_kernel(place_ref, minus_ref, at_ref, own_ref, other_ref, x_ref, err_ref, yt):
    lanes = own_ref.shape[1] // 2
    for ref, core in ((own_ref, place_ref[0]), (other_ref, 1 - place_ref[0])):
        for y in range(2):
            yt[:, aligned(2 * y + core, lanes)] = ref[:, y * lanes : (y + 1) * lanes]
    target = yt[...]
    attend = at_ref[...]
    cross = lax.dot_general(target, attend, NT, precision=HIGH, preferred_element_type=F32)
    fitted = -lax.dot_general(cross, minus_ref[...], NN, precision=HIGH, preferred_element_type=F32)
    x_ref[...] = fitted.T
    misfit = lax.dot_general(fitted, attend, NN, precision=HIGH, preferred_element_type=F32) - target
    error = jnp.sum(misfit * misfit) / jnp.sum(target * target)
    err_ref[...] = jnp.full(err_ref.shape, error, F32)


def per_device(queries, keys, values, kept, roots):
    rows, dims = queries.shape[2:]
    count = kept.shape[1]
    score_scale = 1.0 / math.sqrt(dims)
    shard = lax.axis_index("ctx")
    place = jnp.stack(
        [shard % 2, shard // 2 % 2, (shard == roots[0]).astype(shard.dtype), shard * keys.shape[1], shard]
    ).astype(jnp.int32)

    reference, kept_keys = spread(place, queries[0, 0], kept, keys[0])
    rounds = target_rounds(place, *attention(place, reference, keys[0], values[0], score_scale))
    came = next(rounds)
    ends = None

    def beside(arrays):
        nonlocal came, ends
        if ends is None:
            arrays, came = lax.optimization_barrier((arrays, came))
            try:
                came = rounds.send(came)
            except StopIteration as stop:
                ends = stop.value
        return arrays

    system_shape = ((count, count), F32)
    (attend,) = call(
        functools.partial(attend_kernel, score_scale), (place, reference, kept_keys), [((count, rows), F32)], 10**9, name="attend"
    )
    attend = beside(attend)
    (system,) = call(gram_kernel, (place, attend), [system_shape], 4 * 10**9, name="gram")
    system = beside(system)
    for panel in range(count // PANEL):
        (inverse,) = call(
            functools.partial(invert_kernel, panel), (place, system), [((PANEL, PANEL), F32)], 5 * 10**9, name="invert"
        )
        inverse = beside(inverse)
        (system,) = call(
            functools.partial(update_kernel, panel), (place, system, inverse), [system_shape], 2 * 10**9, name="update"
        )
        if panel == 0 or panel == count // PANEL - 1:
            system = beside(system)
    while ends is None:
        system = beside(system)

    compact, error = call(
        fit_kernel,
        (place, system, attend, *ends),
        [((count, dims), F32), ((SUB, 128), F32)],
        10**9,
        scratch=[pltpu.VMEM((dims, rows), F32)],
        name="fit",
    )
    heads = lax.axis_size("head")
    step = 1
    while step < heads:
        error = error + swap(error, "head", step)
        step *= 2
    return (compact[None], error[0, 0] / heads)


def solution(mesh):
    placed = (
        P("head", "ctx", None, None),
        P("head", "ctx", None),
        P("head", "ctx", None),
        P("head", None),
        P("head"),
    )
    return jax.shard_map(
        per_device,
        mesh=mesh,
        in_specs=placed,
        out_specs=(P("head", None, None), P()),
        check_vma=False,
    )
```

```python
import functools
import math

import jax
import jax.numpy as jnp
from jax import lax
from jax.experimental import pallas as pl
from jax.experimental.pallas import tpu as pltpu
from jax.sharding import PartitionSpec as P

KBLK = 1024
PANEL = 128
SUB = 8
RIDGE_SHARE = 0.01
F32 = jnp.float32
BF16 = jnp.bfloat16
HIGH = lax.Precision.HIGHEST
VMEM_LIMIT = 48 * 1024 * 1024
VMEM = pl.BlockSpec(memory_space=pltpu.VMEM)
SMEM = pl.BlockSpec(memory_space=pltpu.SMEM)
NT = (((1,), (1,)), ((), ()))
TN = (((0,), (0,)), ((), ()))
NN = (((1,), (0,)), ((), ()))


def swap(array, axis, step):
    size = lax.axis_size(axis)
    return lax.ppermute(array, axis, [(i, i ^ step) for i in range(size)])


def call(kernel, ins, outs, cost=10**5, scratch=(), name=None, specs=None):
    return pl.pallas_call(
        kernel,
        in_specs=specs or [SMEM if x.size == 1 else VMEM for x in ins],
        out_specs=[VMEM] * len(outs),
        out_shape=[jax.ShapeDtypeStruct(shape, kind) for shape, kind in outs],
        scratch_shapes=list(scratch),
        compiler_params=pltpu.CompilerParams(vmem_limit_bytes=VMEM_LIMIT),
        cost_estimate=pl.CostEstimate(flops=cost, bytes_accessed=10**5, transcendentals=0),
        name=name,
    )(*ins)


def aligned(value, unit):
    return pl.ds(pl.multiple_of(value * unit, unit), unit)


def prepare_kernel(window, shard_ref, root_ref, q_hbm, kept_hbm, k_hbm, *refs):
    outs, k_ref, (q_ref, kept_ref, spots, picked, sems) = refs[:4], refs[4], refs[5:]
    slab, dims = k_ref.shape
    kept = kept_ref.shape[1]
    steps = sems.shape[0] - 2
    chunk = slab // steps
    loads = [pltpu.make_async_copy(kept_hbm, kept_ref, sems.at[steps])]
    for i in range(steps):
        part = pl.ds(i * chunk, chunk)
        loads.append(pltpu.make_async_copy(k_hbm.at[part], k_ref.at[part], sems.at[i]))
    loads.append(pltpu.make_async_copy(q_hbm, q_ref, sems.at[steps + 1]))
    for load in loads:
        load.start()
    base = shard_ref[0] * slab
    loads[0].wait()
    positions = kept_ref[...]
    before = jnp.sum((positions < base).astype(jnp.int32))
    start = jnp.minimum(before // 16, (kept - window) // 16)
    local = (positions - base).astype(F32)
    for i in range(0, kept, 128):
        spots[i : i + 128, :] = jnp.broadcast_to(local[:, i : i + 128], (128, 128)).T
    spot = pl.ds(pl.multiple_of(start * 16, 16), window)
    mine = spots[spot, :]
    column = lax.broadcasted_iota(jnp.int32, (window, 128), 1).astype(F32)
    rows = jnp.zeros((window, dims), F32)
    for i in range(steps):
        onehot = jnp.concatenate(
            [jnp.where(mine == column + float(j), 1.0, 0.0).astype(BF16) for j in range(i * chunk, (i + 1) * chunk, 128)],
            axis=1,
        )
        loads[1 + i].wait()
        rows += lax.dot_general(onehot, k_ref[i * chunk : (i + 1) * chunk, :], NN, preferred_element_type=F32)
    picked[...] = jnp.zeros_like(picked)
    picked[spot, :] = rows.astype(BF16)
    loads[-1].wait()
    share, part = q_ref.shape[0] // 4, kept // 4
    is_root = shard_ref[0] == root_ref[0]
    for s, out in enumerate(outs):
        place = (shard_ref[0] % 4) ^ s
        q = q_ref[aligned(place, share), :]
        out[:share, :] = jnp.where(is_root, q, jnp.zeros_like(q))
        out[share:, :] = picked[aligned(place, part), :]


def sum_kernel(*refs):
    total = refs[0][...]
    for ref in refs[1:-1]:
        total = total + ref[...]
    refs[-1][...] = total


def spread(shard, queries, kept, keys, roots):
    (rows, dims), (slab, _) = queries.shape, keys.shape
    count = kept.shape[1]
    devices = lax.axis_size("ctx")
    tall = ((rows + count) // 4, dims)
    anywhere = pl.BlockSpec(memory_space=pl.ANY)
    *pieces, keys = call(
        functools.partial(prepare_kernel, 4 * count // devices + 16),
        (shard, roots, queries, kept, keys),
        [(tall, BF16)] * 4 + [(keys.shape, BF16)],
        scratch=[
            pltpu.VMEM((rows, dims), BF16),
            pltpu.VMEM((1, count), jnp.int32),
            pltpu.VMEM((count, 128), F32),
            pltpu.VMEM((count, dims), BF16),
            pltpu.SemaphoreType.DMA((6,)),
        ],
        name="prepare",
        specs=[SMEM, SMEM, anywhere, anywhere, anywhere],
    )
    total = lambda arrays: call(sum_kernel, arrays, [(tall, BF16)], name="total")[0]
    piece = total([pieces[0]] + [swap(pieces[s], "ctx", s) for s in (1, 2, 3)])
    step = 4
    while step < devices:
        ways = math.gcd(devices // step, 4)
        piece = total([piece] + [swap(piece, "ctx", t * step) for t in range(1, ways)])
        step *= ways
    return [piece] + [swap(piece, "ctx", s) for s in (1, 2, 3)], keys


def turn_kernel(v_ref, vt_ref):
    dims = v_ref.shape[1]
    vt_ref[:dims, :] = v_ref[...].T
    vt_ref[dims:, :] = jnp.ones((vt_ref.shape[0] - dims, v_ref.shape[0]), BF16)


def attention_kernel(pieces, lanes, block, score_scale, *refs):
    q_refs, k_ref, vt_ref, before, out_ref = refs[:pieces], refs[pieces], refs[pieces + 1], refs[pieces + 2 : -1], refs[-1]
    dims = k_ref.shape[1]
    blocks = k_ref.shape[0] // block
    factor = score_scale * math.log2(math.e)
    skip = len(before) * lanes
    for ref in before:
        out_ref[:, :skip] = ref[...]

    def scores(i, b):
        return lax.dot_general(
            k_ref[b * block : (b + 1) * block, :], q_refs[i][:lanes, :], NT, preferred_element_type=F32
        )

    stages = [(i, b) for i in range(pieces) for b in range(blocks)]
    ahead = scores(*stages[0])
    for n, (i, b) in enumerate(stages):
        s = ahead
        if n + 1 < len(stages):
            ahead = scores(*stages[n + 1])
        at = slice(skip + i * lanes, skip + (i + 1) * lanes)
        top = jnp.max(s, axis=0, keepdims=True)
        e = jnp.exp2((s - top) * factor).astype(BF16)
        out = lax.dot_general(vt_ref[:, b * block : (b + 1) * block], e, NN, preferred_element_type=F32)
        top = top * factor
        total = out[dims : dims + 1, :]
        out = out[:dims, :]
        if b:
            old_top = out_ref[dims : dims + 1, at]
            joint = jnp.maximum(old_top, top)
            old_scale = jnp.exp2(old_top - joint)
            new_scale = jnp.exp2(top - joint)
            out = out_ref[:dims, at] * old_scale + out * new_scale
            total = out_ref[dims + 1 : dims + 2, at] * old_scale + total * new_scale
            top = joint
        out_ref[:dims, at] = out
        out_ref[dims:, at] = tail(top, total)


def attention(pieces, lanes, keys, turned, score_scale, before=()):
    slab, dims = keys.shape
    return call(
        functools.partial(attention_kernel, len(pieces), lanes, min(KBLK, slab), score_scale),
        (*pieces, keys, turned, *before),
        [((dims + SUB, lanes * (len(pieces) + len(before))), F32)],
        4 * lanes * len(pieces) * slab * dims,
        name="attention",
    )[0]


def merged(a_ref, b_ref):
    dims = a_ref.shape[0] - SUB
    a_top, b_top = a_ref[dims : dims + 1, :], b_ref[dims : dims + 1, :]
    top = jnp.maximum(a_top, b_top)
    a_scale, b_scale = jnp.exp2(a_top - top), jnp.exp2(b_top - top)
    total = a_ref[dims + 1 : dims + 2, :] * a_scale + b_ref[dims + 1 : dims + 2, :] * b_scale
    out = a_ref[:dims, :] * a_scale + b_ref[:dims, :] * b_scale
    return out, top, total


def tail(top, total):
    return jnp.concatenate([top, total, jnp.zeros((SUB - 2, top.shape[1]), F32)], axis=0)


def merge_lanes_kernel(a_ref, b_ref, keep_ref, send_ref):
    out, top, total = merged(a_ref, b_ref)
    dims, lanes = out.shape[0], keep_ref.shape[1]
    for ref, at in ((keep_ref, slice(0, lanes)), (send_ref, slice(lanes, 2 * lanes))):
        ref[:dims, :] = out[:, at]
        ref[dims:, :] = tail(top[:, at], total[:, at])


def merge_rows_kernel(step, shard_ref, a_ref, b_ref, keep_ref, send_ref, work):
    out, top, total = merged(a_ref, b_ref)
    rows = keep_ref.shape[0] - SUB
    work[...] = out
    bit = (shard_ref[0] // step) % 2
    for ref, which in ((keep_ref, bit), (send_ref, 1 - bit)):
        ref[:rows, :] = work[aligned(which, rows), :]
        ref[rows:, :] = tail(top, total)


def finish_kernel(a_ref, b_ref, out_ref):
    out, _, total = merged(a_ref, b_ref)
    out_ref[...] = out / total


def stack_rows_kernel(step, shard_ref, a_ref, b_ref, out_ref):
    rows = a_ref.shape[0]
    bit = (shard_ref[0] // step) % 2
    out_ref[aligned(bit, rows), :] = a_ref[...]
    out_ref[aligned(1 - bit, rows), :] = b_ref[...]


def stack_lanes_kernel(a_ref, b_ref, out_ref):
    lanes = a_ref.shape[1]
    out_ref[:, :lanes] = a_ref[...]
    out_ref[:, lanes:] = b_ref[...]


def target_rounds(shard, keep, came):
    dims, lanes = keep.shape[0] - SUB, keep.shape[1] // 2
    devices = lax.axis_size("ctx")
    keep, send = call(merge_lanes_kernel, (keep, came), [((dims + SUB, lanes), F32)] * 2, name="merge")
    came = yield swap(send, "ctx", 2)
    step, rows = devices // 2, dims
    while step >= 4:
        keep, send = call(
            functools.partial(merge_rows_kernel, step),
            (shard, keep, came),
            [((rows // 2 + SUB, lanes), F32)] * 2,
            scratch=[pltpu.VMEM((rows, lanes), F32)],
            name="merge",
        )
        came = yield swap(send, "ctx", step)
        rows //= 2
        step //= 2
    (block,) = call(finish_kernel, (keep, came), [((rows, lanes), F32)], name="finish")
    step = 4
    while step < devices:
        came = yield swap(block, "ctx", step)
        rows *= 2
        (block,) = call(functools.partial(stack_rows_kernel, step), (shard, block, came), [((rows, lanes), F32)], name="stack")
        step *= 2
    came = yield swap(block, "ctx", 2)
    (block,) = call(stack_lanes_kernel, (block, came), [((dims, 2 * lanes), F32)], name="stack")
    came = yield swap(block, "ctx", 1)
    return block, came


def attend_kernel(score_scale, shard_ref, *refs):
    pieces, at_ref, c_all = refs[:4], refs[4], refs[5]
    part, rows = c_all.shape[0] // 4, at_ref.shape[1] // 4
    places = [(shard_ref[0] % 4) ^ s for s in range(4)]
    for place, piece in zip(places, pieces):
        c_all[aligned(place, part), :] = piece[rows:, :]
    for place, piece in zip(places, pieces):
        scores = lax.dot_general(c_all[...], piece[:rows, :], NT, preferred_element_type=F32) * score_scale
        weights = jnp.exp(scores - jnp.max(scores, axis=0, keepdims=True))
        at_ref[:, aligned(place, rows)] = weights / jnp.sum(weights, axis=0, keepdims=True)


def gram_kernel(at_ref, h_ref):
    gram = lax.dot_general(at_ref[...], at_ref[...], NT, precision=HIGH, preferred_element_type=F32)
    kept = gram.shape[0]
    diagonal = lax.broadcasted_iota(jnp.int32, gram.shape, 0) == lax.broadcasted_iota(jnp.int32, gram.shape, 1)
    trace = jnp.sum(jnp.where(diagonal, gram, 0.0))
    h_ref[...] = gram + jnp.where(diagonal, RIDGE_SHARE * trace / kept, 0.0)


def invert_block(rows):
    count = len(rows)
    size = count * SUB
    lane = lax.broadcasted_iota(jnp.int32, (SUB, size), 1)
    sub = lax.broadcasted_iota(jnp.int32, (SUB, size), 0)
    spread = lambda array, column: jnp.broadcast_to(array[:, column : column + 1], (SUB, size))
    line = lambda array, row: jnp.broadcast_to(array[row : row + 1, :], (SUB, size))
    for k in range(count):
        base = k * SUB
        inside = (lane >= base) & (lane < base + SUB)
        columns = [spread(rows[k], base + j) for j in range(SUB)]
        work = jnp.where(inside, jnp.where(lane - base == sub, 1.0, 0.0), rows[k])
        for j in range(SUB):
            here = sub == j
            inverse = 1.0 / line(columns[j], j)
            step = lambda v: (lambda t: jnp.where(here, t, v - columns[j] * t))(line(v, j) * inverse)
            for i in range(j + 1, SUB):
                columns[i] = step(columns[i])
            work = step(work)
        lines = [line(work, j) for j in range(SUB)]
        updated = []
        for i in range(count):
            if i == k:
                updated.append(work)
                continue
            fresh = jnp.where(inside, 0.0, rows[i])
            for j in range(SUB):
                fresh = fresh - spread(rows[i], base + j) * lines[j]
            updated.append(fresh)
        rows = updated
    return rows


def invert_kernel(panel, h_ref, out_ref):
    at = slice(panel * PANEL, (panel + 1) * PANEL)
    block = h_ref[at, at]
    out_ref[...] = jnp.concatenate(
        invert_block([block[i * SUB : (i + 1) * SUB, :] for i in range(PANEL // SUB)]), axis=0
    )


def update_kernel(panel, h_ref, inverse_ref, out_ref):
    at = slice(panel * PANEL, (panel + 1) * PANEL)
    across = h_ref[at, :]
    turned = lax.dot_general(inverse_ref[...], across, NN, precision=HIGH, preferred_element_type=F32)
    out_ref[...] = h_ref[...] - lax.dot_general(across, turned, TN, precision=HIGH, preferred_element_type=F32)
    out_ref[:, at] = turned.T
    out_ref[at, :] = turned
    out_ref[at, at] = -inverse_ref[...]


def fit_kernel(shard_ref, minus_ref, at_ref, own_ref, other_ref, x_ref, err_ref, yt):
    lanes = own_ref.shape[1] // 2
    place = shard_ref[0] % 4
    for s, ref in ((1, own_ref), (3, own_ref), (0, other_ref), (2, other_ref)):
        half = s // 2
        yt[:, aligned(place ^ s, lanes)] = ref[:, half * lanes : (half + 1) * lanes]
    target = yt[...]
    attend = at_ref[...]
    cross = lax.dot_general(target, attend, NT, precision=HIGH, preferred_element_type=F32)
    fitted = -lax.dot_general(cross, minus_ref[...], NN, precision=HIGH, preferred_element_type=F32)
    x_ref[...] = fitted.T
    misfit = lax.dot_general(fitted, attend, NN, precision=HIGH, preferred_element_type=F32) - target
    error = jnp.sum(misfit * misfit) / jnp.sum(target * target)
    err_ref[...] = jnp.full(err_ref.shape, error, F32)


def per_device(queries, keys, values, kept, roots):
    rows, dims = queries.shape[2:]
    slab, count = keys.shape[1], kept.shape[1]
    lanes = rows // 4
    score_scale = 1.0 / math.sqrt(dims)
    shard = lax.axis_index("ctx").astype(jnp.int32).reshape(1)

    pieces, own_keys = spread(shard, queries[0, 0], kept, keys[0], roots)
    (turned,) = call(turn_kernel, (values[0],), [((dims + 16, slab), BF16)], name="turn")
    attend_to = functools.partial(attention, lanes=lanes, keys=own_keys, turned=turned, score_scale=score_scale)
    first = attend_to([pieces[0]])
    send = attend_to([pieces[2]], before=[first])
    keep = attend_to([pieces[1], pieces[3]])
    rounds = target_rounds(shard, keep, swap(send, "ctx", 1))
    came = next(rounds)
    ends = None

    def beside(arrays):
        nonlocal came, ends
        if ends is None:
            arrays, came = lax.optimization_barrier((arrays, came))
            try:
                came = rounds.send(came)
            except StopIteration as stop:
                ends = stop.value
        return arrays

    system_shape = ((count, count), F32)
    (attend,) = call(
        functools.partial(attend_kernel, score_scale),
        (shard, *pieces),
        [((count, rows), F32)],
        10**9,
        scratch=[pltpu.VMEM((count, dims), BF16)],
        name="attend",
    )
    (system,) = call(gram_kernel, (attend,), [system_shape], 4 * 10**9, name="gram")
    system = beside(system)
    panels = count // PANEL
    for panel in range(panels):
        (inverse,) = call(
            functools.partial(invert_kernel, panel), (system,), [((PANEL, PANEL), F32)], 5 * 10**9, name="invert"
        )
        inverse = beside(inverse)
        (system,) = call(
            functools.partial(update_kernel, panel), (system, inverse), [system_shape], 2 * 10**9, name="update"
        )
        if panel == 0 or panel == panels - 1:
            system = beside(system)
    while ends is None:
        system = beside(system)

    compact, error = call(
        fit_kernel,
        (shard, system, attend, *ends),
        [((count, dims), F32), ((SUB, 128), F32)],
        10**9,
        scratch=[pltpu.VMEM((dims, rows), F32)],
        name="fit",
    )
    heads = lax.axis_size("head")
    step = 1
    while step < heads:
        error = error + swap(error, "head", step)
        step *= 2
    return (compact[None], error[0, 0] / heads)


def solution(mesh):
    placed = (
        P("head", "ctx", None, None),
        P("head", "ctx", None),
        P("head", "ctx", None),
        P("head", None),
        P("head"),
    )
    return jax.shard_map(
        per_device,
        mesh=mesh,
        in_specs=placed,
        out_specs=(P("head", None, None), P()),
        check_vma=False,
    )
```

```python
import functools
import math

import jax
import jax.numpy as jnp
from jax import lax
from jax.experimental import pallas as pl
from jax.experimental.pallas import tpu as pltpu
from jax.sharding import PartitionSpec as P

KBLK = 1024
PANEL = 128
SUB = 8
RIDGE_SHARE = 0.01
F32 = jnp.float32
BF16 = jnp.bfloat16
VMEM_LIMIT = 48 * 1024 * 1024
VMEM = pl.BlockSpec(memory_space=pltpu.VMEM)
SMEM = pl.BlockSpec(memory_space=pltpu.SMEM)
HBM = pl.BlockSpec(memory_space=pltpu.HBM)
NT = (((1,), (1,)), ((), ()))
TN = (((0,), (0,)), ((), ()))
NN = (((1,), (0,)), ((), ()))


def swap(array, axis, step):
    size = lax.axis_size(axis)
    return lax.ppermute(array, axis, [(i, i ^ step) for i in range(size)])


def call(kernel, ins, outs, cost=10**5, scratch=(), name=None, specs=None):
    return pl.pallas_call(
        kernel,
        in_specs=specs or [SMEM if x.size == 1 else VMEM for x in ins],
        out_specs=[VMEM] * len(outs),
        out_shape=[jax.ShapeDtypeStruct(shape, kind) for shape, kind in outs],
        scratch_shapes=list(scratch),
        compiler_params=pltpu.CompilerParams(vmem_limit_bytes=VMEM_LIMIT),
        cost_estimate=pl.CostEstimate(flops=cost, bytes_accessed=10**5, transcendentals=0),
        name=name,
    )(*ins)


def aligned(value, unit):
    return pl.ds(pl.multiple_of(value * unit, unit), unit)


def halves(array):
    high = array.astype(BF16)
    return high, (array - high.astype(F32)).astype(BF16)


def dot(left, right, dims):
    return lax.dot_general(left, right, dims, preferred_element_type=F32)


def product(left, right, dims):
    (high, low), (right_high, right_low) = left, right
    rows = high.shape[0]
    both = dot(jnp.concatenate([high, low], axis=0), right_high, dims)
    return both[:rows] + (both[rows:] + dot(high, right_low, dims))


def prepare_kernel(window, shard_ref, root_ref, q_hbm, kept_hbm, k_hbm, *refs):
    outs, k_ref, (q_ref, kept_ref, spots, picked, sems) = refs[:4], refs[4], refs[5:]
    slab, dims = k_ref.shape
    kept = kept_ref.shape[1]
    steps = sems.shape[0] - 2
    chunk = slab // steps
    loads = [pltpu.make_async_copy(kept_hbm, kept_ref, sems.at[steps])]
    for i in range(steps):
        part = pl.ds(i * chunk, chunk)
        loads.append(pltpu.make_async_copy(k_hbm.at[part], k_ref.at[part], sems.at[i]))
    loads.append(pltpu.make_async_copy(q_hbm, q_ref, sems.at[steps + 1]))
    for load in loads:
        load.start()
    base = shard_ref[0] * slab
    loads[0].wait()
    positions = kept_ref[...]
    before = jnp.sum((positions < base).astype(jnp.int32))
    start = jnp.minimum(before // 16, (kept - window) // 16)
    local = (positions - base).astype(F32)
    for i in range(0, kept, 128):
        spots[i : i + 128, :] = jnp.broadcast_to(local[:, i : i + 128], (128, 128)).T
    spot = pl.ds(pl.multiple_of(start * 16, 16), window)
    mine = spots[spot, :]
    column = lax.broadcasted_iota(jnp.int32, (window, 128), 1).astype(F32)
    rows = jnp.zeros((window, dims), F32)
    for i in range(steps):
        onehot = jnp.concatenate(
            [jnp.where(mine == column + float(j), 1.0, 0.0).astype(BF16) for j in range(i * chunk, (i + 1) * chunk, 128)],
            axis=1,
        )
        loads[1 + i].wait()
        rows += lax.dot_general(onehot, k_ref[i * chunk : (i + 1) * chunk, :], NN, preferred_element_type=F32)
    picked[...] = jnp.zeros_like(picked)
    picked[spot, :] = rows.astype(BF16)
    loads[-1].wait()
    share, part = q_ref.shape[0] // 4, kept // 4
    is_root = shard_ref[0] == root_ref[0]
    for s, out in enumerate(outs):
        place = (shard_ref[0] % 4) ^ s
        q = q_ref[aligned(place, share), :]
        out[:share, :] = jnp.where(is_root, q, jnp.zeros_like(q))
        out[share:, :] = picked[aligned(place, part), :]


def sum_kernel(*refs):
    total = refs[0][...]
    for ref in refs[1:-1]:
        total = total + ref[...]
    refs[-1][...] = total


def spread(shard, queries, kept, keys, roots):
    (rows, dims), (slab, _) = queries.shape, keys.shape
    count = kept.shape[1]
    devices = lax.axis_size("ctx")
    tall = ((rows + count) // 4, dims)
    *pieces, keys = call(
        functools.partial(prepare_kernel, 4 * count // devices + 16),
        (shard, roots, queries, kept, keys),
        [(tall, BF16)] * 4 + [(keys.shape, BF16)],
        scratch=[
            pltpu.VMEM((rows, dims), BF16),
            pltpu.VMEM((1, count), jnp.int32),
            pltpu.VMEM((count, 128), F32),
            pltpu.VMEM((count, dims), BF16),
            pltpu.SemaphoreType.DMA((6,)),
        ],
        name="prepare",
        specs=[SMEM, SMEM, HBM, HBM, HBM],
    )
    total = lambda arrays: call(sum_kernel, arrays, [(tall, BF16)], name="total")[0]
    piece = total([pieces[0]] + [swap(pieces[s], "ctx", s) for s in (1, 2, 3)])
    step = 4
    while step < devices:
        ways = math.gcd(devices // step, 4)
        piece = total([piece] + [swap(piece, "ctx", t * step) for t in range(1, ways)])
        step *= ways
    return [piece] + [swap(piece, "ctx", s) for s in (1, 2, 3)], keys


def turn_kernel(v_ref, vt_ref):
    dims = v_ref.shape[1]
    vt_ref[:dims, :] = v_ref[...].T
    vt_ref[dims:, :] = jnp.ones((vt_ref.shape[0] - dims, v_ref.shape[0]), BF16)


def attention_kernel(pieces, lanes, block, score_scale, *refs):
    q_refs, k_ref, vt_ref, before, out_ref = refs[:pieces], refs[pieces], refs[pieces + 1], refs[pieces + 2 : -1], refs[-1]
    dims = k_ref.shape[1]
    blocks = k_ref.shape[0] // block
    factor = score_scale * math.log2(math.e)
    skip = len(before) * lanes
    for ref in before:
        out_ref[:, :skip] = ref[...]

    def scores(i, b):
        return lax.dot_general(
            k_ref[b * block : (b + 1) * block, :], q_refs[i][:lanes, :], NT, preferred_element_type=F32
        )

    stages = [(i, b) for i in range(pieces) for b in range(blocks)]
    ahead = scores(*stages[0])
    for n, (i, b) in enumerate(stages):
        s = ahead
        if n + 1 < len(stages):
            ahead = scores(*stages[n + 1])
        at = slice(skip + i * lanes, skip + (i + 1) * lanes)
        top = jnp.max(s, axis=0, keepdims=True)
        e = jnp.exp2((s - top) * factor).astype(BF16)
        out = lax.dot_general(vt_ref[:, b * block : (b + 1) * block], e, NN, preferred_element_type=F32)
        top = top * factor
        total = out[dims : dims + 1, :]
        out = out[:dims, :]
        if b:
            old_top = out_ref[dims : dims + 1, at]
            joint = jnp.maximum(old_top, top)
            old_scale = jnp.exp2(old_top - joint)
            new_scale = jnp.exp2(top - joint)
            out = out_ref[:dims, at] * old_scale + out * new_scale
            total = out_ref[dims + 1 : dims + 2, at] * old_scale + total * new_scale
            top = joint
        out_ref[:dims, at] = out
        out_ref[dims:, at] = tail(top, total)


def attention(pieces, lanes, keys, turned, score_scale, before=()):
    slab, dims = keys.shape
    return call(
        functools.partial(attention_kernel, len(pieces), lanes, min(KBLK, slab), score_scale),
        (*pieces, keys, turned, *before),
        [((dims + SUB, lanes * (len(pieces) + len(before))), F32)],
        4 * lanes * len(pieces) * slab * dims,
        name="attention",
    )[0]


def merged(a_ref, b_ref):
    dims = a_ref.shape[0] - SUB
    a_top, b_top = a_ref[dims : dims + 1, :], b_ref[dims : dims + 1, :]
    top = jnp.maximum(a_top, b_top)
    a_scale, b_scale = jnp.exp2(a_top - top), jnp.exp2(b_top - top)
    total = a_ref[dims + 1 : dims + 2, :] * a_scale + b_ref[dims + 1 : dims + 2, :] * b_scale
    out = a_ref[:dims, :] * a_scale + b_ref[:dims, :] * b_scale
    return out, top, total


def tail(top, total):
    return jnp.concatenate([top, total, jnp.zeros((SUB - 2, top.shape[1]), F32)], axis=0)


def merge_lanes_kernel(a_ref, b_ref, keep_ref, send_ref):
    out, top, total = merged(a_ref, b_ref)
    dims, lanes = out.shape[0], keep_ref.shape[1]
    for ref, at in ((keep_ref, slice(0, lanes)), (send_ref, slice(lanes, 2 * lanes))):
        ref[:dims, :] = out[:, at]
        ref[dims:, :] = tail(top[:, at], total[:, at])


def merge_rows_kernel(step, shard_ref, a_ref, b_ref, keep_ref, send_ref, work):
    out, top, total = merged(a_ref, b_ref)
    rows = keep_ref.shape[0] - SUB
    work[...] = out
    bit = (shard_ref[0] // step) % 2
    for ref, which in ((keep_ref, bit), (send_ref, 1 - bit)):
        ref[:rows, :] = work[aligned(which, rows), :]
        ref[rows:, :] = tail(top, total)


def finish_kernel(a_ref, b_ref, out_ref):
    out, _, total = merged(a_ref, b_ref)
    out_ref[...] = out / total


def stack_rows_kernel(step, shard_ref, a_ref, b_ref, out_ref):
    rows = a_ref.shape[0]
    bit = (shard_ref[0] // step) % 2
    out_ref[aligned(bit, rows), :] = a_ref[...]
    out_ref[aligned(1 - bit, rows), :] = b_ref[...]


def stack_lanes_kernel(a_ref, b_ref, out_ref):
    lanes = a_ref.shape[1]
    out_ref[:, :lanes] = a_ref[...]
    out_ref[:, lanes:] = b_ref[...]


def target_rounds(shard, keep, came):
    dims, lanes = keep.shape[0] - SUB, keep.shape[1] // 2
    devices = lax.axis_size("ctx")
    keep, send = call(merge_lanes_kernel, (keep, came), [((dims + SUB, lanes), F32)] * 2, name="merge")
    came = yield swap(send, "ctx", 2)
    step, rows = devices // 2, dims
    while step >= 4:
        keep, send = call(
            functools.partial(merge_rows_kernel, step),
            (shard, keep, came),
            [((rows // 2 + SUB, lanes), F32)] * 2,
            scratch=[pltpu.VMEM((rows, lanes), F32)],
            name="merge",
        )
        came = yield swap(send, "ctx", step)
        rows //= 2
        step //= 2
    (block,) = call(finish_kernel, (keep, came), [((rows, lanes), F32)], name="finish")
    step = 4
    while step < devices:
        came = yield swap(block, "ctx", step)
        rows *= 2
        (block,) = call(functools.partial(stack_rows_kernel, step), (shard, block, came), [((rows, lanes), F32)], name="stack")
        step *= 2
    came = yield swap(block, "ctx", 2)
    (block,) = call(stack_lanes_kernel, (block, came), [((dims, 2 * lanes), F32)], name="stack")
    came = yield swap(block, "ctx", 1)
    return block, came


def attend_kernel(score_scale, shard_ref, *refs):
    pieces, (high_ref, low_ref, c_all) = refs[:4], refs[4:]
    part, rows = c_all.shape[0] // 4, high_ref.shape[1] // 4
    places = [(shard_ref[0] % 4) ^ s for s in range(4)]
    for place, piece in zip(places, pieces):
        c_all[aligned(place, part), :] = piece[rows:, :]
    for place, piece in zip(places, pieces):
        scores = lax.dot_general(c_all[...], piece[:rows, :], NT, preferred_element_type=F32) * score_scale
        weights = jnp.exp(scores - jnp.max(scores, axis=0, keepdims=True))
        weights = weights * (1.0 / jnp.sum(weights, axis=0, keepdims=True))
        high_ref[:, aligned(place, rows)], low_ref[:, aligned(place, rows)] = halves(weights)


def gram_kernel(high_ref, low_ref, h_ref):
    high, low = high_ref[...], low_ref[...]
    cross = dot(high, low, NT)
    gram = dot(high, high, NT) + (dot(low, low, NT) + (cross + cross.T))
    kept = gram.shape[0]
    diagonal = lax.broadcasted_iota(jnp.int32, gram.shape, 0) == lax.broadcasted_iota(jnp.int32, gram.shape, 1)
    trace = jnp.sum(jnp.where(diagonal, gram, 0.0))
    h_ref[...] = gram + jnp.where(diagonal, RIDGE_SHARE * trace / kept, 0.0)


def invert_block(rows):
    count = len(rows)
    size = count * SUB
    lane = lax.broadcasted_iota(jnp.int32, (SUB, size), 1)
    sub = lax.broadcasted_iota(jnp.int32, (SUB, size), 0)
    spread_lane = lambda array, column: jnp.broadcast_to(array[:, column : column + 1], (SUB, size))
    line = lambda array, row: jnp.broadcast_to(array[row : row + 1, :], (SUB, size))
    for k in range(count):
        base = k * SUB
        inside = (lane >= base) & (lane < base + SUB)
        columns = [spread_lane(rows[k], base + j) for j in range(SUB)]
        work = jnp.where(inside, jnp.where(lane - base == sub, 1.0, 0.0), rows[k])
        for j in range(0, SUB, 2):
            first, second = columns[j], columns[j + 1]
            a, b, c, d = line(first, j), line(second, j), line(first, j + 1), line(second, j + 1)
            inverse = 1.0 / (a * d - b * c)
            at_first, at_second = sub == j, sub == j + 1

            def step(v):
                upper, lower = line(v, j), line(v, j + 1)
                new_upper = (d * upper - b * lower) * inverse
                new_lower = (a * lower - c * upper) * inverse
                other = v - (first * new_upper + second * new_lower)
                return jnp.where(at_first, new_upper, jnp.where(at_second, new_lower, other))

            for i in range(j + 2, SUB):
                columns[i] = step(columns[i])
            work = step(work)
        lines = [line(work, j) for j in range(SUB)]
        updated = list(rows)
        updated[k] = work
        for i in list(range(k + 1, count)) + list(range(k)):
            terms = [spread_lane(rows[i], base + j) * lines[j] for j in range(SUB)]
            while len(terms) > 1:
                terms = [x + y for x, y in zip(terms[::2], terms[1::2])]
            updated[i] = jnp.where(inside, 0.0, rows[i]) - terms[0]
        rows = updated
    return rows


def invert_kernel(panel, h_ref, out_ref):
    at = slice(panel * PANEL, (panel + 1) * PANEL)
    block = h_ref[at, at]
    out_ref[...] = jnp.concatenate(
        invert_block([block[i * SUB : (i + 1) * SUB, :] for i in range(PANEL // SUB)]), axis=0
    )


def update_kernel(panel, h_ref, inverse_ref, out_ref):
    at = slice(panel * PANEL, (panel + 1) * PANEL)
    turned = product(halves(inverse_ref[...]), halves(h_ref[at, :]), NN)
    out_ref[...] = h_ref[...] - product(halves(h_ref[:, at]), halves(turned), NN)
    out_ref[:, at] = turned.T
    out_ref[at, :] = turned
    out_ref[at, at] = -inverse_ref[...]


def fit_kernel(shard_ref, minus_ref, high_ref, low_ref, own_ref, other_ref, x_ref, err_ref, yt):
    lanes = own_ref.shape[1] // 2
    place = shard_ref[0] % 4
    for s, ref in ((1, own_ref), (3, own_ref), (0, other_ref), (2, other_ref)):
        half = s // 2
        yt[:, aligned(place ^ s, lanes)] = ref[:, half * lanes : (half + 1) * lanes]
    target = yt[...]
    attend = high_ref[...], low_ref[...]
    cross = product(halves(target), attend, NT)
    fitted = -product(halves(cross), halves(minus_ref[...]), NN)
    x_ref[...] = fitted
    misfit = product(halves(fitted), attend, NN) - target
    error = jnp.sum(misfit * misfit) / jnp.sum(target * target)
    err_ref[...] = jnp.full(err_ref.shape, error, F32)


def flip_kernel(x_ref, out_ref):
    out_ref[...] = x_ref[...].T


def mean_kernel(heads, *refs):
    total = refs[0][:1, :1]
    for ref in refs[1:-1]:
        total = total + ref[:1, :1]
    refs[-1][...] = total / heads


def per_device(queries, keys, values, kept, roots):
    rows, dims = queries.shape[2:]
    slab, count = keys.shape[1], kept.shape[1]
    lanes = rows // 4
    score_scale = 1.0 / math.sqrt(dims)
    shard = lax.axis_index("ctx").astype(jnp.int32).reshape(1)

    pieces, own_keys = spread(shard, queries[0, 0], kept, keys[0], roots)
    (turned,) = call(turn_kernel, (values[0],), [((dims + 16, slab), BF16)], name="turn")
    attend_to = functools.partial(attention, lanes=lanes, keys=own_keys, turned=turned, score_scale=score_scale)
    first = attend_to([pieces[0]])
    send = attend_to([pieces[2]], before=[first])
    keep = attend_to([pieces[1], pieces[3]])
    rounds = target_rounds(shard, keep, swap(send, "ctx", 1))
    came = next(rounds)
    ends = None

    def beside(arrays):
        nonlocal came, ends
        if ends is None:
            arrays, came = lax.optimization_barrier((arrays, came))
            try:
                came = rounds.send(came)
            except StopIteration as stop:
                ends = stop.value
        return arrays

    system_shape = ((count, count), F32)
    attend = call(
        functools.partial(attend_kernel, score_scale),
        (shard, *pieces),
        [((count, rows), BF16)] * 2,
        10**9,
        scratch=[pltpu.VMEM((count, dims), BF16)],
        name="attend",
    )
    (system,) = call(gram_kernel, attend, [system_shape], 4 * 10**9, name="gram")
    system = beside(system)
    panels = count // PANEL
    for panel in range(panels):
        (inverse,) = call(
            functools.partial(invert_kernel, panel), (system,), [((PANEL, PANEL), F32)], 5 * 10**9, name="invert"
        )
        inverse = beside(inverse)
        (system,) = call(
            functools.partial(update_kernel, panel), (system, inverse), [system_shape], 2 * 10**9, name="update"
        )
        if panel == 0 or panel == panels - 1:
            system = beside(system)
    while ends is None:
        system = beside(system)

    turned_fit, error = call(
        fit_kernel,
        (shard, system, *attend, *ends),
        [((dims, count), F32), ((SUB, 128), F32)],
        10**9,
        scratch=[pltpu.VMEM((dims, rows), F32)],
        name="fit",
    )
    heads = lax.axis_size("head")
    errors, step = [error], 1
    while step < heads:
        if len(errors) > 1:
            errors = list(call(sum_kernel, errors, [((SUB, 128), F32)], name="total"))
        errors.append(swap(errors[0], "head", step))
        step *= 2
    (compact,) = call(flip_kernel, (turned_fit,), [((count, dims), F32)], 10**6, name="flip")
    (error,) = call(functools.partial(mean_kernel, heads), errors, [((1, 1), F32)], name="mean")
    return (compact[None], error.reshape(()))


def solution(mesh):
    placed = (
        P("head", "ctx", None, None),
        P("head", "ctx", None),
        P("head", "ctx", None),
        P("head", None),
        P("head"),
    )
    return jax.shard_map(
        per_device,
        mesh=mesh,
        in_specs=placed,
        out_specs=(P("head", None, None), P()),
        check_vma=False,
    )
```

```python
import functools
import math

import jax
import jax.numpy as jnp
from jax import lax
from jax.experimental import pallas as pl
from jax.experimental.pallas import tpu as pltpu
from jax.sharding import PartitionSpec as P

KBLK = 1024
PANEL = 64
SUB = 8
RIDGE_SHARE = 0.01
F32 = jnp.float32
BF16 = jnp.bfloat16
VMEM_LIMIT = 48 * 1024 * 1024
VMEM = pl.BlockSpec(memory_space=pltpu.VMEM)
SMEM = pl.BlockSpec(memory_space=pltpu.SMEM)
HBM = pl.BlockSpec(memory_space=pltpu.HBM)
NT = (((1,), (1,)), ((), ()))
TN = (((0,), (0,)), ((), ()))
NN = (((1,), (0,)), ((), ()))


def swap(array, axis, step):
    size = lax.axis_size(axis)
    return lax.ppermute(array, axis, [(i, i ^ step) for i in range(size)])


def call(kernel, ins, outs, cost=10**5, scratch=(), name=None, specs=None):
    return pl.pallas_call(
        kernel,
        in_specs=specs or [SMEM if x.size == 1 else VMEM for x in ins],
        out_specs=[VMEM] * len(outs),
        out_shape=[jax.ShapeDtypeStruct(shape, kind) for shape, kind in outs],
        scratch_shapes=list(scratch),
        compiler_params=pltpu.CompilerParams(vmem_limit_bytes=VMEM_LIMIT),
        cost_estimate=pl.CostEstimate(flops=cost, bytes_accessed=10**5, transcendentals=0),
        name=name,
    )(*ins)


def aligned(value, unit):
    return pl.ds(pl.multiple_of(value * unit, unit), unit)


def halves(array):
    high = array.astype(BF16)
    return high, (array - high.astype(F32)).astype(BF16)


def dot(left, right, dims):
    return lax.dot_general(left, right, dims, preferred_element_type=F32)


def product(left, right, dims):
    (high, low), (right_high, right_low) = left, right
    rows = high.shape[0]
    both = dot(jnp.concatenate([high, low], axis=0), right_high, dims)
    return both[:rows] + (both[rows:] + dot(high, right_low, dims))


def prepare_kernel(window, shard_ref, root_ref, q_hbm, kept_hbm, k_hbm, *refs):
    keep_ref, send_ref, k_ref, q_ref, kept_ref, spots, picked, sems = refs
    slab, dims = k_ref.shape
    kept = kept_ref.shape[1]
    steps = sems.shape[0] - 2
    chunk = slab // steps
    loads = [pltpu.make_async_copy(kept_hbm, kept_ref, sems.at[steps])]
    for i in range(steps):
        part = pl.ds(i * chunk, chunk)
        loads.append(pltpu.make_async_copy(k_hbm.at[part], k_ref.at[part], sems.at[i]))
    loads.append(pltpu.make_async_copy(q_hbm, q_ref, sems.at[steps + 1]))
    for load in loads:
        load.start()
    base = shard_ref[0] * slab
    loads[0].wait()
    positions = kept_ref[...]
    before = jnp.sum((positions < base).astype(jnp.int32))
    start = jnp.minimum(before // 16, (kept - window) // 16)
    local = (positions - base).astype(F32)
    for i in range(0, kept, 128):
        spots[i : i + 128, :] = jnp.broadcast_to(local[:, i : i + 128], (128, 128)).T
    spot = pl.ds(pl.multiple_of(start * 16, 16), window)
    mine = spots[spot, :]
    column = lax.broadcasted_iota(jnp.int32, (window, 128), 1).astype(F32)
    rows = jnp.zeros((window, dims), F32)
    for i in range(steps):
        onehot = jnp.concatenate(
            [jnp.where(mine == column + float(j), 1.0, 0.0).astype(BF16) for j in range(i * chunk, (i + 1) * chunk, 128)],
            axis=1,
        )
        loads[1 + i].wait()
        rows += lax.dot_general(onehot, k_ref[i * chunk : (i + 1) * chunk, :], NN, preferred_element_type=F32)
    picked[...] = jnp.zeros_like(picked)
    picked[spot, :] = rows.astype(BF16)
    loads[-1].wait()
    share, part = q_ref.shape[0] // 4, kept // 4
    is_root = shard_ref[0] == root_ref[0]
    tall = share + part
    for s in range(4):
        out, at = (keep_ref, send_ref)[s % 2], s // 2 * tall
        place = (shard_ref[0] % 4) ^ s
        q = q_ref[aligned(place, share), :]
        out[at : at + share, :] = jnp.where(is_root, q, jnp.zeros_like(q))
        out[at + share : at + tall, :] = picked[aligned(place, part), :]


def sum_kernel(*refs):
    total = refs[0][...]
    for ref in refs[1:-1]:
        total = total + ref[...]
    refs[-1][...] = total


def halve_kernel(a_ref, b_ref, near_ref, far_ref):
    rows = near_ref.shape[0]
    near_ref[...] = a_ref[:rows, :] + b_ref[:rows, :]
    far_ref[...] = a_ref[rows:, :] + b_ref[rows:, :]


def stack_kernel(a_ref, b_ref, out_ref):
    rows = a_ref.shape[0]
    out_ref[:rows, :] = a_ref[...]
    out_ref[rows:, :] = b_ref[...]


def spread(shard, queries, kept, keys, roots):
    (rows, dims), (slab, _) = queries.shape, keys.shape
    count = kept.shape[1]
    devices = lax.axis_size("ctx")
    quarter = ((rows + count) // 4, dims)
    half = (2 * quarter[0], dims)
    in_hbm = lambda x: pltpu.with_memory_space_constraint(x, pltpu.HBM)
    keep, send, keys = call(
        functools.partial(prepare_kernel, 4 * count // devices + 16),
        (shard, roots, in_hbm(queries), in_hbm(kept), in_hbm(keys)),
        [(half, BF16)] * 2 + [(keys.shape, BF16)],
        scratch=[
            pltpu.VMEM((rows, dims), BF16),
            pltpu.VMEM((1, count), jnp.int32),
            pltpu.VMEM((count, 128), F32),
            pltpu.VMEM((count, dims), BF16),
            pltpu.SemaphoreType.DMA((6,)),
        ],
        name="prepare",
        specs=[SMEM, SMEM, HBM, HBM, HBM],
    )
    near, far = call(halve_kernel, (keep, swap(send, "ctx", 1)), [(quarter, BF16)] * 2, name="halve")
    total = lambda arrays: call(sum_kernel, arrays, [(quarter, BF16)], name="total")[0]
    near = total([near, swap(far, "ctx", 2)])
    step = 4
    while step < devices:
        ways = math.gcd(devices // step, 4)
        near = total([near] + [swap(near, "ctx", t * step) for t in range(1, ways)])
        step *= ways
    far = swap(near, "ctx", 2)
    (both,) = call(stack_kernel, (near, far), [(half, BF16)], name="stack")
    return near, far, swap(both, "ctx", 1), keys


def turn_kernel(v_ref, vt_ref):
    dims = v_ref.shape[1]
    vt_ref[:dims, :] = v_ref[...].T
    vt_ref[dims:, :] = jnp.ones((vt_ref.shape[0] - dims, v_ref.shape[0]), BF16)


def quarters_of(ref, rows, tall):
    return [ref[i : i + rows, :] for i in range(0, ref.shape[0], tall)]


def attention_kernel(lanes, tall, block, score_scale, q_ref, k_ref, vt_ref, *refs):
    before, out_ref = refs[:-1], refs[-1]
    quarters = quarters_of(q_ref, lanes, tall)
    dims = k_ref.shape[1]
    blocks = k_ref.shape[0] // block
    factor = score_scale * math.log2(math.e)
    skip = len(before) * lanes
    for ref in before:
        out_ref[:, :skip] = ref[...]

    def scores(i, b):
        return lax.dot_general(
            k_ref[b * block : (b + 1) * block, :], quarters[i], NT, preferred_element_type=F32
        )

    stages = [(i, b) for i in range(len(quarters)) for b in range(blocks)]
    ahead = scores(*stages[0])
    for n, (i, b) in enumerate(stages):
        s = ahead
        if n + 1 < len(stages):
            ahead = scores(*stages[n + 1])
        at = slice(skip + i * lanes, skip + (i + 1) * lanes)
        top = jnp.max(s, axis=0, keepdims=True)
        e = jnp.exp2((s - top) * factor).astype(BF16)
        out = lax.dot_general(vt_ref[:, b * block : (b + 1) * block], e, NN, preferred_element_type=F32)
        top = top * factor
        total = out[dims : dims + 1, :]
        out = out[:dims, :]
        if b:
            old_top = out_ref[dims : dims + 1, at]
            joint = jnp.maximum(old_top, top)
            old_scale = jnp.exp2(old_top - joint)
            new_scale = jnp.exp2(top - joint)
            out = out_ref[:dims, at] * old_scale + out * new_scale
            total = out_ref[dims + 1 : dims + 2, at] * old_scale + total * new_scale
            top = joint
        out_ref[:dims, at] = out
        out_ref[dims:, at] = tail(top, total)


def attention(piece, lanes, tall, keys, turned, score_scale, before=()):
    slab, dims = keys.shape
    count = piece.shape[0] // tall
    return call(
        functools.partial(attention_kernel, lanes, tall, min(KBLK, slab), score_scale),
        (piece, keys, turned, *before),
        [((dims + SUB, lanes * (count + len(before))), F32)],
        4 * lanes * count * slab * dims,
        name="attention",
    )[0]


def merged(a_ref, b_ref):
    dims = a_ref.shape[0] - SUB
    a_top, b_top = a_ref[dims : dims + 1, :], b_ref[dims : dims + 1, :]
    top = jnp.maximum(a_top, b_top)
    a_scale, b_scale = jnp.exp2(a_top - top), jnp.exp2(b_top - top)
    total = a_ref[dims + 1 : dims + 2, :] * a_scale + b_ref[dims + 1 : dims + 2, :] * b_scale
    out = a_ref[:dims, :] * a_scale + b_ref[:dims, :] * b_scale
    return out, top, total


def tail(top, total):
    return jnp.concatenate([top, total, jnp.zeros((SUB - 2, top.shape[1]), F32)], axis=0)


def merge_lanes_kernel(a_ref, b_ref, keep_ref, send_ref):
    out, top, total = merged(a_ref, b_ref)
    dims, lanes = out.shape[0], keep_ref.shape[1]
    for ref, at in ((keep_ref, slice(0, lanes)), (send_ref, slice(lanes, 2 * lanes))):
        ref[:dims, :] = out[:, at]
        ref[dims:, :] = tail(top[:, at], total[:, at])


def merge_rows_kernel(step, shard_ref, a_ref, b_ref, keep_ref, send_ref, work):
    out, top, total = merged(a_ref, b_ref)
    rows = keep_ref.shape[0] - SUB
    work[...] = out
    bit = (shard_ref[0] // step) % 2
    for ref, which in ((keep_ref, bit), (send_ref, 1 - bit)):
        ref[:rows, :] = work[aligned(which, rows), :]
        ref[rows:, :] = tail(top, total)


def finish_kernel(a_ref, b_ref, out_ref):
    out, _, total = merged(a_ref, b_ref)
    out_ref[...] = out / total


def stack_rows_kernel(step, shard_ref, a_ref, b_ref, out_ref):
    rows = a_ref.shape[0]
    bit = (shard_ref[0] // step) % 2
    out_ref[aligned(bit, rows), :] = a_ref[...]
    out_ref[aligned(1 - bit, rows), :] = b_ref[...]


def stack_lanes_kernel(a_ref, b_ref, out_ref):
    lanes = a_ref.shape[1]
    out_ref[:, :lanes] = a_ref[...]
    out_ref[:, lanes:] = b_ref[...]


def target_rounds(shard, keep, came):
    dims, lanes = keep.shape[0] - SUB, keep.shape[1] // 2
    devices = lax.axis_size("ctx")
    keep, send = call(merge_lanes_kernel, (keep, came), [((dims + SUB, lanes), F32)] * 2, name="merge")
    came = yield swap(send, "ctx", 2)
    step, rows = devices // 2, dims
    while step >= 4:
        keep, send = call(
            functools.partial(merge_rows_kernel, step),
            (shard, keep, came),
            [((rows // 2 + SUB, lanes), F32)] * 2,
            scratch=[pltpu.VMEM((rows, lanes), F32)],
            name="merge",
        )
        came = yield swap(send, "ctx", step)
        rows //= 2
        step //= 2
    (block,) = call(finish_kernel, (keep, came), [((rows, lanes), F32)], name="finish")
    step = 4
    while step < devices:
        came = yield swap(block, "ctx", step)
        rows *= 2
        (block,) = call(functools.partial(stack_rows_kernel, step), (shard, block, came), [((rows, lanes), F32)], name="stack")
        step *= 2
    came = yield swap(block, "ctx", 2)
    (block,) = call(stack_lanes_kernel, (block, came), [((dims, 2 * lanes), F32)], name="stack")
    came = yield swap(block, "ctx", 1)
    return block, came


def attend_kernel(score_scale, shard_ref, near_ref, far_ref, other_ref, high_ref, low_ref, c_all):
    part, rows = c_all.shape[0] // 4, high_ref.shape[1] // 4
    tall = part + rows
    pieces = [(near_ref, 0), (other_ref, 0), (far_ref, 0), (other_ref, tall)]
    places = [(shard_ref[0] % 4) ^ s for s in range(4)]
    for place, (ref, at) in zip(places, pieces):
        c_all[aligned(place, part), :] = ref[at + rows : at + tall, :]
    for place, (ref, at) in zip(places, pieces):
        scores = lax.dot_general(c_all[...], ref[at : at + rows, :], NT, preferred_element_type=F32) * score_scale
        weights = jnp.exp(scores - jnp.max(scores, axis=0, keepdims=True))
        weights = weights * (1.0 / jnp.sum(weights, axis=0, keepdims=True))
        high_ref[:, aligned(place, rows)], low_ref[:, aligned(place, rows)] = halves(weights)


def gram_kernel(high_ref, low_ref, h_ref):
    high, low = high_ref[...], low_ref[...]
    cross = dot(high, low, NT)
    gram = dot(high, high, NT) + (dot(low, low, NT) + (cross + cross.T))
    kept = gram.shape[0]
    diagonal = lax.broadcasted_iota(jnp.int32, gram.shape, 0) == lax.broadcasted_iota(jnp.int32, gram.shape, 1)
    trace = jnp.sum(jnp.where(diagonal, gram, 0.0))
    h_ref[...] = gram + jnp.where(diagonal, RIDGE_SHARE * trace / kept, 0.0)


def invert_block(rows):
    count = len(rows)
    size = count * SUB
    lane = lax.broadcasted_iota(jnp.int32, (SUB, size), 1)
    sub = lax.broadcasted_iota(jnp.int32, (SUB, size), 0)
    spread_lane = lambda array, column: jnp.broadcast_to(array[:, column : column + 1], (SUB, size))
    line = lambda array, row: jnp.broadcast_to(array[row : row + 1, :], (SUB, size))
    for k in range(count):
        base = k * SUB
        inside = (lane >= base) & (lane < base + SUB)
        columns = [spread_lane(rows[k], base + j) for j in range(SUB)]
        work = jnp.where(inside, jnp.where(lane - base == sub, 1.0, 0.0), rows[k])
        for j in range(0, SUB, 2):
            first, second = columns[j], columns[j + 1]
            a, b, c, d = line(first, j), line(second, j), line(first, j + 1), line(second, j + 1)
            inverse = 1.0 / (a * d - b * c)
            at_first, at_second = sub == j, sub == j + 1

            def step(v):
                upper, lower = line(v, j), line(v, j + 1)
                new_upper = (d * upper - b * lower) * inverse
                new_lower = (a * lower - c * upper) * inverse
                other = v - (first * new_upper + second * new_lower)
                return jnp.where(at_first, new_upper, jnp.where(at_second, new_lower, other))

            for i in range(j + 2, SUB):
                columns[i] = step(columns[i])
            work = step(work)
        lines = [line(work, j) for j in range(SUB)]
        updated = list(rows)
        updated[k] = work
        for i in list(range(k + 1, count)) + list(range(k)):
            terms = [spread_lane(rows[i], base + j) * lines[j] for j in range(SUB)]
            while len(terms) > 1:
                terms = [x + y for x, y in zip(terms[::2], terms[1::2])]
            updated[i] = jnp.where(inside, 0.0, rows[i]) - terms[0]
        rows = updated
        yield
    return jnp.concatenate(rows, axis=0)


def inverse_beside(block, work=()):
    work = list(work)
    groups = invert_block([block[i : i + SUB, :] for i in range(0, block.shape[0], SUB)])
    while True:
        try:
            next(groups)
        except StopIteration as stop:
            for piece in work:
                piece()
            return stop.value
        if work:
            work.pop(0)()


def invert_kernel(h_ref, out_ref):
    out_ref[...] = inverse_beside(h_ref[:PANEL, :PANEL])


def sweep_kernel(panel, h_ref, inverse_ref, out_ref, *next_ref):
    size = h_ref.shape[0]
    at = slice(panel * PANEL, (panel + 1) * PANEL)
    wide = slice(panel * PANEL // 128 * 128, panel * PANEL // 128 * 128 + 128)
    offset = at.start - wide.start
    inverse = inverse_ref[...]
    turned = product(halves(inverse), halves(h_ref[at, :]), NN)
    padded = jnp.concatenate(
        [turned if i == offset else jnp.zeros_like(turned) for i in range(0, 128, PANEL)], axis=0
    )
    split = halves(padded)
    columns = padded.T
    lane = lax.broadcasted_iota(jnp.int32, (128, 128), 1)
    inside = (lane >= offset) & (lane < offset + PANEL)

    def rows_update(i):
        def piece():
            rows = slice(i, i + 128)
            old = h_ref[rows, :]
            out_ref[rows, :] = old - product(halves(h_ref[rows, wide]), split, NN)
            out_ref[rows, wide] = jnp.where(inside, columns[rows, :], out_ref[rows, wide])
            if i == wide.start:
                out_ref[at, :] = turned
                out_ref[at, at] = -inverse

        return piece

    work = [rows_update(i) for i in range(0, size, 128)]
    if next_ref:
        after = slice(at.stop, at.stop + PANEL)
        block = h_ref[after, after] - product(
            halves(h_ref[after, wide]), tuple(x[:, after] for x in split), NN
        )
        next_ref[0][...] = inverse_beside(block, work)
    else:
        for piece in work:
            piece()


def fit_kernel(shard_ref, minus_ref, high_ref, low_ref, own_ref, other_ref, x_ref, err_ref, yt):
    lanes = own_ref.shape[1] // 2
    place = shard_ref[0] % 4
    for s, ref in ((1, own_ref), (3, own_ref), (0, other_ref), (2, other_ref)):
        half = s // 2
        yt[:, aligned(place ^ s, lanes)] = ref[:, half * lanes : (half + 1) * lanes]
    target = yt[...]
    attend = high_ref[...], low_ref[...]
    cross = product(halves(target), attend, NT)
    fitted = -product(halves(cross), halves(minus_ref[...]), NN)
    x_ref[...] = fitted
    misfit = product(halves(fitted), attend, NN) - target
    error = jnp.sum(misfit * misfit) / jnp.sum(target * target)
    err_ref[...] = jnp.full(err_ref.shape, error, F32)


def flip_kernel(x_ref, out_ref):
    out_ref[...] = x_ref[...].T


def mean_kernel(heads, *refs):
    total = refs[0][:1, :1]
    for ref in refs[1:-1]:
        total = total + ref[:1, :1]
    refs[-1][...] = total / heads


def per_device(queries, keys, values, kept, roots):
    rows, dims = queries.shape[2:]
    slab, count = keys.shape[1], kept.shape[1]
    lanes = rows // 4
    score_scale = 1.0 / math.sqrt(dims)
    shard = lax.axis_index("ctx").astype(jnp.int32).reshape(1)

    near, far, other, own_keys = spread(shard, queries[0, 0], kept, keys[0], roots)
    (turned,) = call(turn_kernel, (values[0],), [((dims + 16, slab), BF16)], name="turn")
    attend_to = functools.partial(
        attention, lanes=lanes, tall=near.shape[0], keys=own_keys, turned=turned, score_scale=score_scale
    )
    send = attend_to(far, before=[attend_to(near)])
    keep = attend_to(other)
    rounds = target_rounds(shard, keep, swap(send, "ctx", 1))
    came = next(rounds)
    ends = None

    def beside(arrays):
        nonlocal came, ends
        if ends is None:
            arrays, came = lax.optimization_barrier((arrays, came))
            try:
                came = rounds.send(came)
            except StopIteration as stop:
                ends = stop.value
        return arrays

    system_shape = ((count, count), F32)
    attend = call(
        functools.partial(attend_kernel, score_scale),
        (shard, near, far, other),
        [((count, rows), BF16)] * 2,
        10**9,
        scratch=[pltpu.VMEM((count, dims), BF16)],
        name="attend",
    )
    (system,) = call(gram_kernel, attend, [system_shape], 4 * 10**9, name="gram")
    panels = count // PANEL
    block_shape = ((PANEL, PANEL), F32)
    (inverse,) = call(invert_kernel, (system,), [block_shape], 10**9, name="invert")
    system, inverse = beside((system, inverse))
    for panel in range(panels):
        last = panel == panels - 1
        system, *inverse = call(
            functools.partial(sweep_kernel, panel),
            (system, inverse),
            [system_shape] if last else [system_shape, block_shape],
            2 * 10**9,
            name="sweep",
        )
        inverse = None if last else inverse[0]
        if inverse is not None:
            system, inverse = beside((system, inverse))
        else:
            system = beside(system)
    while ends is None:
        system = beside(system)

    turned_fit, error = call(
        fit_kernel,
        (shard, system, *attend, *ends),
        [((dims, count), F32), ((SUB, 128), F32)],
        10**9,
        scratch=[pltpu.VMEM((dims, rows), F32)],
        name="fit",
    )
    heads = lax.axis_size("head")
    errors, step = [error], 1
    while step < heads:
        if len(errors) > 1:
            errors = list(call(sum_kernel, errors, [((SUB, 128), F32)], name="total"))
        errors.append(swap(errors[0], "head", step))
        step *= 2
    (compact,) = call(flip_kernel, (turned_fit,), [((count, dims), F32)], 10**6, name="flip")
    (error,) = call(functools.partial(mean_kernel, heads), errors, [((1, 1), F32)], name="mean")
    return (compact[None], error.reshape(()))


def solution(mesh):
    placed = (
        P("head", "ctx", None, None),
        P("head", "ctx", None),
        P("head", "ctx", None),
        P("head", None),
        P("head"),
    )
    return jax.shard_map(
        per_device,
        mesh=mesh,
        in_specs=placed,
        out_specs=(P("head", None, None), P()),
        check_vma=False,
    )
```

```python
import functools
import math

import jax
import jax.numpy as jnp
from jax import lax
from jax.experimental import pallas as pl
from jax.experimental.pallas import tpu as pltpu
from jax.sharding import PartitionSpec as P

KBLK = 1024
PANEL = 64
SUB = 8
RIDGE_SHARE = 0.01
F32 = jnp.float32
BF16 = jnp.bfloat16
VMEM_LIMIT = 48 * 1024 * 1024
VMEM = pl.BlockSpec(memory_space=pltpu.VMEM)
SMEM = pl.BlockSpec(memory_space=pltpu.SMEM)
HBM = pl.BlockSpec(memory_space=pltpu.HBM)
NT = (((1,), (1,)), ((), ()))
TN = (((0,), (0,)), ((), ()))
NN = (((1,), (0,)), ((), ()))


def swap(array, axis, step):
    size = lax.axis_size(axis)
    return lax.ppermute(array, axis, [(i, i ^ step) for i in range(size)])


def call(kernel, ins, outs, cost=10**5, scratch=(), name=None, specs=None):
    return pl.pallas_call(
        kernel,
        in_specs=specs or [SMEM if x.size == 1 else VMEM for x in ins],
        out_specs=[VMEM] * len(outs),
        out_shape=[jax.ShapeDtypeStruct(shape, kind) for shape, kind in outs],
        scratch_shapes=list(scratch),
        compiler_params=pltpu.CompilerParams(vmem_limit_bytes=VMEM_LIMIT),
        cost_estimate=pl.CostEstimate(flops=cost, bytes_accessed=10**5, transcendentals=0),
        name=name,
    )(*ins)


def aligned(value, unit):
    return pl.ds(pl.multiple_of(value * unit, unit), unit)


def halves(array):
    high = array.astype(BF16)
    return high, (array - high.astype(F32)).astype(BF16)


def dot(left, right, dims):
    return lax.dot_general(left, right, dims, preferred_element_type=F32)


def product(left, right, dims):
    (high, low), (right_high, right_low) = left, right
    rows = high.shape[0]
    both = dot(jnp.concatenate([high, low], axis=0), right_high, dims)
    return both[:rows] + (both[rows:] + dot(high, right_low, dims))


def prepare_kernel(window, shard_ref, root_ref, q_hbm, kept_hbm, k_hbm, *refs):
    keep_ref, send_ref, k_ref, q_ref, kept_ref, spots, picked, sems = refs
    slab, dims = k_ref.shape
    kept = kept_ref.shape[1]
    steps = sems.shape[0] - 2
    chunk = slab // steps
    loads = [pltpu.make_async_copy(kept_hbm, kept_ref, sems.at[steps])]
    for i in range(steps):
        part = pl.ds(i * chunk, chunk)
        loads.append(pltpu.make_async_copy(k_hbm.at[part], k_ref.at[part], sems.at[i]))
    loads.append(pltpu.make_async_copy(q_hbm, q_ref, sems.at[steps + 1]))
    for load in loads:
        load.start()
    base = shard_ref[0] * slab
    loads[0].wait()
    positions = kept_ref[...]
    before = jnp.sum((positions < base).astype(jnp.int32))
    start = jnp.minimum(before // 16, (kept - window) // 16)
    local = (positions - base).astype(F32)
    for i in range(0, kept, 128):
        spots[i : i + 128, :] = jnp.broadcast_to(local[:, i : i + 128], (128, 128)).T
    spot = pl.ds(pl.multiple_of(start * 16, 16), window)
    mine = spots[spot, :]
    column = lax.broadcasted_iota(jnp.int32, (window, 128), 1).astype(F32)
    rows = jnp.zeros((window, dims), F32)
    for i in range(steps):
        onehot = jnp.concatenate(
            [jnp.where(mine == column + float(j), 1.0, 0.0).astype(BF16) for j in range(i * chunk, (i + 1) * chunk, 128)],
            axis=1,
        )
        loads[1 + i].wait()
        rows += lax.dot_general(onehot, k_ref[i * chunk : (i + 1) * chunk, :], NN, preferred_element_type=F32)
    picked[...] = jnp.zeros_like(picked)
    picked[spot, :] = rows.astype(BF16)
    loads[-1].wait()
    share, part = q_ref.shape[0] // 4, kept // 4
    is_root = shard_ref[0] == root_ref[0]
    tall = share + part
    for s in range(4):
        out, at = (keep_ref, send_ref)[s % 2], s // 2 * tall
        place = (shard_ref[0] % 4) ^ s
        q = q_ref[aligned(place, share), :]
        out[at : at + share, :] = jnp.where(is_root, q, jnp.zeros_like(q))
        out[at + share : at + tall, :] = picked[aligned(place, part), :]


def sum_kernel(*refs):
    total = refs[0][...]
    for ref in refs[1:-1]:
        total = total + ref[...]
    refs[-1][...] = total


def halve_kernel(a_ref, b_ref, near_ref, far_ref):
    rows = near_ref.shape[0]
    near_ref[...] = a_ref[:rows, :] + b_ref[:rows, :]
    far_ref[...] = a_ref[rows:, :] + b_ref[rows:, :]


def stack_kernel(a_ref, b_ref, out_ref):
    rows = a_ref.shape[0]
    out_ref[:rows, :] = a_ref[...]
    out_ref[rows:, :] = b_ref[...]


def spread(shard, queries, kept, keys, roots, values, attend_to):
    (rows, dims), (slab, _) = queries.shape, keys.shape
    count = kept.shape[1]
    devices = lax.axis_size("ctx")
    quarter = ((rows + count) // 4, dims)
    half = (2 * quarter[0], dims)
    in_hbm = lambda x: pltpu.with_memory_space_constraint(x, pltpu.HBM)
    keep, send, keys = call(
        functools.partial(prepare_kernel, 4 * count // devices + 16),
        (shard, roots, in_hbm(queries), in_hbm(kept), in_hbm(keys)),
        [(half, BF16)] * 2 + [(keys.shape, BF16)],
        scratch=[
            pltpu.VMEM((rows, dims), BF16),
            pltpu.VMEM((1, count), jnp.int32),
            pltpu.VMEM((count, 128), F32),
            pltpu.VMEM((count, dims), BF16),
            pltpu.SemaphoreType.DMA((6,)),
        ],
        name="prepare",
        specs=[SMEM, SMEM, HBM, HBM, HBM],
    )
    near, far = call(halve_kernel, (keep, swap(send, "ctx", 1)), [(quarter, BF16)] * 2, name="halve")
    total = lambda arrays: call(sum_kernel, arrays, [(quarter, BF16)], name="total")[0]
    came = swap(far, "ctx", 2)
    (turned,) = call(turn_kernel, (values,), [((dims + 16, slab), BF16)], 10**7, name="turn")
    came, turned = lax.optimization_barrier((came, turned))
    near = total([near, came])
    step = 4
    while step < devices:
        ways = math.gcd(devices // step, 4)
        near = total([near] + [swap(near, "ctx", t * step) for t in range(1, ways)])
        step *= ways
    far = swap(near, "ctx", 2)
    first = attend_to(near, keys, turned)
    far, first = lax.optimization_barrier((far, first))
    (both,) = call(stack_kernel, (near, far), [(half, BF16)], name="stack")
    other = swap(both, "ctx", 1)
    send = attend_to(far, keys, turned, before=[first])
    other, send = lax.optimization_barrier((other, send))
    came = swap(send, "ctx", 1)
    return near, far, other, attend_to(other, keys, turned), came


def turn_kernel(v_ref, vt_ref):
    dims = v_ref.shape[1]
    vt_ref[:dims, :] = v_ref[...].T
    vt_ref[dims:, :] = jnp.ones((vt_ref.shape[0] - dims, v_ref.shape[0]), BF16)


def quarters_of(ref, rows, tall):
    return [ref[i : i + rows, :] for i in range(0, ref.shape[0], tall)]


def attention_kernel(lanes, tall, block, score_scale, q_ref, k_ref, vt_ref, *refs):
    before, out_ref = refs[:-1], refs[-1]
    quarters = quarters_of(q_ref, lanes, tall)
    dims = k_ref.shape[1]
    blocks = k_ref.shape[0] // block
    factor = score_scale * math.log2(math.e)
    skip = len(before) * lanes
    for ref in before:
        out_ref[:, :skip] = ref[...]

    def scores(i, b):
        return lax.dot_general(
            k_ref[b * block : (b + 1) * block, :], quarters[i], NT, preferred_element_type=F32
        )

    stages = [(i, b) for i in range(len(quarters)) for b in range(blocks)]
    ahead = scores(*stages[0])
    for n, (i, b) in enumerate(stages):
        s = ahead
        if n + 1 < len(stages):
            ahead = scores(*stages[n + 1])
        at = slice(skip + i * lanes, skip + (i + 1) * lanes)
        top = jnp.max(s, axis=0, keepdims=True)
        e = jnp.exp2((s - top) * factor).astype(BF16)
        out = lax.dot_general(vt_ref[:, b * block : (b + 1) * block], e, NN, preferred_element_type=F32)
        top = top * factor
        total = out[dims : dims + 1, :]
        out = out[:dims, :]
        if b:
            old_top = out_ref[dims : dims + 1, at]
            joint = jnp.maximum(old_top, top)
            old_scale = jnp.exp2(old_top - joint)
            new_scale = jnp.exp2(top - joint)
            out = out_ref[:dims, at] * old_scale + out * new_scale
            total = out_ref[dims + 1 : dims + 2, at] * old_scale + total * new_scale
            top = joint
        out_ref[:dims, at] = out
        out_ref[dims:, at] = tail(top, total)


def attention(lanes, tall, score_scale, piece, keys, turned, before=()):
    slab, dims = keys.shape
    count = piece.shape[0] // tall
    return call(
        functools.partial(attention_kernel, lanes, tall, min(KBLK, slab), score_scale),
        (piece, keys, turned, *before),
        [((dims + SUB, lanes * (count + len(before))), F32)],
        4 * lanes * count * slab * dims,
        name="attention",
    )[0]


def merged(*refs):
    dims = refs[0].shape[0] - SUB
    tops = [ref[dims : dims + 1, :] for ref in refs]
    top = functools.reduce(jnp.maximum, tops)
    scales = [jnp.exp2(t - top) for t in tops]
    total = sum(ref[dims + 1 : dims + 2, :] * scale for ref, scale in zip(refs, scales))
    out = sum(ref[:dims, :] * scale for ref, scale in zip(refs, scales))
    return out, top, total


def tail(top, total):
    return jnp.concatenate([top, total, jnp.zeros((SUB - 2, top.shape[1]), F32)], axis=0)


def merge_lanes_kernel(a_ref, b_ref, keep_ref, send_ref):
    out, top, total = merged(a_ref, b_ref)
    dims, lanes = out.shape[0], keep_ref.shape[1]
    for ref, at in ((keep_ref, slice(0, lanes)), (send_ref, slice(lanes, 2 * lanes))):
        ref[:dims, :] = out[:, at]
        ref[dims:, :] = tail(top[:, at], total[:, at])


def merge_rows_kernel(step, shard_ref, *refs):
    work, refs = refs[-1], refs[:-1]
    ways = sum(1 for ref in refs if ref.shape[0] != refs[0].shape[0])
    ins, outs = refs[:-ways], refs[-ways:]
    out, top, total = merged(*ins)
    rows = outs[0].shape[0] - SUB
    work[...] = out
    digit = (shard_ref[0] // step) % ways
    for t, ref in enumerate(outs):
        ref[:rows, :] = work[aligned(digit ^ t, rows), :]
        ref[rows:, :] = tail(top, total)


def finish_kernel(*refs):
    out, _, total = merged(*refs[:-1])
    refs[-1][...] = out / total


def stack_rows_kernel(step, shard_ref, *refs):
    ins, out_ref = refs[:-1], refs[-1]
    rows = ins[0].shape[0]
    digit = (shard_ref[0] // step) % len(ins)
    for t, ref in enumerate(ins):
        out_ref[aligned(digit ^ t, rows), :] = ref[...]


def stack_lanes_kernel(a_ref, b_ref, out_ref):
    lanes = a_ref.shape[1]
    out_ref[:, :lanes] = a_ref[...]
    out_ref[:, lanes:] = b_ref[...]


def target_rounds(shard, keep, came):
    dims, lanes = keep.shape[0] - SUB, keep.shape[1] // 2
    devices = lax.axis_size("ctx")
    keep, send = call(merge_lanes_kernel, (keep, came), [((dims + SUB, lanes), F32)] * 2, name="merge")
    came = yield [swap(send, "ctx", 2)]
    digits, step = [], devices
    while step > 4:
        ways = math.gcd(step // 4, 4)
        step //= ways
        digits.append((step, ways))
    rows = dims
    for step, ways in digits:
        keep, *send = call(
            functools.partial(merge_rows_kernel, step),
            (shard, keep, *came),
            [((rows // ways + SUB, lanes), F32)] * ways,
            scratch=[pltpu.VMEM((rows, lanes), F32)],
            name="merge",
        )
        came = yield [swap(x, "ctx", t * step) for t, x in enumerate(send, 1)]
        rows //= ways
    (block,) = call(finish_kernel, (keep, *came), [((rows, lanes), F32)], name="finish")
    for step, ways in reversed(digits):
        came = yield [swap(block, "ctx", t * step) for t in range(1, ways)]
        rows *= ways
        (block,) = call(
            functools.partial(stack_rows_kernel, step), (shard, block, *came), [((rows, lanes), F32)], name="stack"
        )
    came = yield [swap(block, "ctx", 2)]
    (block,) = call(stack_lanes_kernel, (block, *came), [((dims, 2 * lanes), F32)], name="stack")
    came = yield [swap(block, "ctx", 1)]
    return block, *came


def attend_kernel(score_scale, shard_ref, near_ref, far_ref, other_ref, high_ref, low_ref, c_all):
    part, rows = c_all.shape[0] // 4, high_ref.shape[1] // 4
    tall = part + rows
    pieces = [(near_ref, 0), (other_ref, 0), (far_ref, 0), (other_ref, tall)]
    places = [(shard_ref[0] % 4) ^ s for s in range(4)]
    for place, (ref, at) in zip(places, pieces):
        c_all[aligned(place, part), :] = ref[at + rows : at + tall, :]
    for place, (ref, at) in zip(places, pieces):
        scores = lax.dot_general(c_all[...], ref[at : at + rows, :], NT, preferred_element_type=F32) * score_scale
        weights = jnp.exp(scores - jnp.max(scores, axis=0, keepdims=True))
        weights = weights * (1.0 / jnp.sum(weights, axis=0, keepdims=True))
        high_ref[:, aligned(place, rows)], low_ref[:, aligned(place, rows)] = halves(weights)


def gram_kernel(high_ref, low_ref, h_ref):
    high, low = high_ref[...], low_ref[...]
    cross = dot(high, low, NT)
    gram = dot(high, high, NT) + (dot(low, low, NT) + (cross + cross.T))
    kept = gram.shape[0]
    diagonal = lax.broadcasted_iota(jnp.int32, gram.shape, 0) == lax.broadcasted_iota(jnp.int32, gram.shape, 1)
    trace = jnp.sum(jnp.where(diagonal, gram, 0.0))
    h_ref[...] = gram + jnp.where(diagonal, RIDGE_SHARE * trace / kept, 0.0)


def invert_block(rows):
    count = len(rows)
    size = count * SUB
    lane = lax.broadcasted_iota(jnp.int32, (SUB, size), 1)
    sub = lax.broadcasted_iota(jnp.int32, (SUB, size), 0)
    spread_lane = lambda array, column: jnp.broadcast_to(array[:, column : column + 1], (SUB, size))
    line = lambda array, row: jnp.broadcast_to(array[row : row + 1, :], (SUB, size))
    for k in range(count):
        base = k * SUB
        inside = (lane >= base) & (lane < base + SUB)
        columns = [spread_lane(rows[k], base + j) for j in range(SUB)]
        work = jnp.where(inside, jnp.where(lane - base == sub, 1.0, 0.0), rows[k])
        for j in range(0, SUB, 2):
            first, second = columns[j], columns[j + 1]
            a, b, c, d = line(first, j), line(second, j), line(first, j + 1), line(second, j + 1)
            inverse = 1.0 / (a * d - b * c)
            at_first, at_second = sub == j, sub == j + 1

            def step(v):
                upper, lower = line(v, j), line(v, j + 1)
                new_upper = (d * upper - b * lower) * inverse
                new_lower = (a * lower - c * upper) * inverse
                other = v - (first * new_upper + second * new_lower)
                return jnp.where(at_first, new_upper, jnp.where(at_second, new_lower, other))

            for i in range(j + 2, SUB):
                columns[i] = step(columns[i])
            work = step(work)
        lines = [line(work, j) for j in range(SUB)]
        updated = list(rows)
        updated[k] = work
        for i in list(range(k + 1, count)) + list(range(k)):
            terms = [spread_lane(rows[i], base + j) * lines[j] for j in range(SUB)]
            while len(terms) > 1:
                terms = [x + y for x, y in zip(terms[::2], terms[1::2])]
            updated[i] = jnp.where(inside, 0.0, rows[i]) - terms[0]
        rows = updated
        yield
    return jnp.concatenate(rows, axis=0)


def inverse_beside(block, work=()):
    work = list(work)
    groups = invert_block([block[i : i + SUB, :] for i in range(0, block.shape[0], SUB)])
    while True:
        try:
            next(groups)
        except StopIteration as stop:
            for piece in work:
                piece()
            return stop.value
        if work:
            work.pop(0)()


def invert_kernel(h_ref, out_ref):
    out_ref[...] = inverse_beside(h_ref[:PANEL, :PANEL])


def sweep_kernel(panel, h_ref, inverse_ref, out_ref, *next_ref):
    size = h_ref.shape[0]
    at = slice(panel * PANEL, (panel + 1) * PANEL)
    wide = slice(panel * PANEL // 128 * 128, panel * PANEL // 128 * 128 + 128)
    offset = at.start - wide.start
    inverse = inverse_ref[...]
    turned = product(halves(inverse), halves(h_ref[at, :]), NN)
    padded = jnp.concatenate(
        [turned if i == offset else jnp.zeros_like(turned) for i in range(0, 128, PANEL)], axis=0
    )
    split = halves(padded)
    columns = padded.T
    lane = lax.broadcasted_iota(jnp.int32, (128, 128), 1)
    inside = (lane >= offset) & (lane < offset + PANEL)

    def rows_update(i):
        def piece():
            rows = slice(i, i + 128)
            old = h_ref[rows, :]
            out_ref[rows, :] = old - product(halves(h_ref[rows, wide]), split, NN)
            out_ref[rows, wide] = jnp.where(inside, columns[rows, :], out_ref[rows, wide])
            if i == wide.start:
                out_ref[at, :] = turned
                out_ref[at, at] = -inverse

        return piece

    work = [rows_update(i) for i in range(0, size, 128)]
    if next_ref:
        after = slice(at.stop, at.stop + PANEL)
        block = h_ref[after, after] - product(
            halves(h_ref[after, wide]), tuple(x[:, after] for x in split), NN
        )
        next_ref[0][...] = inverse_beside(block, work)
    else:
        for piece in work:
            piece()


def fit_kernel(shard_ref, minus_ref, high_ref, low_ref, own_ref, other_ref, x_ref, err_ref, yt):
    lanes = own_ref.shape[1] // 2
    place = shard_ref[0] % 4
    for s, ref in ((1, own_ref), (3, own_ref), (0, other_ref), (2, other_ref)):
        half = s // 2
        yt[:, aligned(place ^ s, lanes)] = ref[:, half * lanes : (half + 1) * lanes]
    target = yt[...]
    attend = high_ref[...], low_ref[...]
    cross = product(halves(target), attend, NT)
    fitted = -product(halves(cross), halves(minus_ref[...]), NN)
    x_ref[...] = fitted
    misfit = product(halves(fitted), attend, NN) - target
    error = jnp.sum(misfit * misfit) / jnp.sum(target * target)
    err_ref[...] = jnp.full(err_ref.shape, error, F32)


def flip_kernel(x_ref, out_ref):
    out_ref[...] = x_ref[...].T


def mean_kernel(heads, *refs):
    total = refs[0][:1, :1]
    for ref in refs[1:-1]:
        total = total + ref[:1, :1]
    refs[-1][...] = total / heads


def per_device(queries, keys, values, kept, roots):
    rows, dims = queries.shape[2:]
    slab, count = keys.shape[1], kept.shape[1]
    lanes = rows // 4
    score_scale = 1.0 / math.sqrt(dims)
    shard = lax.axis_index("ctx").astype(jnp.int32).reshape(1)

    attend_to = functools.partial(attention, lanes, (rows + count) // 4, score_scale)
    near, far, other, keep, came = spread(shard, queries[0, 0], kept, keys[0], roots, values[0], attend_to)
    rounds = target_rounds(shard, keep, came)
    came = next(rounds)
    ends = None

    def beside(arrays):
        nonlocal came, ends
        if ends is None:
            arrays, came = lax.optimization_barrier((arrays, came))
            try:
                came = rounds.send(came)
            except StopIteration as stop:
                ends = stop.value
        return arrays

    system_shape = ((count, count), F32)
    attend = call(
        functools.partial(attend_kernel, score_scale),
        (shard, near, far, other),
        [((count, rows), BF16)] * 2,
        10**9,
        scratch=[pltpu.VMEM((count, dims), BF16)],
        name="attend",
    )
    (system,) = call(gram_kernel, attend, [system_shape], 4 * 10**9, name="gram")
    panels = count // PANEL
    block_shape = ((PANEL, PANEL), F32)
    (inverse,) = call(invert_kernel, (system,), [block_shape], 10**9, name="invert")
    system, inverse = beside((system, inverse))
    for panel in range(panels):
        last = panel == panels - 1
        system, *inverse = call(
            functools.partial(sweep_kernel, panel),
            (system, inverse),
            [system_shape] if last else [system_shape, block_shape],
            2 * 10**9,
            name="sweep",
        )
        inverse = None if last else inverse[0]
        if panel % 2 == 1 or panel >= panels - 2:
            system, inverse = beside((system, inverse))
    while ends is None:
        system = beside(system)

    turned_fit, error = call(
        fit_kernel,
        (shard, system, *attend, *ends),
        [((dims, count), F32), ((SUB, 128), F32)],
        10**9,
        scratch=[pltpu.VMEM((dims, rows), F32)],
        name="fit",
    )
    heads = lax.axis_size("head")
    errors, step = [error], 1
    while step < heads:
        if len(errors) > 1:
            errors = list(call(sum_kernel, errors, [((SUB, 128), F32)], name="total"))
        errors.append(swap(errors[0], "head", step))
        step *= 2
    (compact,) = call(flip_kernel, (turned_fit,), [((count, dims), F32)], 10**6, name="flip")
    (error,) = call(functools.partial(mean_kernel, heads), errors, [((1, 1), F32)], name="mean")
    return (compact[None], error.reshape(()))


def solution(mesh):
    placed = (
        P("head", "ctx", None, None),
        P("head", "ctx", None),
        P("head", "ctx", None),
        P("head", None),
        P("head"),
    )
    return jax.shard_map(
        per_device,
        mesh=mesh,
        in_specs=placed,
        out_specs=(P("head", None, None), P()),
        check_vma=False,
    )
```

```python
import functools
import math

import jax
import jax.numpy as jnp
from jax import lax
from jax.experimental import pallas as pl
from jax.experimental.pallas import tpu as pltpu
from jax.sharding import PartitionSpec as P

KBLK = 1024
PANEL = 64
SUB = 8
RIDGE_SHARE = 0.01
F32 = jnp.float32
BF16 = jnp.bfloat16
VMEM_LIMIT = 48 * 1024 * 1024
VMEM = pl.BlockSpec(memory_space=pltpu.VMEM)
SMEM = pl.BlockSpec(memory_space=pltpu.SMEM)
HBM = pl.BlockSpec(memory_space=pltpu.HBM)
NT = (((1,), (1,)), ((), ()))
TN = (((0,), (0,)), ((), ()))
NN = (((1,), (0,)), ((), ()))


def swap(array, axis, step):
    size = lax.axis_size(axis)
    return lax.ppermute(array, axis, [(i, i ^ step) for i in range(size)])


def call(kernel, ins, outs, cost=10**5, scratch=(), name=None, specs=None):
    return pl.pallas_call(
        kernel,
        in_specs=specs or [SMEM if x.size == 1 else VMEM for x in ins],
        out_specs=[VMEM] * len(outs),
        out_shape=[jax.ShapeDtypeStruct(shape, kind) for shape, kind in outs],
        scratch_shapes=list(scratch),
        compiler_params=pltpu.CompilerParams(vmem_limit_bytes=VMEM_LIMIT),
        cost_estimate=pl.CostEstimate(flops=cost, bytes_accessed=10**5, transcendentals=0),
        name=name,
    )(*ins)


def aligned(value, unit):
    return pl.ds(pl.multiple_of(value * unit, unit), unit)


def halves(array):
    high = array.astype(BF16)
    return high, (array - high.astype(F32)).astype(BF16)


def dot(left, right, dims):
    return lax.dot_general(left, right, dims, preferred_element_type=F32)


def product(left, right, dims):
    (high, low), (right_high, right_low) = left, right
    rows = high.shape[0]
    both = dot(jnp.concatenate([high, low], axis=0), right_high, dims)
    return both[:rows] + (both[rows:] + dot(high, right_low, dims))


def prepare_kernel(window, shard_ref, root_ref, q_hbm, kept_hbm, k_hbm, *refs):
    keep_ref, send_ref, k_ref, q_ref, kept_ref, spots, picked, sems = refs
    slab, dims = k_ref.shape
    kept = kept_ref.shape[1]
    steps = sems.shape[0] - 2
    chunk = slab // steps
    loads = [pltpu.make_async_copy(kept_hbm, kept_ref, sems.at[steps])]
    for i in range(steps):
        part = pl.ds(i * chunk, chunk)
        loads.append(pltpu.make_async_copy(k_hbm.at[part], k_ref.at[part], sems.at[i]))
    loads.append(pltpu.make_async_copy(q_hbm, q_ref, sems.at[steps + 1]))
    for load in loads:
        load.start()
    base = shard_ref[0] * slab
    loads[0].wait()
    positions = kept_ref[...]
    before = jnp.sum((positions < base).astype(jnp.int32))
    start = jnp.minimum(before // 16, (kept - window) // 16)
    local = (positions - base).astype(F32)
    for i in range(0, kept, 128):
        spots[i : i + 128, :] = jnp.broadcast_to(local[:, i : i + 128], (128, 128)).T
    spot = pl.ds(pl.multiple_of(start * 16, 16), window)
    mine = spots[spot, :]
    column = lax.broadcasted_iota(jnp.int32, (window, 128), 1).astype(F32)
    rows = jnp.zeros((window, dims), F32)
    for i in range(steps):
        onehot = jnp.concatenate(
            [jnp.where(mine == column + float(j), 1.0, 0.0).astype(BF16) for j in range(i * chunk, (i + 1) * chunk, 128)],
            axis=1,
        )
        loads[1 + i].wait()
        rows += lax.dot_general(onehot, k_ref[i * chunk : (i + 1) * chunk, :], NN, preferred_element_type=F32)
    picked[...] = jnp.zeros_like(picked)
    picked[spot, :] = rows.astype(BF16)
    loads[-1].wait()
    share, part = q_ref.shape[0] // 4, kept // 4
    is_root = shard_ref[0] == root_ref[0]
    tall = share + part
    for s in range(4):
        out, at = (keep_ref, send_ref)[s % 2], s // 2 * tall
        place = (shard_ref[0] % 4) ^ s
        q = q_ref[aligned(place, share), :]
        out[at : at + share, :] = jnp.where(is_root, q, jnp.zeros_like(q))
        out[at + share : at + tall, :] = picked[aligned(place, part), :]


def sum_kernel(*refs):
    total = refs[0][...]
    for ref in refs[1:-1]:
        total = total + ref[...]
    refs[-1][...] = total


def halve_kernel(a_ref, b_ref, near_ref, far_ref):
    rows = near_ref.shape[0]
    near_ref[...] = a_ref[:rows, :] + b_ref[:rows, :]
    far_ref[...] = a_ref[rows:, :] + b_ref[rows:, :]


def stack_kernel(a_ref, b_ref, out_ref):
    rows = a_ref.shape[0]
    out_ref[:rows, :] = a_ref[...]
    out_ref[rows:, :] = b_ref[...]


def spread(shard, queries, kept, keys, roots, values, attend_to):
    (rows, dims), (slab, _) = queries.shape, keys.shape
    count = kept.shape[1]
    devices = lax.axis_size("ctx")
    quarter = ((rows + count) // 4, dims)
    half = (2 * quarter[0], dims)
    in_hbm = lambda x: pltpu.with_memory_space_constraint(x, pltpu.HBM)
    keep, send, keys = call(
        functools.partial(prepare_kernel, 4 * count // devices + 16),
        (shard, roots, in_hbm(queries), in_hbm(kept), in_hbm(keys)),
        [(half, BF16)] * 2 + [(keys.shape, BF16)],
        scratch=[
            pltpu.VMEM((rows, dims), BF16),
            pltpu.VMEM((1, count), jnp.int32),
            pltpu.VMEM((count, 128), F32),
            pltpu.VMEM((count, dims), BF16),
            pltpu.SemaphoreType.DMA((6,)),
        ],
        name="prepare",
        specs=[SMEM, SMEM, HBM, HBM, HBM],
    )
    near, far = call(halve_kernel, (keep, swap(send, "ctx", 1)), [(quarter, BF16)] * 2, name="halve")
    total = lambda arrays: call(sum_kernel, arrays, [(quarter, BF16)], name="total")[0]
    came = swap(far, "ctx", 2)
    (turned,) = call(turn_kernel, (values,), [((dims + 16, slab), BF16)], 10**7, name="turn")
    came, turned = lax.optimization_barrier((came, turned))
    near = total([near, came])
    step = 4
    while step < devices:
        ways = math.gcd(devices // step, 4)
        near = total([near] + [swap(near, "ctx", t * step) for t in range(1, ways)])
        step *= ways
    far = swap(near, "ctx", 2)
    first = attend_to(near, keys, turned)
    far, first = lax.optimization_barrier((far, first))
    (both,) = call(stack_kernel, (near, far), [(half, BF16)], name="stack")
    other = swap(both, "ctx", 1)
    send = attend_to(far, keys, turned, before=[first])
    other, send = lax.optimization_barrier((other, send))
    came = swap(send, "ctx", 1)
    return near, far, other, attend_to(other, keys, turned), came


def turn_kernel(v_ref, vt_ref):
    dims = v_ref.shape[1]
    vt_ref[:dims, :] = v_ref[...].T
    vt_ref[dims:, :] = jnp.ones((vt_ref.shape[0] - dims, v_ref.shape[0]), BF16)


def quarters_of(ref, rows, tall):
    return [ref[i : i + rows, :] for i in range(0, ref.shape[0], tall)]


def attention_kernel(lanes, tall, block, score_scale, q_ref, k_ref, vt_ref, *refs):
    before, out_ref = refs[:-1], refs[-1]
    quarters = quarters_of(q_ref, lanes, tall)
    dims = k_ref.shape[1]
    blocks = k_ref.shape[0] // block
    factor = score_scale * math.log2(math.e)
    skip = len(before) * lanes
    for ref in before:
        out_ref[:, :skip] = ref[...]

    def scores(i, b):
        return lax.dot_general(
            k_ref[b * block : (b + 1) * block, :], quarters[i], NT, preferred_element_type=F32
        )

    stages = [(i, b) for i in range(len(quarters)) for b in range(blocks)]
    ahead = scores(*stages[0])
    for n, (i, b) in enumerate(stages):
        s = ahead
        if n + 1 < len(stages):
            ahead = scores(*stages[n + 1])
        at = slice(skip + i * lanes, skip + (i + 1) * lanes)
        top = jnp.max(s, axis=0, keepdims=True)
        e = jnp.exp2((s - top) * factor).astype(BF16)
        out = lax.dot_general(vt_ref[:, b * block : (b + 1) * block], e, NN, preferred_element_type=F32)
        top = top * factor
        total = out[dims : dims + 1, :]
        out = out[:dims, :]
        if b:
            old_top = out_ref[dims : dims + 1, at]
            joint = jnp.maximum(old_top, top)
            old_scale = jnp.exp2(old_top - joint)
            new_scale = jnp.exp2(top - joint)
            out = out_ref[:dims, at] * old_scale + out * new_scale
            total = out_ref[dims + 1 : dims + 2, at] * old_scale + total * new_scale
            top = joint
        out_ref[:dims, at] = out
        out_ref[dims:, at] = tail(top, total)


def attention(lanes, tall, score_scale, piece, keys, turned, before=()):
    slab, dims = keys.shape
    count = piece.shape[0] // tall
    return call(
        functools.partial(attention_kernel, lanes, tall, min(KBLK, slab), score_scale),
        (piece, keys, turned, *before),
        [((dims + SUB, lanes * (count + len(before))), F32)],
        4 * lanes * count * slab * dims,
        name="attention",
    )[0]


def merged(*refs):
    dims = refs[0].shape[0] - SUB
    tops = [ref[dims : dims + 1, :] for ref in refs]
    top = functools.reduce(jnp.maximum, tops)
    scales = [jnp.exp2(t - top) for t in tops]
    total = sum(ref[dims + 1 : dims + 2, :] * scale for ref, scale in zip(refs, scales))
    out = sum(ref[:dims, :] * scale for ref, scale in zip(refs, scales))
    return out, top, total


def tail(top, total):
    return jnp.concatenate([top, total, jnp.zeros((SUB - 2, top.shape[1]), F32)], axis=0)


def merge_lanes_kernel(a_ref, b_ref, keep_ref, send_ref):
    out, top, total = merged(a_ref, b_ref)
    dims, lanes = out.shape[0], keep_ref.shape[1]
    for ref, at in ((keep_ref, slice(0, lanes)), (send_ref, slice(lanes, 2 * lanes))):
        ref[:dims, :] = out[:, at]
        ref[dims:, :] = tail(top[:, at], total[:, at])


def merge_rows_kernel(step, shard_ref, *refs):
    work, refs = refs[-1], refs[:-1]
    ways = sum(1 for ref in refs if ref.shape[0] != refs[0].shape[0])
    ins, outs = refs[:-ways], refs[-ways:]
    out, top, total = merged(*ins)
    rows = outs[0].shape[0] - SUB
    work[...] = out
    digit = (shard_ref[0] // step) % ways
    for t, ref in enumerate(outs):
        ref[:rows, :] = work[aligned(digit ^ t, rows), :]
        ref[rows:, :] = tail(top, total)


def finish_kernel(*refs):
    out, _, total = merged(*refs[:-1])
    refs[-1][...] = out / total


def stack_rows_kernel(step, shard_ref, *refs):
    ins, out_ref = refs[:-1], refs[-1]
    rows = ins[0].shape[0]
    digit = (shard_ref[0] // step) % len(ins)
    for t, ref in enumerate(ins):
        out_ref[aligned(digit ^ t, rows), :] = ref[...]


def stack_lanes_kernel(a_ref, b_ref, out_ref):
    lanes = a_ref.shape[1]
    out_ref[:, :lanes] = a_ref[...]
    out_ref[:, lanes:] = b_ref[...]


def target_rounds(shard, keep, came):
    dims, lanes = keep.shape[0] - SUB, keep.shape[1] // 2
    devices = lax.axis_size("ctx")
    keep, send = call(merge_lanes_kernel, (keep, came), [((dims + SUB, lanes), F32)] * 2, name="merge")
    came = yield [swap(send, "ctx", 2)]
    digits = [(step, 2) for step in (2**i for i in range(2, devices.bit_length() - 1))]
    rows = dims
    for step, ways in digits:
        keep, *send = call(
            functools.partial(merge_rows_kernel, step),
            (shard, keep, *came),
            [((rows // ways + SUB, lanes), F32)] * ways,
            scratch=[pltpu.VMEM((rows, lanes), F32)],
            name="merge",
        )
        came = yield [swap(x, "ctx", t * step) for t, x in enumerate(send, 1)]
        rows //= ways
    (block,) = call(finish_kernel, (keep, *came), [((rows, lanes), F32)], name="finish")
    for step, ways in reversed(digits):
        came = yield [swap(block, "ctx", t * step) for t in range(1, ways)]
        rows *= ways
        (block,) = call(
            functools.partial(stack_rows_kernel, step), (shard, block, *came), [((rows, lanes), F32)], name="stack"
        )
    came = yield [swap(block, "ctx", 2)]
    (block,) = call(stack_lanes_kernel, (block, *came), [((dims, 2 * lanes), F32)], name="stack")
    came = yield [swap(block, "ctx", 1)]
    return block, *came


def attend_kernel(score_scale, shard_ref, near_ref, far_ref, other_ref, high_ref, low_ref, c_all):
    part, rows = c_all.shape[0] // 4, high_ref.shape[1] // 4
    tall = part + rows
    pieces = [(near_ref, 0), (other_ref, 0), (far_ref, 0), (other_ref, tall)]
    places = [(shard_ref[0] % 4) ^ s for s in range(4)]
    for place, (ref, at) in zip(places, pieces):
        c_all[aligned(place, part), :] = ref[at + rows : at + tall, :]
    for place, (ref, at) in zip(places, pieces):
        scores = lax.dot_general(c_all[...], ref[at : at + rows, :], NT, preferred_element_type=F32) * score_scale
        weights = jnp.exp(scores - jnp.max(scores, axis=0, keepdims=True))
        weights = weights * (1.0 / jnp.sum(weights, axis=0, keepdims=True))
        high_ref[:, aligned(place, rows)], low_ref[:, aligned(place, rows)] = halves(weights)


def gram_kernel(high_ref, low_ref, h_ref):
    high, low = high_ref[...], low_ref[...]
    cross = dot(high, low, NT)
    gram = dot(high, high, NT) + (dot(low, low, NT) + (cross + cross.T))
    kept = gram.shape[0]
    diagonal = lax.broadcasted_iota(jnp.int32, gram.shape, 0) == lax.broadcasted_iota(jnp.int32, gram.shape, 1)
    trace = jnp.sum(jnp.where(diagonal, gram, 0.0))
    h_ref[...] = gram + jnp.where(diagonal, RIDGE_SHARE * trace / kept, 0.0)


def invert_block(rows):
    count = len(rows)
    size = count * SUB
    lane = lax.broadcasted_iota(jnp.int32, (SUB, size), 1)
    sub = lax.broadcasted_iota(jnp.int32, (SUB, size), 0)
    spread_lane = lambda array, column: jnp.broadcast_to(array[:, column : column + 1], (SUB, size))
    line = lambda array, row: jnp.broadcast_to(array[row : row + 1, :], (SUB, size))
    for k in range(count):
        base = k * SUB
        inside = (lane >= base) & (lane < base + SUB)
        columns = [spread_lane(rows[k], base + j) for j in range(SUB)]
        work = jnp.where(inside, jnp.where(lane - base == sub, 1.0, 0.0), rows[k])
        for j in range(0, SUB, 2):
            first, second = columns[j], columns[j + 1]
            a, b, c, d = line(first, j), line(second, j), line(first, j + 1), line(second, j + 1)
            inverse = 1.0 / (a * d - b * c)
            at_first, at_second = sub == j, sub == j + 1

            def step(v):
                upper, lower = line(v, j), line(v, j + 1)
                new_upper = (d * upper - b * lower) * inverse
                new_lower = (a * lower - c * upper) * inverse
                other = v - (first * new_upper + second * new_lower)
                return jnp.where(at_first, new_upper, jnp.where(at_second, new_lower, other))

            for i in range(j + 2, SUB):
                columns[i] = step(columns[i])
            work = step(work)
        lines = [line(work, j) for j in range(SUB)]
        updated = list(rows)
        updated[k] = work
        for i in list(range(k + 1, count)) + list(range(k)):
            terms = [spread_lane(rows[i], base + j) * lines[j] for j in range(SUB)]
            while len(terms) > 1:
                terms = [x + y for x, y in zip(terms[::2], terms[1::2])]
            updated[i] = jnp.where(inside, 0.0, rows[i]) - terms[0]
        rows = updated
        yield
    return jnp.concatenate(rows, axis=0)


def inverse_beside(block, work=()):
    work = list(work)
    groups = invert_block([block[i : i + SUB, :] for i in range(0, block.shape[0], SUB)])
    while True:
        try:
            next(groups)
        except StopIteration as stop:
            for piece in work:
                piece()
            return stop.value
        if work:
            work.pop(0)()


def invert_kernel(h_ref, out_ref):
    out_ref[...] = inverse_beside(h_ref[:PANEL, :PANEL])


def sweep_kernel(panel, h_ref, inverse_ref, out_ref, *next_ref):
    size = h_ref.shape[0]
    at = slice(panel * PANEL, (panel + 1) * PANEL)
    wide = slice(panel * PANEL // 128 * 128, panel * PANEL // 128 * 128 + 128)
    offset = at.start - wide.start
    inverse = inverse_ref[...]
    turned = product(halves(inverse), halves(h_ref[at, :]), NN)
    padded = jnp.concatenate(
        [turned if i == offset else jnp.zeros_like(turned) for i in range(0, 128, PANEL)], axis=0
    )
    split = halves(padded)
    columns = padded.T
    lane = lax.broadcasted_iota(jnp.int32, (128, 128), 1)
    inside = (lane >= offset) & (lane < offset + PANEL)

    def rows_update(i):
        def piece():
            rows = slice(i, i + 128)
            old = h_ref[rows, :]
            out_ref[rows, :] = old - product(halves(h_ref[rows, wide]), split, NN)
            out_ref[rows, wide] = jnp.where(inside, columns[rows, :], out_ref[rows, wide])
            if i == wide.start:
                out_ref[at, :] = turned
                out_ref[at, at] = -inverse

        return piece

    work = [rows_update(i) for i in range(0, size, 128)]
    if next_ref:
        after = slice(at.stop, at.stop + PANEL)
        block = h_ref[after, after] - product(
            halves(h_ref[after, wide]), tuple(x[:, after] for x in split), NN
        )
        next_ref[0][...] = inverse_beside(block, work)
    else:
        for piece in work:
            piece()


def fit_kernel(shard_ref, minus_ref, high_ref, low_ref, own_ref, other_ref, x_ref, err_ref, yt):
    lanes = own_ref.shape[1] // 2
    place = shard_ref[0] % 4
    for s, ref in ((1, own_ref), (3, own_ref), (0, other_ref), (2, other_ref)):
        half = s // 2
        yt[:, aligned(place ^ s, lanes)] = ref[:, half * lanes : (half + 1) * lanes]
    target = yt[...]
    attend = high_ref[...], low_ref[...]
    cross = product(halves(target), attend, NT)
    fitted = -product(halves(cross), halves(minus_ref[...]), NN)
    x_ref[...] = fitted
    misfit = product(halves(fitted), attend, NN) - target
    error = jnp.sum(misfit * misfit) / jnp.sum(target * target)
    err_ref[...] = jnp.full(err_ref.shape, error, F32)


def flip_kernel(x_ref, out_ref):
    out_ref[...] = x_ref[...].T


def mean_kernel(heads, *refs):
    total = refs[0][:1, :1]
    for ref in refs[1:-1]:
        total = total + ref[:1, :1]
    refs[-1][...] = total / heads


def per_device(queries, keys, values, kept, roots):
    rows, dims = queries.shape[2:]
    slab, count = keys.shape[1], kept.shape[1]
    lanes = rows // 4
    score_scale = 1.0 / math.sqrt(dims)
    shard = lax.axis_index("ctx").astype(jnp.int32).reshape(1)

    attend_to = functools.partial(attention, lanes, (rows + count) // 4, score_scale)
    near, far, other, keep, came = spread(shard, queries[0, 0], kept, keys[0], roots, values[0], attend_to)
    rounds = target_rounds(shard, keep, came)
    came = next(rounds)
    ends = None

    def beside(arrays):
        nonlocal came, ends
        if ends is None:
            arrays, came = lax.optimization_barrier((arrays, came))
            try:
                came = rounds.send(came)
            except StopIteration as stop:
                ends = stop.value
        return arrays

    system_shape = ((count, count), F32)
    attend = call(
        functools.partial(attend_kernel, score_scale),
        (shard, near, far, other),
        [((count, rows), BF16)] * 2,
        10**9,
        scratch=[pltpu.VMEM((count, dims), BF16)],
        name="attend",
    )
    (system,) = call(gram_kernel, attend, [system_shape], 4 * 10**9, name="gram")
    panels = count // PANEL
    block_shape = ((PANEL, PANEL), F32)
    (inverse,) = call(invert_kernel, (system,), [block_shape], 10**9, name="invert")
    system, inverse = beside((system, inverse))
    for panel in range(panels):
        last = panel == panels - 1
        system, *inverse = call(
            functools.partial(sweep_kernel, panel),
            (system, inverse),
            [system_shape] if last else [system_shape, block_shape],
            2 * 10**9,
            name="sweep",
        )
        inverse = None if last else inverse[0]
        if panel not in (panels - 7, panels - 3):
            system, inverse = beside((system, inverse))
    while ends is None:
        system = beside(system)

    turned_fit, error = call(
        fit_kernel,
        (shard, system, *attend, *ends),
        [((dims, count), F32), ((SUB, 128), F32)],
        10**9,
        scratch=[pltpu.VMEM((dims, rows), F32)],
        name="fit",
    )
    heads = lax.axis_size("head")
    errors, step = [error], 1
    while step < heads:
        if len(errors) > 1:
            errors = list(call(sum_kernel, errors, [((SUB, 128), F32)], name="total"))
        errors.append(swap(errors[0], "head", step))
        step *= 2
    (compact,) = call(flip_kernel, (turned_fit,), [((count, dims), F32)], 10**6, name="flip")
    (error,) = call(functools.partial(mean_kernel, heads), errors, [((1, 1), F32)], name="mean")
    return (compact[None], error.reshape(()))


def solution(mesh):
    placed = (
        P("head", "ctx", None, None),
        P("head", "ctx", None),
        P("head", "ctx", None),
        P("head", None),
        P("head"),
    )
    return jax.shard_map(
        per_device,
        mesh=mesh,
        in_specs=placed,
        out_specs=(P("head", None, None), P()),
        check_vma=False,
    )
```

```python
import functools
import math

import jax
import jax.numpy as jnp
from jax import lax
from jax.experimental import pallas as pl
from jax.experimental.pallas import tpu as pltpu
from jax.sharding import PartitionSpec as P

KBLK = 1024
PANEL = 64
SUB = 8
RIDGE_SHARE = 0.01
F32 = jnp.float32
BF16 = jnp.bfloat16
VMEM_LIMIT = 48 * 1024 * 1024
VMEM = pl.BlockSpec(memory_space=pltpu.VMEM)
SMEM = pl.BlockSpec(memory_space=pltpu.SMEM)
HBM = pl.BlockSpec(memory_space=pltpu.HBM)
NT = (((1,), (1,)), ((), ()))
TN = (((0,), (0,)), ((), ()))
NN = (((1,), (0,)), ((), ()))


def swap(array, axis, step):
    size = lax.axis_size(axis)
    return lax.ppermute(array, axis, [(i, i ^ step) for i in range(size)])


def call(kernel, ins, outs, cost=10**5, scratch=(), name=None, specs=None):
    return pl.pallas_call(
        kernel,
        in_specs=specs or [SMEM if x.size == 1 else VMEM for x in ins],
        out_specs=[VMEM] * len(outs),
        out_shape=[jax.ShapeDtypeStruct(shape, kind) for shape, kind in outs],
        scratch_shapes=list(scratch),
        compiler_params=pltpu.CompilerParams(vmem_limit_bytes=VMEM_LIMIT),
        cost_estimate=pl.CostEstimate(flops=cost, bytes_accessed=10**5, transcendentals=0),
        name=name,
    )(*ins)


def aligned(value, unit):
    return pl.ds(pl.multiple_of(value * unit, unit), unit)


def halves(array):
    high = array.astype(BF16)
    return high, (array - high.astype(F32)).astype(BF16)


def dot(left, right, dims):
    return lax.dot_general(left, right, dims, preferred_element_type=F32)


def product(left, right, dims):
    (high, low), (right_high, right_low) = left, right
    rows = high.shape[0]
    both = dot(jnp.concatenate([high, low], axis=0), right_high, dims)
    return both[:rows] + (both[rows:] + dot(high, right_low, dims))


def pack(out, top, total):
    rows = out.shape[0] // 2
    mean = out * (1.0 / total)
    code = (jnp.max(jnp.abs(mean), axis=0, keepdims=True) * 2.0**27).astype(jnp.int32) + 1
    fixed = jnp.round(mean * (32767.0 / (code.astype(F32) * 2.0**-27))).astype(jnp.int32)
    words = (fixed[:rows] << 16) | (fixed[rows:] & 0xFFFF)
    level = jnp.floor(top + jnp.log2(total))
    rest = (total * jnp.exp2(top - level) * 2.0**28).astype(jnp.int32)
    blank = jnp.zeros((SUB - 3, top.shape[1]), jnp.int32)
    return jnp.concatenate([words, code, level.astype(jnp.int32), rest, blank], axis=0)


def means(packed):
    rows = packed.shape[0] - SUB
    words = packed[:rows]
    fixed = jnp.concatenate([words >> 16, (words << 16) >> 16], axis=0)
    return fixed.astype(F32) * (packed[rows : rows + 1].astype(F32) * (2.0**-27 / 32767.0))


def tail(top, total):
    return jnp.concatenate([top, total, jnp.zeros((SUB - 2, top.shape[1]), F32)], axis=0)


def partial_of(ref):
    rows = ref.shape[0] - SUB
    if ref.dtype == F32:
        return ref[:rows, :], ref[rows : rows + 1, :], ref[rows + 1 : rows + 2, :]
    packed = ref[...]
    rest = packed[rows + 2 : rows + 3].astype(F32) * 2.0**-28
    return means(packed) * rest, packed[rows + 1 : rows + 2].astype(F32), rest


def put_partial(ref, out, top, total):
    if ref.dtype == F32:
        ref[: out.shape[0], :] = out
        ref[out.shape[0] :, :] = tail(top, total)
    else:
        ref[...] = pack(out, top, total)


def partial_shape(rows, lanes, packed):
    if packed and rows % 16 == 0:
        return (rows // 2 + SUB, lanes), jnp.int32
    return (rows + SUB, lanes), F32


def prepare_kernel(window, shard_ref, root_ref, q_hbm, kept_hbm, k_hbm, *refs):
    keep_ref, send_ref, k_ref, q_ref, kept_ref, spots, picked, sems = refs
    slab, dims = k_ref.shape
    kept = kept_ref.shape[1]
    steps = sems.shape[0] - 2
    chunk = slab // steps
    loads = [pltpu.make_async_copy(kept_hbm, kept_ref, sems.at[steps])]
    for i in range(steps):
        part = pl.ds(i * chunk, chunk)
        loads.append(pltpu.make_async_copy(k_hbm.at[part], k_ref.at[part], sems.at[i]))
    loads.append(pltpu.make_async_copy(q_hbm, q_ref, sems.at[steps + 1]))
    for load in loads:
        load.start()
    base = shard_ref[0] * slab
    loads[0].wait()
    positions = kept_ref[...]
    before = jnp.sum((positions < base).astype(jnp.int32))
    start = jnp.minimum(before // 16, (kept - window) // 16)
    local = (positions - base).astype(F32)
    for i in range(0, kept, 128):
        spots[i : i + 128, :] = jnp.broadcast_to(local[:, i : i + 128], (128, 128)).T
    spot = pl.ds(pl.multiple_of(start * 16, 16), window)
    mine = spots[spot, :]
    column = lax.broadcasted_iota(jnp.int32, (window, 128), 1).astype(F32)
    rows = jnp.zeros((window, dims), F32)
    for i in range(steps):
        onehot = jnp.concatenate(
            [jnp.where(mine == column + float(j), 1.0, 0.0).astype(BF16) for j in range(i * chunk, (i + 1) * chunk, 128)],
            axis=1,
        )
        loads[1 + i].wait()
        rows += lax.dot_general(onehot, k_ref[i * chunk : (i + 1) * chunk, :], NN, preferred_element_type=F32)
    picked[...] = jnp.zeros_like(picked)
    picked[spot, :] = rows.astype(BF16)
    loads[-1].wait()
    share, part = q_ref.shape[0] // 4, kept // 4
    is_root = shard_ref[0] == root_ref[0]
    tall = share + part
    for s in range(4):
        out, at = (keep_ref, send_ref)[s % 2], s // 2 * tall
        place = (shard_ref[0] % 4) ^ s
        q = q_ref[aligned(place, share), :]
        out[at : at + share, :] = jnp.where(is_root, q, jnp.zeros_like(q))
        out[at + share : at + tall, :] = picked[aligned(place, part), :]


def sum_kernel(*refs):
    total = refs[0][...]
    for ref in refs[1:-1]:
        total = total + ref[...]
    refs[-1][...] = total


def halve_kernel(a_ref, b_ref, near_ref, far_ref):
    rows = near_ref.shape[0]
    near_ref[...] = a_ref[:rows, :] + b_ref[:rows, :]
    far_ref[...] = a_ref[rows:, :] + b_ref[rows:, :]


def stack_kernel(a_ref, b_ref, out_ref):
    rows = a_ref.shape[0]
    out_ref[:rows, :] = a_ref[...]
    out_ref[rows:, :] = b_ref[...]


def spread(shard, queries, kept, keys, roots, values, attend_to):
    (rows, dims), (slab, _) = queries.shape, keys.shape
    count = kept.shape[1]
    devices = lax.axis_size("ctx")
    quarter = ((rows + count) // 4, dims)
    half = (2 * quarter[0], dims)
    in_hbm = lambda x: pltpu.with_memory_space_constraint(x, pltpu.HBM)
    keep, send, keys = call(
        functools.partial(prepare_kernel, 4 * count // devices + 16),
        (shard, roots, in_hbm(queries), in_hbm(kept), in_hbm(keys)),
        [(half, BF16)] * 2 + [(keys.shape, BF16)],
        scratch=[
            pltpu.VMEM((rows, dims), BF16),
            pltpu.VMEM((1, count), jnp.int32),
            pltpu.VMEM((count, 128), F32),
            pltpu.VMEM((count, dims), BF16),
            pltpu.SemaphoreType.DMA((6,)),
        ],
        name="prepare",
        specs=[SMEM, SMEM, HBM, HBM, HBM],
    )
    near, far = call(halve_kernel, (keep, swap(send, "ctx", 1)), [(quarter, BF16)] * 2, name="halve")
    total = lambda arrays: call(sum_kernel, arrays, [(quarter, BF16)], name="total")[0]
    came = swap(far, "ctx", 2)
    (turned,) = call(turn_kernel, (values,), [((dims + 16, slab), BF16)], 10**7, name="turn")
    came, turned = lax.optimization_barrier((came, turned))
    near = total([near, came])
    step = 4
    while step < devices:
        ways = math.gcd(devices // step, 4)
        near = total([near] + [swap(near, "ctx", t * step) for t in range(1, ways)])
        step *= ways
    far = swap(near, "ctx", 2)
    first = attend_to(near, keys, turned)
    far, first = lax.optimization_barrier((far, first))
    (both,) = call(stack_kernel, (near, far), [(half, BF16)], name="stack")
    other, came = swap(both, "ctx", 1), [swap(first, "ctx", 1)]
    second = attend_to(far, keys, turned)
    other, second = lax.optimization_barrier((other, second))
    came.append(swap(second, "ctx", 3))
    third = attend_to(other, keys, turned, start=quarter[0])
    came.append(swap(third, "ctx", 2))
    other, third = lax.optimization_barrier((other, third))
    return near, far, other, attend_to(other, keys, turned, packed=False), came


def turn_kernel(v_ref, vt_ref):
    dims = v_ref.shape[1]
    vt_ref[:dims, :] = v_ref[...].T
    vt_ref[dims:, :] = jnp.ones((vt_ref.shape[0] - dims, v_ref.shape[0]), BF16)


def attention_kernel(start, block, score_scale, q_ref, k_ref, vt_ref, out_ref):
    dims = k_ref.shape[1]
    lanes = out_ref.shape[1]
    factor = score_scale * math.log2(math.e)
    queries = q_ref[start : start + lanes, :]
    scores = lambda b: dot(k_ref[b : b + block, :], queries, NT)
    slab = k_ref.shape[0]
    ahead = scores(0)
    for b in range(0, slab, block):
        s = ahead
        if b + block < slab:
            ahead = scores(b + block)
        top = jnp.max(s, axis=0, keepdims=True)
        e = jnp.exp2((s - top) * factor).astype(BF16)
        out = dot(vt_ref[:, b : b + block], e, NN)
        top = top * factor
        total = out[dims : dims + 1, :]
        out = out[:dims, :]
        if b:
            joint = jnp.maximum(old_top, top)
            old_scale = jnp.exp2(old_top - joint)
            new_scale = jnp.exp2(top - joint)
            out = old_out * old_scale + out * new_scale
            total = old_total * old_scale + total * new_scale
            top = joint
        old_out, old_top, old_total = out, top, total
    put_partial(out_ref, out, top, total)


def attention(lanes, score_scale, piece, keys, turned, start=0, packed=True):
    slab, dims = keys.shape
    return call(
        functools.partial(attention_kernel, start, min(KBLK, slab), score_scale),
        (piece, keys, turned),
        [partial_shape(dims, lanes, packed)],
        10**6,
        name="attention",
    )[0]


def merged(*refs):
    parts = [partial_of(ref) for ref in refs]
    top = functools.reduce(jnp.maximum, [part[1] for part in parts])
    scales = [jnp.exp2(part[1] - top) for part in parts]
    total = sum(part[2] * scale for part, scale in zip(parts, scales))
    out = sum(part[0] * scale for part, scale in zip(parts, scales))
    return out, top, total


def merge_kernel(step, shard_ref, *refs):
    ins, (keep_ref, send_ref, work) = refs[:-3], refs[-3:]
    out, top, total = merged(*ins)
    rows = out.shape[0] // 2
    work[...] = out
    bit = (shard_ref[0] // step) % 2
    put_partial(keep_ref, work[aligned(bit, rows), :], top, total)
    put_partial(send_ref, work[aligned(1 - bit, rows), :], top, total)


def finish_kernel(*refs):
    out, _, total = merged(*refs[:-1])
    refs[-1][...] = out / total


def stack_rows_kernel(step, shard_ref, a_ref, b_ref, out_ref):
    rows = a_ref.shape[0]
    bit = (shard_ref[0] // step) % 2
    out_ref[aligned(bit, rows), :] = a_ref[...]
    out_ref[aligned(1 - bit, rows), :] = b_ref[...]


def pack_kernel(y_ref, out_ref):
    one = jnp.ones((1, y_ref.shape[1]), F32)
    out_ref[...] = pack(y_ref[...], one * 0.0, one)


def target_rounds(shard, keep, came):
    dims, lanes = keep.shape[0] - SUB, keep.shape[1]
    devices = lax.axis_size("ctx")
    came = yield came
    steps = [2**i for i in range(2, devices.bit_length() - 1)]
    rows = dims
    for step in steps:
        keep, send = call(
            functools.partial(merge_kernel, step),
            (shard, keep, *came),
            [partial_shape(rows // 2, lanes, packed) for packed in (False, True)],
            scratch=[pltpu.VMEM((rows, lanes), F32)],
            name="merge",
        )
        came = yield [swap(send, "ctx", step)]
        rows //= 2
    (block,) = call(finish_kernel, (keep, *came), [((rows, lanes), F32)], name="finish")
    for step in reversed(steps):
        came = yield [swap(block, "ctx", step)]
        rows *= 2
        (block,) = call(
            functools.partial(stack_rows_kernel, step), (shard, block, *came), [((rows, lanes), F32)], name="stack"
        )
    shape, kind = partial_shape(dims, lanes, True)
    (block,) = call(pack_kernel, (block,), [(shape, kind)], name="pack")
    came = yield [swap(block, "ctx", 2)]
    (block,) = call(stack_kernel, (block, *came), [((2 * shape[0], lanes), kind)], name="stack")
    came = yield [swap(block, "ctx", 1)]
    return block, *came


def attend_kernel(score_scale, shard_ref, near_ref, far_ref, other_ref, high_ref, low_ref, c_all):
    part, rows = c_all.shape[0] // 4, high_ref.shape[1] // 4
    tall = part + rows
    pieces = [(near_ref, 0), (other_ref, 0), (far_ref, 0), (other_ref, tall)]
    places = [(shard_ref[0] % 4) ^ s for s in range(4)]
    for place, (ref, at) in zip(places, pieces):
        c_all[aligned(place, part), :] = ref[at + rows : at + tall, :]
    for place, (ref, at) in zip(places, pieces):
        scores = lax.dot_general(c_all[...], ref[at : at + rows, :], NT, preferred_element_type=F32) * score_scale
        weights = jnp.exp(scores - jnp.max(scores, axis=0, keepdims=True))
        weights = weights * (1.0 / jnp.sum(weights, axis=0, keepdims=True))
        high_ref[:, aligned(place, rows)], low_ref[:, aligned(place, rows)] = halves(weights)


def gram_kernel(high_ref, low_ref, h_ref):
    high, low = high_ref[...], low_ref[...]
    cross = dot(high, low, NT)
    gram = dot(high, high, NT) + (dot(low, low, NT) + (cross + cross.T))
    kept = gram.shape[0]
    diagonal = lax.broadcasted_iota(jnp.int32, gram.shape, 0) == lax.broadcasted_iota(jnp.int32, gram.shape, 1)
    trace = jnp.sum(jnp.where(diagonal, gram, 0.0))
    h_ref[...] = gram + jnp.where(diagonal, RIDGE_SHARE * trace / kept, 0.0)


def invert_block(rows):
    count = len(rows)
    size = count * SUB
    lane = lax.broadcasted_iota(jnp.int32, (SUB, size), 1)
    sub = lax.broadcasted_iota(jnp.int32, (SUB, size), 0)
    spread_lane = lambda array, column: jnp.broadcast_to(array[:, column : column + 1], (SUB, size))
    line = lambda array, row: jnp.broadcast_to(array[row : row + 1, :], (SUB, size))
    for k in range(count):
        base = k * SUB
        inside = (lane >= base) & (lane < base + SUB)
        columns = [spread_lane(rows[k], base + j) for j in range(SUB)]
        work = jnp.where(inside, jnp.where(lane - base == sub, 1.0, 0.0), rows[k])
        for j in range(0, SUB, 2):
            first, second = columns[j], columns[j + 1]
            a, b, c, d = line(first, j), line(second, j), line(first, j + 1), line(second, j + 1)
            inverse = 1.0 / (a * d - b * c)
            at_first, at_second = sub == j, sub == j + 1

            def step(v):
                upper, lower = line(v, j), line(v, j + 1)
                new_upper = (d * upper - b * lower) * inverse
                new_lower = (a * lower - c * upper) * inverse
                other = v - (first * new_upper + second * new_lower)
                return jnp.where(at_first, new_upper, jnp.where(at_second, new_lower, other))

            for i in range(j + 2, SUB):
                columns[i] = step(columns[i])
            work = step(work)
        lines = [line(work, j) for j in range(SUB)]
        updated = list(rows)
        updated[k] = work
        for i in list(range(k + 1, count)) + list(range(k)):
            terms = [spread_lane(rows[i], base + j) * lines[j] for j in range(SUB)]
            while len(terms) > 1:
                terms = [x + y for x, y in zip(terms[::2], terms[1::2])]
            updated[i] = jnp.where(inside, 0.0, rows[i]) - terms[0]
        rows = updated
        yield
    return jnp.concatenate(rows, axis=0)


def inverse_beside(block, work=()):
    work = list(work)
    groups = invert_block([block[i : i + SUB, :] for i in range(0, block.shape[0], SUB)])
    while True:
        try:
            next(groups)
        except StopIteration as stop:
            for piece in work:
                piece()
            return stop.value
        if work:
            work.pop(0)()


def invert_kernel(h_ref, out_ref):
    out_ref[...] = inverse_beside(h_ref[:PANEL, :PANEL])


def sweep_kernel(panel, h_ref, inverse_ref, out_ref, *next_ref):
    size = h_ref.shape[0]
    at = slice(panel * PANEL, (panel + 1) * PANEL)
    wide = slice(panel * PANEL // 128 * 128, panel * PANEL // 128 * 128 + 128)
    offset = at.start - wide.start
    inverse = inverse_ref[...]
    turned = product(halves(inverse), halves(h_ref[at, :]), NN)
    padded = jnp.concatenate(
        [turned if i == offset else jnp.zeros_like(turned) for i in range(0, 128, PANEL)], axis=0
    )
    split = halves(padded)
    columns = padded.T
    lane = lax.broadcasted_iota(jnp.int32, (128, 128), 1)
    inside = (lane >= offset) & (lane < offset + PANEL)

    def rows_update(i):
        def piece():
            rows = slice(i, i + 128)
            old = h_ref[rows, :]
            out_ref[rows, :] = old - product(halves(h_ref[rows, wide]), split, NN)
            out_ref[rows, wide] = jnp.where(inside, columns[rows, :], out_ref[rows, wide])
            if i == wide.start:
                out_ref[at, :] = turned
                out_ref[at, at] = -inverse

        return piece

    work = [rows_update(i) for i in range(0, size, 128)]
    if next_ref:
        after = slice(at.stop, at.stop + PANEL)
        block = h_ref[after, after] - product(
            halves(h_ref[after, wide]), tuple(x[:, after] for x in split), NN
        )
        next_ref[0][...] = inverse_beside(block, work)
    else:
        for piece in work:
            piece()


def fit_kernel(shard_ref, minus_ref, high_ref, low_ref, own_ref, other_ref, x_ref, err_ref, yt):
    rows, lanes = own_ref.shape[0] // 2, own_ref.shape[1]
    place = shard_ref[0] % 4
    for s, ref in ((1, own_ref), (3, own_ref), (0, other_ref), (2, other_ref)):
        half = s // 2
        yt[:, aligned(place ^ s, lanes)] = means(ref[half * rows : (half + 1) * rows, :])
    target = yt[...]
    attend = high_ref[...], low_ref[...]
    cross = product(halves(target), attend, NT)
    fitted = -product(halves(cross), halves(minus_ref[...]), NN)
    x_ref[...] = fitted
    misfit = product(halves(fitted), attend, NN) - target
    error = jnp.sum(misfit * misfit) / jnp.sum(target * target)
    err_ref[...] = jnp.full(err_ref.shape, error, F32)


def flip_kernel(x_ref, out_ref):
    out_ref[...] = x_ref[...].T


def mean_kernel(heads, *refs):
    total = refs[0][:1, :1]
    for ref in refs[1:-1]:
        total = total + ref[:1, :1]
    refs[-1][...] = total / heads


def per_device(queries, keys, values, kept, roots):
    rows, dims = queries.shape[2:]
    slab, count = keys.shape[1], kept.shape[1]
    lanes = rows // 4
    score_scale = 1.0 / math.sqrt(dims)
    shard = lax.axis_index("ctx").astype(jnp.int32).reshape(1)

    attend_to = functools.partial(attention, lanes, score_scale)
    near, far, other, keep, came = spread(shard, queries[0, 0], kept, keys[0], roots, values[0], attend_to)
    rounds = target_rounds(shard, keep, came)
    came = next(rounds)
    ends = None

    def beside(arrays):
        nonlocal came, ends
        if ends is None:
            arrays, came = lax.optimization_barrier((arrays, came))
            try:
                came = rounds.send(came)
            except StopIteration as stop:
                ends = stop.value
        return arrays

    system_shape = ((count, count), F32)
    attend = call(
        functools.partial(attend_kernel, score_scale),
        (shard, near, far, other),
        [((count, rows), BF16)] * 2,
        10**6,
        scratch=[pltpu.VMEM((count, dims), BF16)],
        name="attend",
    )
    attend = beside(attend)
    (system,) = call(gram_kernel, attend, [system_shape], 4 * 10**9, name="gram")
    system = beside(system)
    panels = count // PANEL
    block_shape = ((PANEL, PANEL), F32)
    (inverse,) = call(invert_kernel, (system,), [block_shape], 10**9, name="invert")
    for panel in range(panels):
        last = panel == panels - 1
        system, *inverse = call(
            functools.partial(sweep_kernel, panel),
            (system, inverse),
            [system_shape] if last else [system_shape, block_shape],
            2 * 10**9,
            name="sweep",
        )
        inverse = None if last else inverse[0]
        if panel in (0, 2, 3, 5, 6):
            system, inverse = beside((system, inverse))
    while ends is None:
        system = beside(system)

    turned_fit, error = call(
        fit_kernel,
        (shard, system, *attend, *ends),
        [((dims, count), F32), ((SUB, 128), F32)],
        10**9,
        scratch=[pltpu.VMEM((dims, rows), F32)],
        name="fit",
    )
    heads = lax.axis_size("head")
    errors, step = [error], 1
    while step < heads:
        if len(errors) > 1:
            errors = list(call(sum_kernel, errors, [((SUB, 128), F32)], name="total"))
        errors.append(swap(errors[0], "head", step))
        step *= 2
    (compact,) = call(flip_kernel, (turned_fit,), [((count, dims), F32)], 10**6, name="flip")
    (error,) = call(functools.partial(mean_kernel, heads), errors, [((1, 1), F32)], name="mean")
    return (compact[None], error.reshape(()))


def solution(mesh):
    placed = (
        P("head", "ctx", None, None),
        P("head", "ctx", None),
        P("head", "ctx", None),
        P("head", None),
        P("head"),
    )
    return jax.shard_map(
        per_device,
        mesh=mesh,
        in_specs=placed,
        out_specs=(P("head", None, None), P()),
        check_vma=False,
    )
```

```python
import functools
import math

import jax
import jax.numpy as jnp
from jax import lax
from jax.experimental import pallas as pl
from jax.experimental.pallas import tpu as pltpu
from jax.sharding import PartitionSpec as P

KBLK = 1024
PANEL = 64
SUB = 8
RIDGE_SHARE = 0.01
F32 = jnp.float32
BF16 = jnp.bfloat16
VMEM_LIMIT = 48 * 1024 * 1024
VMEM = pl.BlockSpec(memory_space=pltpu.VMEM)
SMEM = pl.BlockSpec(memory_space=pltpu.SMEM)
HBM = pl.BlockSpec(memory_space=pltpu.HBM)
NT = (((1,), (1,)), ((), ()))
TN = (((0,), (0,)), ((), ()))
NN = (((1,), (0,)), ((), ()))


def swap(array, axis, step):
    size = lax.axis_size(axis)
    return lax.ppermute(array, axis, [(i, i ^ step) for i in range(size)])


def call(kernel, ins, outs, cost=10**5, scratch=(), name=None, specs=None):
    return pl.pallas_call(
        kernel,
        in_specs=specs or [SMEM if x.size == 1 else VMEM for x in ins],
        out_specs=[VMEM] * len(outs),
        out_shape=[jax.ShapeDtypeStruct(shape, kind) for shape, kind in outs],
        scratch_shapes=list(scratch),
        compiler_params=pltpu.CompilerParams(vmem_limit_bytes=VMEM_LIMIT),
        cost_estimate=pl.CostEstimate(flops=cost, bytes_accessed=10**5, transcendentals=0),
        name=name,
    )(*ins)


def aligned(value, unit):
    return pl.ds(pl.multiple_of(value * unit, unit), unit)


def halves(array):
    high = array.astype(BF16)
    return high, (array - high.astype(F32)).astype(BF16)


def dot(left, right, dims):
    return lax.dot_general(left, right, dims, preferred_element_type=F32)


def product(left, right, dims):
    (high, low), (right_high, right_low) = left, right
    rows = high.shape[0]
    both = dot(jnp.concatenate([high, low], axis=0), right_high, dims)
    return both[:rows] + (both[rows:] + dot(high, right_low, dims))


def pack(out, top, total):
    rows = out.shape[0] // 2
    mean = out * (1.0 / total)
    code = (jnp.max(jnp.abs(mean), axis=0, keepdims=True) * 2.0**27).astype(jnp.int32) + 1
    fixed = jnp.round(mean * (32767.0 / (code.astype(F32) * 2.0**-27))).astype(jnp.int32)
    words = (fixed[:rows] << 16) | (fixed[rows:] & 0xFFFF)
    level = jnp.floor(top + jnp.log2(total))
    rest = (total * jnp.exp2(top - level) * 2.0**28).astype(jnp.int32)
    blank = jnp.zeros((SUB - 3, top.shape[1]), jnp.int32)
    return jnp.concatenate([words, code, level.astype(jnp.int32), rest, blank], axis=0)


def means(packed):
    rows = packed.shape[0] - SUB
    words = packed[:rows]
    fixed = jnp.concatenate([words >> 16, (words << 16) >> 16], axis=0)
    return fixed.astype(F32) * (packed[rows : rows + 1].astype(F32) * (2.0**-27 / 32767.0))


def tail(top, total):
    return jnp.concatenate([top, total, jnp.zeros((SUB - 2, top.shape[1]), F32)], axis=0)


def partial_of(ref):
    rows = ref.shape[0] - SUB
    if ref.dtype == F32:
        return ref[:rows, :], ref[rows : rows + 1, :], ref[rows + 1 : rows + 2, :]
    packed = ref[...]
    rest = packed[rows + 2 : rows + 3].astype(F32) * 2.0**-28
    return means(packed) * rest, packed[rows + 1 : rows + 2].astype(F32), rest


def put_partial(ref, out, top, total):
    if ref.dtype == F32:
        ref[: out.shape[0], :] = out
        ref[out.shape[0] :, :] = tail(top, total)
    else:
        ref[...] = pack(out, top, total)


def partial_shape(rows, lanes, packed):
    if packed and rows % 16 == 0:
        return (rows // 2 + SUB, lanes), jnp.int32
    return (rows + SUB, lanes), F32


def quarters_out(keep_ref, send_ref, shard, rows, get):
    for s in range(4):
        at = s // 2 * rows
        (keep_ref, send_ref)[s % 2][at : at + rows, :] = get(aligned((shard % 4) ^ s, rows))


def root_kernel(shard_ref, root_ref, q_hbm, keep_ref, send_ref, q_ref, sem):
    load = pltpu.make_async_copy(q_hbm, q_ref, sem)
    load.start()
    load.wait()
    is_root = shard_ref[0] == root_ref[0]

    def get(at):
        q = q_ref[at, :]
        return jnp.where(is_root, q, jnp.zeros_like(q))

    quarters_out(keep_ref, send_ref, shard_ref[0], q_ref.shape[0] // 4, get)


def pick_kernel(window, shard_ref, kept_hbm, k_hbm, keep_ref, send_ref, k_ref, kept_ref, spots, picked, sems):
    slab, dims = k_ref.shape
    kept = kept_ref.shape[1]
    steps = sems.shape[0] - 1
    chunk = slab // steps
    loads = [pltpu.make_async_copy(kept_hbm, kept_ref, sems.at[steps])]
    for i in range(steps):
        part = pl.ds(i * chunk, chunk)
        loads.append(pltpu.make_async_copy(k_hbm.at[part], k_ref.at[part], sems.at[i]))
    for load in loads:
        load.start()
    base = shard_ref[0] * slab
    loads[0].wait()
    positions = kept_ref[...]
    before = jnp.sum((positions < base).astype(jnp.int32))
    start = jnp.minimum(before // 16, (kept - window) // 16)
    local = (positions - base).astype(F32)
    for i in range(0, kept, 128):
        spots[i : i + 128, :] = jnp.broadcast_to(local[:, i : i + 128], (128, 128)).T
    spot = pl.ds(pl.multiple_of(start * 16, 16), window)
    mine = spots[spot, :]
    column = lax.broadcasted_iota(jnp.int32, (window, 128), 1).astype(F32)
    rows = jnp.zeros((window, dims), F32)
    for i in range(steps):
        onehot = jnp.concatenate(
            [jnp.where(mine == column + float(j), 1.0, 0.0).astype(BF16) for j in range(i * chunk, (i + 1) * chunk, 128)],
            axis=1,
        )
        loads[1 + i].wait()
        rows += dot(onehot, k_ref[i * chunk : (i + 1) * chunk, :], NN)
    picked[...] = jnp.zeros_like(picked)
    picked[spot, :] = rows.astype(BF16)
    quarters_out(keep_ref, send_ref, shard_ref[0], kept // 4, lambda at: picked[at, :])


def sum_kernel(*refs):
    total = refs[0][...]
    for ref in refs[1:-1]:
        total = total + ref[...]
    refs[-1][...] = total


def halve_kernel(a_ref, b_ref, near_ref, far_ref):
    rows = near_ref.shape[0]
    near_ref[...] = a_ref[:rows, :] + b_ref[:rows, :]
    far_ref[...] = a_ref[rows:, :] + b_ref[rows:, :]


def stack_kernel(a_ref, b_ref, out_ref):
    rows = a_ref.shape[0]
    out_ref[:rows, :] = a_ref[...]
    out_ref[rows:, :] = b_ref[...]


def total(arrays):
    return call(sum_kernel, arrays, [(arrays[0].shape, arrays[0].dtype)], name="total")[0]


def after(first, then):
    return lax.optimization_barrier((first, then))


def halved(keep, send):
    rows, dims = keep.shape
    return call(halve_kernel, (keep, swap(send, "ctx", 1)), [((rows // 2, dims), BF16)] * 2, name="halve")


def across_groups(near, beside):
    step, devices = 4, lax.axis_size("ctx")
    while step < devices:
        ways = math.gcd(devices // step, 4)
        came = [swap(near, "ctx", t * step) for t in range(1, ways)]
        if step == 4:
            beside, came = after(beside, came)
        near = total([near] + came)
        step *= ways
    return near, beside


def both_of(near, far):
    return call(stack_kernel, (near, far), [((2 * near.shape[0], near.shape[1]), BF16)], name="stack")[0]


def spread(shard, queries, kept, keys, roots, values, attend_to):
    (rows, dims), (slab, _) = queries.shape, keys.shape
    count = kept.shape[1]
    in_hbm = lambda x: pltpu.with_memory_space_constraint(x, pltpu.HBM)
    keep, send = call(
        root_kernel,
        (shard, roots, in_hbm(queries)),
        [((rows // 2, dims), BF16)] * 2,
        scratch=[pltpu.VMEM((rows, dims), BF16), pltpu.SemaphoreType.DMA],
        name="root",
        specs=[SMEM, SMEM, HBM],
    )
    near, far = halved(keep, send)
    came = swap(far, "ctx", 2)
    keep, send, keys = call(
        functools.partial(pick_kernel, 4 * count // lax.axis_size("ctx") + 16),
        (shard, in_hbm(kept), in_hbm(keys)),
        [((count // 2, dims), BF16)] * 2 + [(keys.shape, BF16)],
        scratch=[
            pltpu.VMEM((1, count), jnp.int32),
            pltpu.VMEM((count, 128), F32),
            pltpu.VMEM((count, dims), BF16),
            pltpu.SemaphoreType.DMA((5,)),
        ],
        name="pick",
        specs=[SMEM, HBM, HBM],
    )
    (turned,) = call(turn_kernel, (values,), [((dims + 16, slab), BF16)], 10**7, name="turn")
    kept_near, kept_far = halved(keep, send)
    kept_near = total([kept_near, swap(kept_far, "ctx", 2)])
    (kept_near, turned), came = after((kept_near, turned), came)
    near = total([near, came])
    steps = [2**i for i in range(2, lax.axis_size("ctx").bit_length() - 1)]
    for step in steps[:1]:
        kept_near = total([kept_near, swap(kept_near, "ctx", step)])
    near, kept_near = across_groups(near, kept_near)
    for step in steps[1:]:
        kept_near = total([kept_near, swap(kept_near, "ctx", step)])

    far = swap(near, "ctx", 2)
    first = attend_to(near, keys, turned)
    (first, kept_near), far = after((first, kept_near), far)
    other, came = swap(both_of(near, far), "ctx", 1), [swap(first, "ctx", 1)]
    kept_far = swap(kept_near, "ctx", 2)
    second = attend_to(far, keys, turned)
    other, second, kept_far = lax.optimization_barrier((other, second, kept_far))
    came.append(swap(second, "ctx", 3))
    kept_other = swap(both_of(kept_near, kept_far), "ctx", 1)
    third = attend_to(other, keys, turned, start=rows // 4)
    came.append(swap(third, "ctx", 2))
    other, third = after(other, third)
    keep = attend_to(other, keys, turned, packed=False)
    return (near, far, other), (kept_near, kept_far, kept_other), keep, came


def turn_kernel(v_ref, vt_ref):
    dims = v_ref.shape[1]
    vt_ref[:dims, :] = v_ref[...].T
    vt_ref[dims:, :] = jnp.ones((vt_ref.shape[0] - dims, v_ref.shape[0]), BF16)


def attention_kernel(start, block, score_scale, q_ref, k_ref, vt_ref, out_ref):
    dims = k_ref.shape[1]
    lanes = out_ref.shape[1]
    factor = score_scale * math.log2(math.e)
    queries = q_ref[start : start + lanes, :]
    scores = lambda b: dot(k_ref[b : b + block, :], queries, NT)
    slab = k_ref.shape[0]
    ahead = scores(0)
    for b in range(0, slab, block):
        s = ahead
        if b + block < slab:
            ahead = scores(b + block)
        top = jnp.max(s, axis=0, keepdims=True)
        e = jnp.exp2((s - top) * factor).astype(BF16)
        out = dot(vt_ref[:, b : b + block], e, NN)
        top = top * factor
        total = out[dims : dims + 1, :]
        out = out[:dims, :]
        if b:
            joint = jnp.maximum(old_top, top)
            old_scale = jnp.exp2(old_top - joint)
            new_scale = jnp.exp2(top - joint)
            out = old_out * old_scale + out * new_scale
            total = old_total * old_scale + total * new_scale
            top = joint
        old_out, old_top, old_total = out, top, total
    put_partial(out_ref, out, top, total)


def attention(lanes, score_scale, piece, keys, turned, start=0, packed=True):
    slab, dims = keys.shape
    return call(
        functools.partial(attention_kernel, start, min(KBLK, slab), score_scale),
        (piece, keys, turned),
        [partial_shape(dims, lanes, packed)],
        10**6,
        name="attention",
    )[0]


def merged(*refs):
    parts = [partial_of(ref) for ref in refs]
    top = functools.reduce(jnp.maximum, [part[1] for part in parts])
    scales = [jnp.exp2(part[1] - top) for part in parts]
    total = sum(part[2] * scale for part, scale in zip(parts, scales))
    out = sum(part[0] * scale for part, scale in zip(parts, scales))
    return out, top, total


def merge_kernel(step, shard_ref, *refs):
    ins, (keep_ref, send_ref, work) = refs[:-3], refs[-3:]
    out, top, total = merged(*ins)
    rows = out.shape[0] // 2
    work[...] = out
    bit = (shard_ref[0] // step) % 2
    put_partial(keep_ref, work[aligned(bit, rows), :], top, total)
    put_partial(send_ref, work[aligned(1 - bit, rows), :], top, total)


def finish_kernel(*refs):
    out, _, total = merged(*refs[:-1])
    refs[-1][...] = out / total


def stack_rows_kernel(step, shard_ref, a_ref, b_ref, out_ref):
    rows = a_ref.shape[0]
    bit = (shard_ref[0] // step) % 2
    out_ref[aligned(bit, rows), :] = a_ref[...]
    out_ref[aligned(1 - bit, rows), :] = b_ref[...]


def pack_kernel(y_ref, out_ref):
    one = jnp.ones((1, y_ref.shape[1]), F32)
    out_ref[...] = pack(y_ref[...], one * 0.0, one)


def target_rounds(shard, keep, came):
    dims, lanes = keep.shape[0] - SUB, keep.shape[1]
    devices = lax.axis_size("ctx")
    came = yield came
    steps = [2**i for i in range(2, devices.bit_length() - 1)]
    rows = dims
    for step in steps:
        keep, send = call(
            functools.partial(merge_kernel, step),
            (shard, keep, *came),
            [partial_shape(rows // 2, lanes, packed) for packed in (False, True)],
            scratch=[pltpu.VMEM((rows, lanes), F32)],
            name="merge",
        )
        came = yield [swap(send, "ctx", step)]
        rows //= 2
    (block,) = call(finish_kernel, (keep, *came), [((rows, lanes), F32)], name="finish")
    for step in reversed(steps):
        came = yield [swap(block, "ctx", step)]
        rows *= 2
        (block,) = call(
            functools.partial(stack_rows_kernel, step), (shard, block, *came), [((rows, lanes), F32)], name="stack"
        )
    shape, kind = partial_shape(dims, lanes, True)
    (block,) = call(pack_kernel, (block,), [(shape, kind)], name="pack")
    came = yield [swap(block, "ctx", 2)]
    (block,) = call(stack_kernel, (block, *came), [((2 * shape[0], lanes), kind)], name="stack")
    came = yield [swap(block, "ctx", 1)]
    return block, *came


def attend_kernel(score_scale, shard_ref, *refs):
    queries, kept, (high_ref, low_ref, c_all) = refs[:3], refs[3:6], refs[6:]

    def quarters(near_ref, far_ref, other_ref):
        rows = near_ref.shape[0]
        return rows, [near_ref[...], other_ref[:rows, :], far_ref[...], other_ref[rows:, :]]

    rows, pieces = quarters(*kept)
    for s, piece in enumerate(pieces):
        c_all[aligned((shard_ref[0] % 4) ^ s, rows), :] = piece
    rows, pieces = quarters(*queries)
    for s, piece in enumerate(pieces):
        scores = dot(c_all[...], piece, NT) * score_scale
        weights = jnp.exp(scores - jnp.max(scores, axis=0, keepdims=True))
        weights = weights * (1.0 / jnp.sum(weights, axis=0, keepdims=True))
        at = aligned((shard_ref[0] % 4) ^ s, rows)
        high_ref[:, at], low_ref[:, at] = halves(weights)


def gram_kernel(high_ref, low_ref, h_ref):
    high, low = high_ref[...], low_ref[...]
    cross = dot(high, low, NT)
    gram = dot(high, high, NT) + (dot(low, low, NT) + (cross + cross.T))
    kept = gram.shape[0]
    diagonal = lax.broadcasted_iota(jnp.int32, gram.shape, 0) == lax.broadcasted_iota(jnp.int32, gram.shape, 1)
    trace = jnp.sum(jnp.where(diagonal, gram, 0.0))
    h_ref[...] = gram + jnp.where(diagonal, RIDGE_SHARE * trace / kept, 0.0)


def invert_block(rows):
    count = len(rows)
    size = count * SUB
    lane = lax.broadcasted_iota(jnp.int32, (SUB, size), 1)
    sub = lax.broadcasted_iota(jnp.int32, (SUB, size), 0)
    spread_lane = lambda array, column: jnp.broadcast_to(array[:, column : column + 1], (SUB, size))
    line = lambda array, row: jnp.broadcast_to(array[row : row + 1, :], (SUB, size))
    for k in range(count):
        base = k * SUB
        inside = (lane >= base) & (lane < base + SUB)
        columns = [spread_lane(rows[k], base + j) for j in range(SUB)]
        work = jnp.where(inside, jnp.where(lane - base == sub, 1.0, 0.0), rows[k])
        for j in range(0, SUB, 2):
            first, second = columns[j], columns[j + 1]
            a, b, c, d = line(first, j), line(second, j), line(first, j + 1), line(second, j + 1)
            inverse = 1.0 / (a * d - b * c)
            at_first, at_second = sub == j, sub == j + 1

            def step(v):
                upper, lower = line(v, j), line(v, j + 1)
                new_upper = (d * upper - b * lower) * inverse
                new_lower = (a * lower - c * upper) * inverse
                other = v - (first * new_upper + second * new_lower)
                return jnp.where(at_first, new_upper, jnp.where(at_second, new_lower, other))

            for i in range(j + 2, SUB):
                columns[i] = step(columns[i])
            work = step(work)
        lines = [line(work, j) for j in range(SUB)]
        updated = list(rows)
        updated[k] = work
        for i in list(range(k + 1, count)) + list(range(k)):
            terms = [spread_lane(rows[i], base + j) * lines[j] for j in range(SUB)]
            while len(terms) > 1:
                terms = [x + y for x, y in zip(terms[::2], terms[1::2])]
            updated[i] = jnp.where(inside, 0.0, rows[i]) - terms[0]
        rows = updated
        yield
    return jnp.concatenate(rows, axis=0)


def inverse_beside(block, work=()):
    work = list(work)
    groups = invert_block([block[i : i + SUB, :] for i in range(0, block.shape[0], SUB)])
    while True:
        try:
            next(groups)
        except StopIteration as stop:
            for piece in work:
                piece()
            return stop.value
        if work:
            work.pop(0)()


def invert_kernel(h_ref, out_ref):
    out_ref[...] = inverse_beside(h_ref[:PANEL, :PANEL])


def sweep_kernel(panel, h_ref, inverse_ref, out_ref, *next_ref):
    size = h_ref.shape[0]
    at = slice(panel * PANEL, (panel + 1) * PANEL)
    wide = slice(panel * PANEL // 128 * 128, panel * PANEL // 128 * 128 + 128)
    offset = at.start - wide.start
    inverse = inverse_ref[...]
    turned = product(halves(inverse), halves(h_ref[at, :]), NN)
    padded = jnp.concatenate(
        [turned if i == offset else jnp.zeros_like(turned) for i in range(0, 128, PANEL)], axis=0
    )
    split = halves(padded)
    columns = padded.T
    lane = lax.broadcasted_iota(jnp.int32, (128, 128), 1)
    inside = (lane >= offset) & (lane < offset + PANEL)

    def rows_update(i):
        def piece():
            rows = slice(i, i + 128)
            old = h_ref[rows, :]
            out_ref[rows, :] = old - product(halves(h_ref[rows, wide]), split, NN)
            out_ref[rows, wide] = jnp.where(inside, columns[rows, :], out_ref[rows, wide])
            if i == wide.start:
                out_ref[at, :] = turned
                out_ref[at, at] = -inverse

        return piece

    work = [rows_update(i) for i in range(0, size, 128)]
    if next_ref:
        after = slice(at.stop, at.stop + PANEL)
        block = h_ref[after, after] - product(
            halves(h_ref[after, wide]), tuple(x[:, after] for x in split), NN
        )
        next_ref[0][...] = inverse_beside(block, work)
    else:
        for piece in work:
            piece()


def fit_kernel(shard_ref, minus_ref, high_ref, low_ref, own_ref, other_ref, x_ref, err_ref, yt):
    rows, lanes = own_ref.shape[0] // 2, own_ref.shape[1]
    place = shard_ref[0] % 4
    for s, ref in ((1, own_ref), (3, own_ref), (0, other_ref), (2, other_ref)):
        half = s // 2
        yt[:, aligned(place ^ s, lanes)] = means(ref[half * rows : (half + 1) * rows, :])
    target = yt[...]
    attend = high_ref[...], low_ref[...]
    cross = product(halves(target), attend, NT)
    fitted = -product(halves(cross), halves(minus_ref[...]), NN)
    x_ref[...] = fitted
    misfit = product(halves(fitted), attend, NN) - target
    error = jnp.sum(misfit * misfit) / jnp.sum(target * target)
    err_ref[...] = jnp.full(err_ref.shape, error, F32)


def flip_kernel(x_ref, out_ref):
    out_ref[...] = x_ref[...].T


def mean_kernel(heads, *refs):
    total = refs[0][:1, :1]
    for ref in refs[1:-1]:
        total = total + ref[:1, :1]
    refs[-1][...] = total / heads


def per_device(queries, keys, values, kept, roots):
    rows, dims = queries.shape[2:]
    slab, count = keys.shape[1], kept.shape[1]
    lanes = rows // 4
    score_scale = 1.0 / math.sqrt(dims)
    shard = lax.axis_index("ctx").astype(jnp.int32).reshape(1)

    attend_to = functools.partial(attention, lanes, score_scale)
    pieces, kept_pieces, keep, came = spread(shard, queries[0, 0], kept, keys[0], roots, values[0], attend_to)
    rounds = target_rounds(shard, keep, came)
    came = next(rounds)
    ends = None

    def beside(arrays):
        nonlocal came, ends
        if ends is None:
            arrays, came = lax.optimization_barrier((arrays, came))
            try:
                came = rounds.send(came)
            except StopIteration as stop:
                ends = stop.value
        return arrays

    system_shape = ((count, count), F32)
    attend = call(
        functools.partial(attend_kernel, score_scale),
        (shard, *pieces, *kept_pieces),
        [((count, rows), BF16)] * 2,
        10**6,
        scratch=[pltpu.VMEM((count, dims), BF16)],
        name="attend",
    )
    attend = beside(attend)
    (system,) = call(gram_kernel, attend, [system_shape], 4 * 10**9, name="gram")
    system = beside(system)
    panels = count // PANEL
    block_shape = ((PANEL, PANEL), F32)
    (inverse,) = call(invert_kernel, (system,), [block_shape], 10**9, name="invert")
    for panel in range(panels):
        last = panel == panels - 1
        system, *inverse = call(
            functools.partial(sweep_kernel, panel),
            (system, inverse),
            [system_shape] if last else [system_shape, block_shape],
            2 * 10**9,
            name="sweep",
        )
        inverse = None if last else inverse[0]
        if panel in (0, 2, 3, 5, 6):
            system, inverse = beside((system, inverse))
    while ends is None:
        system = beside(system)

    turned_fit, error = call(
        fit_kernel,
        (shard, system, *attend, *ends),
        [((dims, count), F32), ((SUB, 128), F32)],
        10**9,
        scratch=[pltpu.VMEM((dims, rows), F32)],
        name="fit",
    )
    heads = lax.axis_size("head")
    errors, step = [error], 1
    while step < heads:
        if len(errors) > 1:
            errors = list(call(sum_kernel, errors, [((SUB, 128), F32)], name="total"))
        errors.append(swap(errors[0], "head", step))
        step *= 2
    (compact,) = call(flip_kernel, (turned_fit,), [((count, dims), F32)], 10**6, name="flip")
    (error,) = call(functools.partial(mean_kernel, heads), errors, [((1, 1), F32)], name="mean")
    return (compact[None], error.reshape(()))


def solution(mesh):
    placed = (
        P("head", "ctx", None, None),
        P("head", "ctx", None),
        P("head", "ctx", None),
        P("head", None),
        P("head"),
    )
    return jax.shard_map(
        per_device,
        mesh=mesh,
        in_specs=placed,
        out_specs=(P("head", None, None), P()),
        check_vma=False,
    )
```

```python
import functools
import math

import jax
import jax.numpy as jnp
from jax import lax
from jax.experimental import pallas as pl
from jax.experimental.pallas import tpu as pltpu
from jax.sharding import PartitionSpec as P

KBLK = 1024
PANEL = 64
SUB = 8
RIDGE_SHARE = 0.01
F32 = jnp.float32
BF16 = jnp.bfloat16
VMEM_LIMIT = 48 * 1024 * 1024
VMEM = pl.BlockSpec(memory_space=pltpu.VMEM)
SMEM = pl.BlockSpec(memory_space=pltpu.SMEM)
HBM = pl.BlockSpec(memory_space=pltpu.HBM)
NT = (((1,), (1,)), ((), ()))
TN = (((0,), (0,)), ((), ()))
NN = (((1,), (0,)), ((), ()))


def swap(array, axis, step):
    size = lax.axis_size(axis)
    return lax.ppermute(array, axis, [(i, i ^ step) for i in range(size)])


def one_way(array, step, core):
    size = lax.axis_size("ctx")
    return lax.ppermute(array, "ctx", [(i, i ^ step) for i in range(size) if i % 2 == core])


def call(kernel, ins, outs, cost=10**5, scratch=(), name=None, specs=None):
    return pl.pallas_call(
        kernel,
        in_specs=specs or [SMEM if x.size == 1 else VMEM for x in ins],
        out_specs=[VMEM] * len(outs),
        out_shape=[jax.ShapeDtypeStruct(shape, kind) for shape, kind in outs],
        scratch_shapes=list(scratch),
        compiler_params=pltpu.CompilerParams(vmem_limit_bytes=VMEM_LIMIT),
        cost_estimate=pl.CostEstimate(flops=cost, bytes_accessed=10**5, transcendentals=0),
        name=name,
    )(*ins)


def aligned(value, unit):
    return pl.ds(pl.multiple_of(value * unit, unit), unit)


def halves(array):
    high = array.astype(BF16)
    return high, (array - high.astype(F32)).astype(BF16)


def dot(left, right, dims):
    return lax.dot_general(left, right, dims, preferred_element_type=F32)


def product(left, right, dims):
    (high, low), (right_high, right_low) = left, right
    rows = high.shape[0]
    both = dot(jnp.concatenate([high, low], axis=0), right_high, dims)
    return both[:rows] + (both[rows:] + dot(high, right_low, dims))


def pack(out, top, total):
    rows = out.shape[0] // 2
    mean = out * (1.0 / total)
    code = (jnp.max(jnp.abs(mean), axis=0, keepdims=True) * 2.0**27).astype(jnp.int32) + 1
    fixed = jnp.round(mean * (32767.0 / (code.astype(F32) * 2.0**-27))).astype(jnp.int32)
    words = (fixed[:rows] << 16) | (fixed[rows:] & 0xFFFF)
    level = jnp.floor(top + jnp.log2(total))
    rest = (total * jnp.exp2(top - level) * 2.0**28).astype(jnp.int32)
    blank = jnp.zeros((SUB - 3, top.shape[1]), jnp.int32)
    return jnp.concatenate([words, code, level.astype(jnp.int32), rest, blank], axis=0)


def means(packed):
    rows = packed.shape[0] - SUB
    words = packed[:rows]
    fixed = jnp.concatenate([words >> 16, (words << 16) >> 16], axis=0)
    return fixed.astype(F32) * (packed[rows : rows + 1].astype(F32) * (2.0**-27 / 32767.0))


def tail(top, total):
    return jnp.concatenate([top, total, jnp.zeros((SUB - 2, top.shape[1]), F32)], axis=0)


def partial_of(ref):
    rows = ref.shape[0] - SUB
    if ref.dtype == F32:
        return ref[:rows, :], ref[rows : rows + 1, :], ref[rows + 1 : rows + 2, :]
    packed = ref[...]
    rest = packed[rows + 2 : rows + 3].astype(F32) * 2.0**-28
    return means(packed) * rest, packed[rows + 1 : rows + 2].astype(F32), rest


def put_partial(ref, out, top, total):
    if ref.dtype == F32:
        ref[: out.shape[0], :] = out
        ref[out.shape[0] :, :] = tail(top, total)
    else:
        ref[...] = pack(out, top, total)


def partial_shape(rows, lanes, packed):
    if packed and rows % 16 == 0:
        return (rows // 2 + SUB, lanes), jnp.int32
    return (rows + SUB, lanes), F32


def prepare_kernel(window, shard_ref, root_ref, q_hbm, kept_hbm, k_hbm, *refs):
    keep_ref, send_ref, k_ref, q_ref, kept_ref, spots, picked, sems = refs
    slab, dims = k_ref.shape
    kept = kept_ref.shape[1]
    steps = sems.shape[0] - 2
    chunk = slab // steps
    loads = [pltpu.make_async_copy(kept_hbm, kept_ref, sems.at[steps])]
    for i in range(steps):
        part = pl.ds(i * chunk, chunk)
        loads.append(pltpu.make_async_copy(k_hbm.at[part], k_ref.at[part], sems.at[i]))
    loads.append(pltpu.make_async_copy(q_hbm, q_ref, sems.at[steps + 1]))
    for load in loads:
        load.start()
    base = shard_ref[0] * slab
    loads[0].wait()
    positions = kept_ref[...]
    before = jnp.sum((positions < base).astype(jnp.int32))
    start = jnp.minimum(before // 16, (kept - window) // 16)
    local = (positions - base).astype(F32)
    for i in range(0, kept, 128):
        spots[i : i + 128, :] = jnp.broadcast_to(local[:, i : i + 128], (128, 128)).T
    spot = pl.ds(pl.multiple_of(start * 16, 16), window)
    mine = spots[spot, :]
    column = lax.broadcasted_iota(jnp.int32, (window, 128), 1).astype(F32)
    rows = jnp.zeros((window, dims), F32)
    for i in range(steps):
        onehot = jnp.concatenate(
            [jnp.where(mine == column + float(j), 1.0, 0.0).astype(BF16) for j in range(i * chunk, (i + 1) * chunk, 128)],
            axis=1,
        )
        loads[1 + i].wait()
        rows += lax.dot_general(onehot, k_ref[i * chunk : (i + 1) * chunk, :], NN, preferred_element_type=F32)
    picked[...] = jnp.zeros_like(picked)
    picked[spot, :] = rows.astype(BF16)
    loads[-1].wait()
    share, part = q_ref.shape[0] // 4, kept // 4
    is_root = shard_ref[0] == root_ref[0]
    tall = share + part
    for s in range(4):
        out, at = (keep_ref, send_ref)[s % 2], s // 2 * tall
        place = (shard_ref[0] % 4) ^ s
        q = q_ref[aligned(place, share), :]
        out[at : at + share, :] = jnp.where(is_root, q, jnp.zeros_like(q))
        out[at + share : at + tall, :] = picked[aligned(place, part), :]


def sum_kernel(*refs):
    total = refs[0][...]
    for ref in refs[1:-1]:
        total = total + ref[...]
    refs[-1][...] = total


def halve_kernel(a_ref, b_ref, near_ref, far_ref):
    rows = near_ref.shape[0]
    near_ref[...] = a_ref[:rows, :] + b_ref[:rows, :]
    far_ref[...] = a_ref[rows:, :] + b_ref[rows:, :]


def stack_kernel(a_ref, b_ref, out_ref):
    rows = a_ref.shape[0]
    out_ref[:rows, :] = a_ref[...]
    out_ref[rows:, :] = b_ref[...]


def spread(shard, queries, kept, keys, roots, values, attend_to):
    (rows, dims), (slab, _) = queries.shape, keys.shape
    count = kept.shape[1]
    devices = lax.axis_size("ctx")
    quarter = ((rows + count) // 4, dims)
    half = (2 * quarter[0], dims)
    in_hbm = lambda x: pltpu.with_memory_space_constraint(x, pltpu.HBM)
    keep, send, keys = call(
        functools.partial(prepare_kernel, 4 * count // devices + 16),
        (shard, roots, in_hbm(queries), in_hbm(kept), in_hbm(keys)),
        [(half, BF16)] * 2 + [(keys.shape, BF16)],
        scratch=[
            pltpu.VMEM((rows, dims), BF16),
            pltpu.VMEM((1, count), jnp.int32),
            pltpu.VMEM((count, 128), F32),
            pltpu.VMEM((count, dims), BF16),
            pltpu.SemaphoreType.DMA((6,)),
        ],
        name="prepare",
        specs=[SMEM, SMEM, HBM, HBM, HBM],
    )
    near, far = call(halve_kernel, (keep, swap(send, "ctx", 1)), [(quarter, BF16)] * 2, name="halve")
    total = lambda arrays: call(sum_kernel, arrays, [(quarter, BF16)], name="total")[0]
    came = swap(far, "ctx", 2)
    (turned,) = call(turn_kernel, (values,), [((dims + 16, slab), BF16)], 10**7, name="turn")
    came, turned = lax.optimization_barrier((came, turned))
    near = total([near, came])
    step = 4
    while step < devices:
        ways = math.gcd(devices // step, 4)
        near = total([near] + [swap(near, "ctx", t * step) for t in range(1, ways)])
        step *= ways
    far = swap(near, "ctx", 2)
    first = attend_to(near, keys, turned)
    far, first = lax.optimization_barrier((far, first))
    (both,) = call(stack_kernel, (near, far), [(half, BF16)], name="stack")
    other = swap(both, "ctx", 1)
    partials, handed = [first], [one_way(first, 1, 0)]
    second = attend_to(far, keys, turned)
    other, second = lax.optimization_barrier((other, second))
    partials.append(second)
    handed.append(one_way(second, 1, 0))
    third = attend_to(other, keys, turned, start=quarter[0])
    partials.append(third)
    handed.append(one_way(third, 1, 0))
    shape, kind = partial_shape(values.shape[1], 2 * (rows // 4), True)
    (send,) = call(far_half_kernel, (second, third, handed[1], handed[2]), [(shape, kind)], name="far_half")
    other, send = lax.optimization_barrier((other, send))
    came = one_way(send, 2, 1)
    fourth = attend_to(other, keys, turned)
    partials.append(fourth)
    handed.append(one_way(fourth, 1, 0))
    return near, far, other, (first, fourth, handed[0], handed[3], came)


def turn_kernel(v_ref, vt_ref):
    dims = v_ref.shape[1]
    vt_ref[:dims, :] = v_ref[...].T
    vt_ref[dims:, :] = jnp.ones((vt_ref.shape[0] - dims, v_ref.shape[0]), BF16)


def attention_kernel(start, block, score_scale, q_ref, k_ref, vt_ref, out_ref):
    dims = k_ref.shape[1]
    lanes = out_ref.shape[1]
    factor = score_scale * math.log2(math.e)
    queries = q_ref[start : start + lanes, :]
    scores = lambda b: dot(k_ref[b : b + block, :], queries, NT)
    slab = k_ref.shape[0]
    ahead = scores(0)
    for b in range(0, slab, block):
        s = ahead
        if b + block < slab:
            ahead = scores(b + block)
        top = jnp.max(s, axis=0, keepdims=True)
        e = jnp.exp2((s - top) * factor).astype(BF16)
        out = dot(vt_ref[:, b : b + block], e, NN)
        top = top * factor
        total = out[dims : dims + 1, :]
        out = out[:dims, :]
        if b:
            joint = jnp.maximum(old_top, top)
            old_scale = jnp.exp2(old_top - joint)
            new_scale = jnp.exp2(top - joint)
            out = old_out * old_scale + out * new_scale
            total = old_total * old_scale + total * new_scale
            top = joint
        old_out, old_top, old_total = out, top, total
    put_partial(out_ref, out, top, total)


def attention(lanes, score_scale, piece, keys, turned, start=0, packed=True):
    slab, dims = keys.shape
    return call(
        functools.partial(attention_kernel, start, min(KBLK, slab), score_scale),
        (piece, keys, turned),
        [partial_shape(dims, lanes, packed)],
        10**6,
        name="attention",
    )[0]


def join(*parts):
    top = functools.reduce(jnp.maximum, [part[1] for part in parts])
    scales = [jnp.exp2(part[1] - top) for part in parts]
    total = sum(part[2] * scale for part, scale in zip(parts, scales))
    out = sum(part[0] * scale for part, scale in zip(parts, scales))
    return out, top, total


def merged(*refs):
    return join(*[partial_of(ref) for ref in refs])


def far_half_kernel(second_ref, third_ref, handed_second_ref, handed_third_ref, out_ref):
    lanes = second_ref.shape[1]
    out_ref[:, :lanes] = pack(*merged(third_ref, handed_second_ref))
    out_ref[:, lanes:] = pack(*merged(second_ref, handed_third_ref))


def near_half_kernel(step, shard_ref, first_ref, fourth_ref, handed_first_ref, handed_fourth_ref, came_ref, keep_ref, send_ref, work):
    lanes = first_ref.shape[1]
    own = [merged(fourth_ref, handed_first_ref), merged(first_ref, handed_fourth_ref)]
    own = [jnp.concatenate(pair, axis=1) for pair in zip(*own)]
    out, top, total = join(tuple(own), partial_of(came_ref))
    split_rows(step, shard_ref, out, top, total, keep_ref, send_ref, work)


def split_rows(step, shard_ref, out, top, total, keep_ref, send_ref, work):
    rows = out.shape[0] // 2
    work[...] = out
    bit = (shard_ref[0] // step) % 2
    put_partial(keep_ref, work[aligned(bit, rows), :], top, total)
    put_partial(send_ref, work[aligned(1 - bit, rows), :], top, total)


def merge_kernel(step, shard_ref, *refs):
    split_rows(step, shard_ref, *merged(*refs[:-3]), *refs[-3:])


def finish_kernel(*refs):
    out, _, total = merged(*refs[:-1])
    refs[-1][...] = out / total


def stack_rows_kernel(step, shard_ref, a_ref, b_ref, out_ref):
    rows = a_ref.shape[0]
    bit = (shard_ref[0] // step) % 2
    out_ref[aligned(bit, rows), :] = a_ref[...]
    out_ref[aligned(1 - bit, rows), :] = b_ref[...]


def pack_kernel(y_ref, out_ref):
    one = jnp.ones((1, y_ref.shape[1]), F32)
    out_ref[...] = pack(y_ref[...], one * 0.0, one)


def target_rounds(shard, parts):
    dims, lanes = 2 * (parts[0].shape[0] - SUB), 2 * parts[0].shape[1]
    devices = lax.axis_size("ctx")
    parts = yield list(parts)
    steps = [2**i for i in range(2, devices.bit_length() - 1)]
    rows, kernel = dims, near_half_kernel
    for step in steps:
        keep, send = call(
            functools.partial(kernel, step),
            (shard, *parts),
            [partial_shape(rows // 2, lanes, packed) for packed in (False, True)],
            scratch=[pltpu.VMEM((rows, lanes), F32)],
            name="merge",
        )
        came = yield [one_way(send, step, 1)]
        parts, kernel = (keep, *came), merge_kernel
        rows //= 2
    (block,) = call(finish_kernel, parts, [((rows, lanes), F32)], name="finish")
    for step in reversed(steps):
        came = yield [one_way(block, step, 1)]
        rows *= 2
        (block,) = call(
            functools.partial(stack_rows_kernel, step), (shard, block, *came), [((rows, lanes), F32)], name="stack"
        )
    shape, kind = partial_shape(dims, lanes, True)
    (block,) = call(pack_kernel, (block,), [(shape, kind)], name="pack")
    came = yield [one_way(block, 2, 1)]
    (block,) = call(stack_kernel, (block, *came), [((2 * shape[0], lanes), kind)], name="stack")
    came = yield [one_way(block, 1, 1)]
    return block, *came


def attend_kernel(score_scale, shard_ref, near_ref, far_ref, other_ref, high_ref, low_ref, c_all):
    part, rows = c_all.shape[0] // 4, high_ref.shape[1] // 4
    tall = part + rows
    pieces = [(near_ref, 0), (other_ref, 0), (far_ref, 0), (other_ref, tall)]
    places = [(shard_ref[0] % 4) ^ s for s in range(4)]
    for place, (ref, at) in zip(places, pieces):
        c_all[aligned(place, part), :] = ref[at + rows : at + tall, :]
    for place, (ref, at) in zip(places, pieces):
        scores = lax.dot_general(c_all[...], ref[at : at + rows, :], NT, preferred_element_type=F32) * score_scale
        weights = jnp.exp(scores - jnp.max(scores, axis=0, keepdims=True))
        weights = weights * (1.0 / jnp.sum(weights, axis=0, keepdims=True))
        high_ref[:, aligned(place, rows)], low_ref[:, aligned(place, rows)] = halves(weights)


def gram_kernel(high_ref, low_ref, h_ref):
    high, low = high_ref[...], low_ref[...]
    cross = dot(high, low, NT)
    gram = dot(high, high, NT) + (dot(low, low, NT) + (cross + cross.T))
    kept = gram.shape[0]
    diagonal = lax.broadcasted_iota(jnp.int32, gram.shape, 0) == lax.broadcasted_iota(jnp.int32, gram.shape, 1)
    trace = jnp.sum(jnp.where(diagonal, gram, 0.0))
    h_ref[...] = gram + jnp.where(diagonal, RIDGE_SHARE * trace / kept, 0.0)


def invert_block(rows):
    count = len(rows)
    size = count * SUB
    lane = lax.broadcasted_iota(jnp.int32, (SUB, size), 1)
    sub = lax.broadcasted_iota(jnp.int32, (SUB, size), 0)
    spread_lane = lambda array, column: jnp.broadcast_to(array[:, column : column + 1], (SUB, size))
    line = lambda array, row: jnp.broadcast_to(array[row : row + 1, :], (SUB, size))
    for k in range(count):
        base = k * SUB
        inside = (lane >= base) & (lane < base + SUB)
        columns = [spread_lane(rows[k], base + j) for j in range(SUB)]
        work = jnp.where(inside, jnp.where(lane - base == sub, 1.0, 0.0), rows[k])
        for j in range(0, SUB, 2):
            first, second = columns[j], columns[j + 1]
            a, b, c, d = line(first, j), line(second, j), line(first, j + 1), line(second, j + 1)
            inverse = 1.0 / (a * d - b * c)
            at_first, at_second = sub == j, sub == j + 1

            def step(v):
                upper, lower = line(v, j), line(v, j + 1)
                new_upper = (d * upper - b * lower) * inverse
                new_lower = (a * lower - c * upper) * inverse
                other = v - (first * new_upper + second * new_lower)
                return jnp.where(at_first, new_upper, jnp.where(at_second, new_lower, other))

            for i in range(j + 2, SUB):
                columns[i] = step(columns[i])
            work = step(work)
        lines = [line(work, j) for j in range(SUB)]
        updated = list(rows)
        updated[k] = work
        for i in list(range(k + 1, count)) + list(range(k)):
            terms = [spread_lane(rows[i], base + j) * lines[j] for j in range(SUB)]
            while len(terms) > 1:
                terms = [x + y for x, y in zip(terms[::2], terms[1::2])]
            updated[i] = jnp.where(inside, 0.0, rows[i]) - terms[0]
        rows = updated
        yield
    return jnp.concatenate(rows, axis=0)


def inverse_beside(block, work=()):
    work = list(work)
    groups = invert_block([block[i : i + SUB, :] for i in range(0, block.shape[0], SUB)])
    while True:
        try:
            next(groups)
        except StopIteration as stop:
            for piece in work:
                piece()
            return stop.value
        if work:
            work.pop(0)()


def invert_kernel(h_ref, out_ref):
    out_ref[...] = inverse_beside(h_ref[:PANEL, :PANEL])


def sweep_kernel(panel, h_ref, inverse_ref, out_ref, *next_ref):
    size = h_ref.shape[0]
    at = slice(panel * PANEL, (panel + 1) * PANEL)
    wide = slice(panel * PANEL // 128 * 128, panel * PANEL // 128 * 128 + 128)
    offset = at.start - wide.start
    inverse = inverse_ref[...]
    turned = product(halves(inverse), halves(h_ref[at, :]), NN)
    padded = jnp.concatenate(
        [turned if i == offset else jnp.zeros_like(turned) for i in range(0, 128, PANEL)], axis=0
    )
    split = halves(padded)
    columns = padded.T
    lane = lax.broadcasted_iota(jnp.int32, (128, 128), 1)
    inside = (lane >= offset) & (lane < offset + PANEL)

    def rows_update(i):
        def piece():
            rows = slice(i, i + 128)
            old = h_ref[rows, :]
            out_ref[rows, :] = old - product(halves(h_ref[rows, wide]), split, NN)
            out_ref[rows, wide] = jnp.where(inside, columns[rows, :], out_ref[rows, wide])
            if i == wide.start:
                out_ref[at, :] = turned
                out_ref[at, at] = -inverse

        return piece

    work = [rows_update(i) for i in range(0, size, 128)]
    if next_ref:
        after = slice(at.stop, at.stop + PANEL)
        block = h_ref[after, after] - product(
            halves(h_ref[after, wide]), tuple(x[:, after] for x in split), NN
        )
        next_ref[0][...] = inverse_beside(block, work)
    else:
        for piece in work:
            piece()


def fit_kernel(shard_ref, minus_ref, high_ref, low_ref, own_ref, other_ref, x_ref, err_ref, yt):
    rows, lanes = own_ref.shape[0] // 2, own_ref.shape[1]
    is_core_1, y = shard_ref[0] % 2 == 1, shard_ref[0] // 2 % 2
    packed = jnp.where(is_core_1, own_ref[...], other_ref[...])
    for half in range(2):
        yt[:, aligned(y ^ half, lanes)] = means(packed[half * rows : (half + 1) * rows])
    target = yt[...]
    attend = high_ref[...], low_ref[...]
    cross = product(halves(target), attend, NT)
    fitted = -product(halves(cross), halves(minus_ref[...]), NN)
    x_ref[...] = fitted
    misfit = product(halves(fitted), attend, NN) - target
    error = jnp.sum(misfit * misfit) / jnp.sum(target * target)
    err_ref[...] = jnp.full(err_ref.shape, error, F32)


def flip_kernel(x_ref, out_ref):
    out_ref[...] = x_ref[...].T


def mean_kernel(heads, *refs):
    total = refs[0][:1, :1]
    for ref in refs[1:-1]:
        total = total + ref[:1, :1]
    refs[-1][...] = total / heads


def per_device(queries, keys, values, kept, roots):
    rows, dims = queries.shape[2:]
    slab, count = keys.shape[1], kept.shape[1]
    lanes = rows // 4
    score_scale = 1.0 / math.sqrt(dims)
    shard = lax.axis_index("ctx").astype(jnp.int32).reshape(1)

    attend_to = functools.partial(attention, lanes, score_scale)
    near, far, other, parts = spread(shard, queries[0, 0], kept, keys[0], roots, values[0], attend_to)
    rounds = target_rounds(shard, parts)
    came = next(rounds)
    ends = None

    def beside(arrays):
        nonlocal came, ends
        if ends is None:
            arrays, came = lax.optimization_barrier((arrays, came))
            try:
                came = rounds.send(came)
            except StopIteration as stop:
                ends = stop.value
        return arrays

    system_shape = ((count, count), F32)
    attend = call(
        functools.partial(attend_kernel, score_scale),
        (shard, near, far, other),
        [((count, rows), BF16)] * 2,
        10**6,
        scratch=[pltpu.VMEM((count, dims), BF16)],
        name="attend",
    )
    attend = beside(attend)
    (system,) = call(gram_kernel, attend, [system_shape], 4 * 10**9, name="gram")
    system = beside(system)
    panels = count // PANEL
    block_shape = ((PANEL, PANEL), F32)
    (inverse,) = call(invert_kernel, (system,), [block_shape], 10**9, name="invert")
    for panel in range(panels):
        last = panel == panels - 1
        system, *inverse = call(
            functools.partial(sweep_kernel, panel),
            (system, inverse),
            [system_shape] if last else [system_shape, block_shape],
            2 * 10**9,
            name="sweep",
        )
        inverse = None if last else inverse[0]
        if panel in (0, 2, 3, 5, 6):
            system, inverse = beside((system, inverse))
    while ends is None:
        system = beside(system)

    turned_fit, error = call(
        fit_kernel,
        (shard, system, *attend, *ends),
        [((dims, count), F32), ((SUB, 128), F32)],
        10**9,
        scratch=[pltpu.VMEM((dims, rows), F32)],
        name="fit",
    )
    heads = lax.axis_size("head")
    errors, step = [error], 1
    while step < heads:
        if len(errors) > 1:
            errors = list(call(sum_kernel, errors, [((SUB, 128), F32)], name="total"))
        errors.append(swap(errors[0], "head", step))
        step *= 2
    (compact,) = call(flip_kernel, (turned_fit,), [((count, dims), F32)], 10**6, name="flip")
    (error,) = call(functools.partial(mean_kernel, heads), errors, [((1, 1), F32)], name="mean")
    return (compact[None], error.reshape(()))


def solution(mesh):
    placed = (
        P("head", "ctx", None, None),
        P("head", "ctx", None),
        P("head", "ctx", None),
        P("head", None),
        P("head"),
    )
    return jax.shard_map(
        per_device,
        mesh=mesh,
        in_specs=placed,
        out_specs=(P("head", None, None), P()),
        check_vma=False,
    )
```

```python
import functools
import math

import jax
import jax.numpy as jnp
from jax import lax
from jax.experimental import pallas as pl
from jax.experimental.pallas import tpu as pltpu
from jax.sharding import PartitionSpec as P

KBLK = 1024
PANEL = 64
SUB = 8
RIDGE_SHARE = 0.01
F32 = jnp.float32
BF16 = jnp.bfloat16
VMEM_LIMIT = 48 * 1024 * 1024
VMEM = pl.BlockSpec(memory_space=pltpu.VMEM)
SMEM = pl.BlockSpec(memory_space=pltpu.SMEM)
HBM = pl.BlockSpec(memory_space=pltpu.HBM)
NT = (((1,), (1,)), ((), ()))
TN = (((0,), (0,)), ((), ()))
NN = (((1,), (0,)), ((), ()))


def swap(array, axis, step):
    size = lax.axis_size(axis)
    return lax.ppermute(array, axis, [(i, i ^ step) for i in range(size)])


def call(kernel, ins, outs, cost=10**5, scratch=(), name=None, specs=None):
    return pl.pallas_call(
        kernel,
        in_specs=specs or [SMEM if x.size == 1 else VMEM for x in ins],
        out_specs=[VMEM] * len(outs),
        out_shape=[jax.ShapeDtypeStruct(shape, kind) for shape, kind in outs],
        scratch_shapes=list(scratch),
        compiler_params=pltpu.CompilerParams(vmem_limit_bytes=VMEM_LIMIT),
        cost_estimate=pl.CostEstimate(flops=cost, bytes_accessed=10**5, transcendentals=0),
        name=name,
    )(*ins)


def aligned(value, unit):
    return pl.ds(pl.multiple_of(value * unit, unit), unit)


def halves(array):
    high = array.astype(BF16)
    return high, (array - high.astype(F32)).astype(BF16)


def dot(left, right, dims):
    return lax.dot_general(left, right, dims, preferred_element_type=F32)


def product(left, right, dims):
    (high, low), (right_high, right_low) = left, right
    rows = high.shape[0]
    both = dot(jnp.concatenate([high, low], axis=0), right_high, dims)
    return both[:rows] + (both[rows:] + dot(high, right_low, dims))


def pack(out, top, total):
    rows = out.shape[0] // 2
    mean = out * (1.0 / total)
    code = (jnp.max(jnp.abs(mean), axis=0, keepdims=True) * 2.0**27).astype(jnp.int32) + 1
    fixed = jnp.round(mean * (32767.0 / (code.astype(F32) * 2.0**-27))).astype(jnp.int32)
    words = (fixed[:rows] << 16) | (fixed[rows:] & 0xFFFF)
    level = jnp.floor(top + jnp.log2(total))
    rest = (total * jnp.exp2(top - level) * 2.0**28).astype(jnp.int32)
    blank = jnp.zeros((SUB - 3, top.shape[1]), jnp.int32)
    return jnp.concatenate([words, code, level.astype(jnp.int32), rest, blank], axis=0)


def means(packed):
    rows = packed.shape[0] - SUB
    words = packed[:rows]
    fixed = jnp.concatenate([words >> 16, (words << 16) >> 16], axis=0)
    return fixed.astype(F32) * (packed[rows : rows + 1].astype(F32) * (2.0**-27 / 32767.0))


def tail(top, total):
    return jnp.concatenate([top, total, jnp.zeros((SUB - 2, top.shape[1]), F32)], axis=0)


def partial_of(ref):
    rows = ref.shape[0] - SUB
    if ref.dtype == F32:
        return ref[:rows, :], ref[rows : rows + 1, :], ref[rows + 1 : rows + 2, :]
    packed = ref[...]
    rest = packed[rows + 2 : rows + 3].astype(F32) * 2.0**-28
    return means(packed) * rest, packed[rows + 1 : rows + 2].astype(F32), rest


def put_partial(ref, out, top, total):
    if ref.dtype == F32:
        ref[: out.shape[0], :] = out
        ref[out.shape[0] :, :] = tail(top, total)
    else:
        ref[...] = pack(out, top, total)


def partial_shape(rows, lanes, packed):
    if packed and rows % 16 == 0:
        return (rows // 2 + SUB, lanes), jnp.int32
    return (rows + SUB, lanes), F32


def prepare_kernel(window, shard_ref, root_ref, q_hbm, kept_hbm, k_hbm, *refs):
    keep_ref, send_ref, k_ref, q_ref, kept_ref, spots, picked, sems = refs
    slab, dims = k_ref.shape
    kept = kept_ref.shape[1]
    steps = sems.shape[0] - 2
    chunk = slab // steps
    loads = [pltpu.make_async_copy(kept_hbm, kept_ref, sems.at[steps])]
    for i in range(steps):
        part = pl.ds(i * chunk, chunk)
        loads.append(pltpu.make_async_copy(k_hbm.at[part], k_ref.at[part], sems.at[i]))
    loads.append(pltpu.make_async_copy(q_hbm, q_ref, sems.at[steps + 1]))
    for load in loads:
        load.start()
    base = shard_ref[0] * slab
    loads[0].wait()
    positions = kept_ref[...]
    before = jnp.sum((positions < base).astype(jnp.int32))
    start = jnp.minimum(before // 16, (kept - window) // 16)
    local = (positions - base).astype(F32)
    for i in range(0, kept, 128):
        spots[i : i + 128, :] = jnp.broadcast_to(local[:, i : i + 128], (128, 128)).T
    spot = pl.ds(pl.multiple_of(start * 16, 16), window)
    mine = spots[spot, :]
    column = lax.broadcasted_iota(jnp.int32, (window, 128), 1).astype(F32)
    rows = jnp.zeros((window, dims), F32)
    for i in range(steps):
        onehot = jnp.concatenate(
            [jnp.where(mine == column + float(j), 1.0, 0.0).astype(BF16) for j in range(i * chunk, (i + 1) * chunk, 128)],
            axis=1,
        )
        loads[1 + i].wait()
        rows += lax.dot_general(onehot, k_ref[i * chunk : (i + 1) * chunk, :], NN, preferred_element_type=F32)
    picked[...] = jnp.zeros_like(picked)
    picked[spot, :] = rows.astype(BF16)
    loads[-1].wait()
    share, part = q_ref.shape[0] // 4, kept // 4
    is_root = shard_ref[0] == root_ref[0]
    tall = share + part
    for s in range(4):
        out, at = (keep_ref, send_ref)[s % 2], s // 2 * tall
        place = (shard_ref[0] % 4) ^ s
        q = q_ref[aligned(place, share), :]
        out[at : at + share, :] = jnp.where(is_root, q, jnp.zeros_like(q))
        out[at + share : at + tall, :] = picked[aligned(place, part), :]


def sum_kernel(*refs):
    total = refs[0][...]
    for ref in refs[1:-1]:
        total = total + ref[...]
    refs[-1][...] = total


def halve_kernel(a_ref, b_ref, near_ref, far_ref):
    rows = near_ref.shape[0]
    near_ref[...] = a_ref[:rows, :] + b_ref[:rows, :]
    far_ref[...] = a_ref[rows:, :] + b_ref[rows:, :]


def stack_kernel(a_ref, b_ref, out_ref):
    rows = a_ref.shape[0]
    out_ref[:rows, :] = a_ref[...]
    out_ref[rows:, :] = b_ref[...]


def spread(shard, queries, kept, keys, roots, values, attend_to):
    (rows, dims), (slab, _) = queries.shape, keys.shape
    count = kept.shape[1]
    devices = lax.axis_size("ctx")
    quarter = ((rows + count) // 4, dims)
    half = (2 * quarter[0], dims)
    in_hbm = lambda x: pltpu.with_memory_space_constraint(x, pltpu.HBM)
    keep, send, keys = call(
        functools.partial(prepare_kernel, 4 * count // devices + 16),
        (shard, roots, in_hbm(queries), in_hbm(kept), in_hbm(keys)),
        [(half, BF16)] * 2 + [(keys.shape, BF16)],
        scratch=[
            pltpu.VMEM((rows, dims), BF16),
            pltpu.VMEM((1, count), jnp.int32),
            pltpu.VMEM((count, 128), F32),
            pltpu.VMEM((count, dims), BF16),
            pltpu.SemaphoreType.DMA((6,)),
        ],
        name="prepare",
        specs=[SMEM, SMEM, HBM, HBM, HBM],
    )
    near, far = call(halve_kernel, (keep, swap(send, "ctx", 1)), [(quarter, BF16)] * 2, name="halve")
    total = lambda arrays: call(sum_kernel, arrays, [(quarter, BF16)], name="total")[0]
    came = swap(far, "ctx", 2)
    (turned,) = call(turn_kernel, (values,), [((dims + 16, slab), BF16)], 10**7, name="turn")
    came, turned = lax.optimization_barrier((came, turned))
    near = total([near, came])
    step = 4
    while step < devices:
        ways = math.gcd(devices // step, 4)
        near = total([near] + [swap(near, "ctx", t * step) for t in range(1, ways)])
        step *= ways
    far = swap(near, "ctx", 2)
    first = attend_to(near, keys, turned)
    far, first = lax.optimization_barrier((far, first))
    (both,) = call(stack_kernel, (near, far), [(half, BF16)], name="stack")
    other, came = swap(both, "ctx", 1), [swap(first, "ctx", 1)]
    second = attend_to(far, keys, turned)
    other, second = lax.optimization_barrier((other, second))
    came.append(swap(second, "ctx", 3))
    third = attend_to(other, keys, turned, start=quarter[0])
    came.append(swap(third, "ctx", 2))
    other, third = lax.optimization_barrier((other, third))
    return near, far, other, attend_to(other, keys, turned, packed=False), came


def turn_kernel(v_ref, vt_ref):
    dims = v_ref.shape[1]
    vt_ref[:dims, :] = v_ref[...].T
    vt_ref[dims:, :] = jnp.ones((vt_ref.shape[0] - dims, v_ref.shape[0]), BF16)


def attention_kernel(start, block, score_scale, q_ref, k_ref, vt_ref, out_ref):
    dims = k_ref.shape[1]
    lanes = out_ref.shape[1]
    factor = score_scale * math.log2(math.e)
    queries = q_ref[start : start + lanes, :]
    scores = lambda b: dot(k_ref[b : b + block, :], queries, NT)
    slab = k_ref.shape[0]
    ahead = scores(0)
    for b in range(0, slab, block):
        s = ahead
        if b + block < slab:
            ahead = scores(b + block)
        top = jnp.max(s, axis=0, keepdims=True)
        e = jnp.exp2((s - top) * factor).astype(BF16)
        out = dot(vt_ref[:, b : b + block], e, NN)
        top = top * factor
        total = out[dims : dims + 1, :]
        out = out[:dims, :]
        if b:
            joint = jnp.maximum(old_top, top)
            old_scale = jnp.exp2(old_top - joint)
            new_scale = jnp.exp2(top - joint)
            out = old_out * old_scale + out * new_scale
            total = old_total * old_scale + total * new_scale
            top = joint
        old_out, old_top, old_total = out, top, total
    put_partial(out_ref, out, top, total)


def attention(lanes, score_scale, piece, keys, turned, start=0, packed=True):
    slab, dims = keys.shape
    return call(
        functools.partial(attention_kernel, start, min(KBLK, slab), score_scale),
        (piece, keys, turned),
        [partial_shape(dims, lanes, packed)],
        10**6,
        name="attention",
    )[0]


def merged(*refs):
    parts = [partial_of(ref) for ref in refs]
    top = functools.reduce(jnp.maximum, [part[1] for part in parts])
    scales = [jnp.exp2(part[1] - top) for part in parts]
    total = sum(part[2] * scale for part, scale in zip(parts, scales))
    out = sum(part[0] * scale for part, scale in zip(parts, scales))
    return out, top, total


def merge_kernel(*refs):
    put_partial(refs[-1], *merged(*refs[:-1]))


def target_rounds(keep, came):
    dims, lanes = keep.shape[0] - SUB, keep.shape[1]
    shape, kind = partial_shape(dims, lanes, True)
    came = yield came
    (mine,) = call(merge_kernel, (keep, *came), [(shape, kind)], name="merge")
    step = 4
    while step < lax.axis_size("ctx"):
        came = yield [swap(mine, "ctx", step)]
        (mine,) = call(merge_kernel, (mine, *came), [(shape, kind)], name="merge")
        step *= 2
    came = yield [swap(mine, "ctx", 2)]
    (both,) = call(stack_kernel, (mine, *came), [((2 * shape[0], lanes), kind)], name="stack")
    came = yield [swap(both, "ctx", 1)]
    return both, *came


def attend_kernel(score_scale, shard_ref, near_ref, far_ref, other_ref, high_ref, low_ref, c_all):
    part, rows = c_all.shape[0] // 4, high_ref.shape[1] // 4
    tall = part + rows
    pieces = [(near_ref, 0), (other_ref, 0), (far_ref, 0), (other_ref, tall)]
    places = [(shard_ref[0] % 4) ^ s for s in range(4)]
    for place, (ref, at) in zip(places, pieces):
        c_all[aligned(place, part), :] = ref[at + rows : at + tall, :]
    for place, (ref, at) in zip(places, pieces):
        scores = lax.dot_general(c_all[...], ref[at : at + rows, :], NT, preferred_element_type=F32) * score_scale
        weights = jnp.exp(scores - jnp.max(scores, axis=0, keepdims=True))
        weights = weights * (1.0 / jnp.sum(weights, axis=0, keepdims=True))
        high_ref[:, aligned(place, rows)], low_ref[:, aligned(place, rows)] = halves(weights)


def gram_kernel(high_ref, low_ref, h_ref):
    high, low = high_ref[...], low_ref[...]
    cross = dot(high, low, NT)
    gram = dot(high, high, NT) + (dot(low, low, NT) + (cross + cross.T))
    kept = gram.shape[0]
    diagonal = lax.broadcasted_iota(jnp.int32, gram.shape, 0) == lax.broadcasted_iota(jnp.int32, gram.shape, 1)
    trace = jnp.sum(jnp.where(diagonal, gram, 0.0))
    h_ref[...] = gram + jnp.where(diagonal, RIDGE_SHARE * trace / kept, 0.0)


def invert_block(rows):
    count = len(rows)
    size = count * SUB
    lane = lax.broadcasted_iota(jnp.int32, (SUB, size), 1)
    sub = lax.broadcasted_iota(jnp.int32, (SUB, size), 0)
    spread_lane = lambda array, column: jnp.broadcast_to(array[:, column : column + 1], (SUB, size))
    line = lambda array, row: jnp.broadcast_to(array[row : row + 1, :], (SUB, size))
    for k in range(count):
        base = k * SUB
        inside = (lane >= base) & (lane < base + SUB)
        columns = [spread_lane(rows[k], base + j) for j in range(SUB)]
        work = jnp.where(inside, jnp.where(lane - base == sub, 1.0, 0.0), rows[k])
        for j in range(0, SUB, 2):
            first, second = columns[j], columns[j + 1]
            a, b, c, d = line(first, j), line(second, j), line(first, j + 1), line(second, j + 1)
            inverse = 1.0 / (a * d - b * c)
            at_first, at_second = sub == j, sub == j + 1

            def step(v):
                upper, lower = line(v, j), line(v, j + 1)
                new_upper = (d * upper - b * lower) * inverse
                new_lower = (a * lower - c * upper) * inverse
                other = v - (first * new_upper + second * new_lower)
                return jnp.where(at_first, new_upper, jnp.where(at_second, new_lower, other))

            for i in range(j + 2, SUB):
                columns[i] = step(columns[i])
            work = step(work)
        lines = [line(work, j) for j in range(SUB)]
        updated = list(rows)
        updated[k] = work
        for i in list(range(k + 1, count)) + list(range(k)):
            terms = [spread_lane(rows[i], base + j) * lines[j] for j in range(SUB)]
            while len(terms) > 1:
                terms = [x + y for x, y in zip(terms[::2], terms[1::2])]
            updated[i] = jnp.where(inside, 0.0, rows[i]) - terms[0]
        rows = updated
        yield
    return jnp.concatenate(rows, axis=0)


def inverse_beside(block, work=()):
    work = list(work)
    groups = invert_block([block[i : i + SUB, :] for i in range(0, block.shape[0], SUB)])
    while True:
        try:
            next(groups)
        except StopIteration as stop:
            for piece in work:
                piece()
            return stop.value
        if work:
            work.pop(0)()


def invert_kernel(h_ref, out_ref):
    out_ref[...] = inverse_beside(h_ref[:PANEL, :PANEL])


def sweep_kernel(panel, h_ref, inverse_ref, out_ref, *next_ref):
    size = h_ref.shape[0]
    at = slice(panel * PANEL, (panel + 1) * PANEL)
    wide = slice(panel * PANEL // 128 * 128, panel * PANEL // 128 * 128 + 128)
    offset = at.start - wide.start
    inverse = inverse_ref[...]
    turned = product(halves(inverse), halves(h_ref[at, :]), NN)
    padded = jnp.concatenate(
        [turned if i == offset else jnp.zeros_like(turned) for i in range(0, 128, PANEL)], axis=0
    )
    split = halves(padded)
    columns = padded.T
    lane = lax.broadcasted_iota(jnp.int32, (128, 128), 1)
    inside = (lane >= offset) & (lane < offset + PANEL)

    def rows_update(i):
        def piece():
            rows = slice(i, i + 128)
            old = h_ref[rows, :]
            out_ref[rows, :] = old - product(halves(h_ref[rows, wide]), split, NN)
            out_ref[rows, wide] = jnp.where(inside, columns[rows, :], out_ref[rows, wide])
            if i == wide.start:
                out_ref[at, :] = turned
                out_ref[at, at] = -inverse

        return piece

    work = [rows_update(i) for i in range(0, size, 128)]
    if next_ref:
        after = slice(at.stop, at.stop + PANEL)
        block = h_ref[after, after] - product(
            halves(h_ref[after, wide]), tuple(x[:, after] for x in split), NN
        )
        next_ref[0][...] = inverse_beside(block, work)
    else:
        for piece in work:
            piece()


def fit_kernel(shard_ref, minus_ref, high_ref, low_ref, own_ref, other_ref, x_ref, err_ref, yt):
    rows, lanes = own_ref.shape[0] // 2, own_ref.shape[1]
    place = shard_ref[0] % 4
    for s, ref in ((1, own_ref), (3, own_ref), (0, other_ref), (2, other_ref)):
        half = s // 2
        yt[:, aligned(place ^ s, lanes)] = means(ref[half * rows : (half + 1) * rows, :])
    target = yt[...]
    attend = high_ref[...], low_ref[...]
    cross = product(halves(target), attend, NT)
    fitted = -product(halves(cross), halves(minus_ref[...]), NN)
    x_ref[...] = fitted
    misfit = product(halves(fitted), attend, NN) - target
    error = jnp.sum(misfit * misfit) / jnp.sum(target * target)
    err_ref[...] = jnp.full(err_ref.shape, error, F32)


def flip_kernel(x_ref, out_ref):
    out_ref[...] = x_ref[...].T


def mean_kernel(heads, *refs):
    total = refs[0][:1, :1]
    for ref in refs[1:-1]:
        total = total + ref[:1, :1]
    refs[-1][...] = total / heads


def per_device(queries, keys, values, kept, roots):
    rows, dims = queries.shape[2:]
    slab, count = keys.shape[1], kept.shape[1]
    lanes = rows // 4
    score_scale = 1.0 / math.sqrt(dims)
    shard = lax.axis_index("ctx").astype(jnp.int32).reshape(1)

    attend_to = functools.partial(attention, lanes, score_scale)
    near, far, other, keep, came = spread(shard, queries[0, 0], kept, keys[0], roots, values[0], attend_to)
    rounds = target_rounds(keep, came)
    came = next(rounds)
    ends = None

    def beside(arrays):
        nonlocal came, ends
        if ends is None:
            arrays, came = lax.optimization_barrier((arrays, came))
            try:
                came = rounds.send(came)
            except StopIteration as stop:
                ends = stop.value
        return arrays

    system_shape = ((count, count), F32)
    attend = call(
        functools.partial(attend_kernel, score_scale),
        (shard, near, far, other),
        [((count, rows), BF16)] * 2,
        10**6,
        scratch=[pltpu.VMEM((count, dims), BF16)],
        name="attend",
    )
    attend = beside(attend)
    (system,) = call(gram_kernel, attend, [system_shape], 4 * 10**9, name="gram")
    panels = count // PANEL
    block_shape = ((PANEL, PANEL), F32)
    (inverse,) = call(invert_kernel, (system,), [block_shape], 10**9, name="invert")
    system, inverse = beside((system, inverse))
    for panel in range(panels):
        last = panel == panels - 1
        system, *inverse = call(
            functools.partial(sweep_kernel, panel),
            (system, inverse),
            [system_shape] if last else [system_shape, block_shape],
            2 * 10**9,
            name="sweep",
        )
        inverse = None if last else inverse[0]
        if panel in (2, 4, 6):
            system, inverse = beside((system, inverse))
    while ends is None:
        system = beside(system)

    turned_fit, error = call(
        fit_kernel,
        (shard, system, *attend, *ends),
        [((dims, count), F32), ((SUB, 128), F32)],
        10**9,
        scratch=[pltpu.VMEM((dims, rows), F32)],
        name="fit",
    )
    heads = lax.axis_size("head")
    errors, step = [error], 1
    while step < heads:
        if len(errors) > 1:
            errors = list(call(sum_kernel, errors, [((SUB, 128), F32)], name="total"))
        errors.append(swap(errors[0], "head", step))
        step *= 2
    (compact,) = call(flip_kernel, (turned_fit,), [((count, dims), F32)], 10**6, name="flip")
    (error,) = call(functools.partial(mean_kernel, heads), errors, [((1, 1), F32)], name="mean")
    return (compact[None], error.reshape(()))


def solution(mesh):
    placed = (
        P("head", "ctx", None, None),
        P("head", "ctx", None),
        P("head", "ctx", None),
        P("head", None),
        P("head"),
    )
    return jax.shard_map(
        per_device,
        mesh=mesh,
        in_specs=placed,
        out_specs=(P("head", None, None), P()),
        check_vma=False,
    )
```

```python
import functools
import math

import jax
import jax.numpy as jnp
from jax import lax
from jax.experimental import pallas as pl
from jax.experimental.pallas import tpu as pltpu
from jax.sharding import PartitionSpec as P

KBLK = 1024
PANEL = 64
SUB = 8
RIDGE_SHARE = 0.01
F32 = jnp.float32
BF16 = jnp.bfloat16
VMEM_LIMIT = 48 * 1024 * 1024
VMEM = pl.BlockSpec(memory_space=pltpu.VMEM)
SMEM = pl.BlockSpec(memory_space=pltpu.SMEM)
HBM = pl.BlockSpec(memory_space=pltpu.HBM)
NT = (((1,), (1,)), ((), ()))
TN = (((0,), (0,)), ((), ()))
NN = (((1,), (0,)), ((), ()))


def swap(array, axis, step):
    size = lax.axis_size(axis)
    return lax.ppermute(array, axis, [(i, i ^ step) for i in range(size)])


def call(kernel, ins, outs, cost=10**5, scratch=(), name=None, specs=None):
    return pl.pallas_call(
        kernel,
        in_specs=specs or [SMEM if x.size == 1 else VMEM for x in ins],
        out_specs=[VMEM] * len(outs),
        out_shape=[jax.ShapeDtypeStruct(shape, kind) for shape, kind in outs],
        scratch_shapes=list(scratch),
        compiler_params=pltpu.CompilerParams(vmem_limit_bytes=VMEM_LIMIT),
        cost_estimate=pl.CostEstimate(flops=cost, bytes_accessed=10**5, transcendentals=0),
        name=name,
    )(*ins)


def aligned(value, unit):
    return pl.ds(pl.multiple_of(value * unit, unit), unit)


def halves(array):
    high = array.astype(BF16)
    return high, (array - high.astype(F32)).astype(BF16)


def dot(left, right, dims):
    return lax.dot_general(left, right, dims, preferred_element_type=F32)


def product(left, right, dims):
    (high, low), (right_high, right_low) = left, right
    rows = high.shape[0]
    both = dot(jnp.concatenate([high, low], axis=0), right_high, dims)
    return both[:rows] + (both[rows:] + dot(high, right_low, dims))


def pack(out, top, total):
    rows = out.shape[0] // 2
    mean = out * (1.0 / total)
    code = (jnp.max(jnp.abs(mean), axis=0, keepdims=True) * 2.0**27).astype(jnp.int32) + 1
    fixed = jnp.round(mean * (32767.0 / (code.astype(F32) * 2.0**-27))).astype(jnp.int32)
    words = (fixed[:rows] << 16) | (fixed[rows:] & 0xFFFF)
    level = jnp.floor(top + jnp.log2(total))
    rest = (total * jnp.exp2(top - level) * 2.0**28).astype(jnp.int32)
    blank = jnp.zeros((SUB - 3, top.shape[1]), jnp.int32)
    return jnp.concatenate([words, code, level.astype(jnp.int32), rest, blank], axis=0)


def means(packed):
    rows = packed.shape[0] - SUB
    words = packed[:rows]
    fixed = jnp.concatenate([words >> 16, (words << 16) >> 16], axis=0)
    return fixed.astype(F32) * (packed[rows : rows + 1].astype(F32) * (2.0**-27 / 32767.0))


def tail(top, total):
    return jnp.concatenate([top, total, jnp.zeros((SUB - 2, top.shape[1]), F32)], axis=0)


def partial_of(ref):
    rows = ref.shape[0] - SUB
    if ref.dtype == F32:
        return ref[:rows, :], ref[rows : rows + 1, :], ref[rows + 1 : rows + 2, :]
    packed = ref[...]
    rest = packed[rows + 2 : rows + 3].astype(F32) * 2.0**-28
    return means(packed) * rest, packed[rows + 1 : rows + 2].astype(F32), rest


def put_partial(ref, out, top, total):
    if ref.dtype == F32:
        ref[: out.shape[0], :] = out
        ref[out.shape[0] :, :] = tail(top, total)
    else:
        ref[...] = pack(out, top, total)


def partial_shape(rows, lanes, packed):
    if packed and rows % 16 == 0:
        return (rows // 2 + SUB, lanes), jnp.int32
    return (rows + SUB, lanes), F32


def prepare_kernel(window, shard_ref, root_ref, q_hbm, kept_hbm, k_hbm, *refs):
    keep_ref, send_ref, k_ref, q_ref, kept_ref, spots, picked, sems = refs
    slab, dims = k_ref.shape
    kept = kept_ref.shape[1]
    steps = sems.shape[0] - 2
    chunk = slab // steps
    loads = [pltpu.make_async_copy(kept_hbm, kept_ref, sems.at[steps])]
    for i in range(steps):
        part = pl.ds(i * chunk, chunk)
        loads.append(pltpu.make_async_copy(k_hbm.at[part], k_ref.at[part], sems.at[i]))
    loads.append(pltpu.make_async_copy(q_hbm, q_ref, sems.at[steps + 1]))
    for load in loads:
        load.start()
    base = shard_ref[0] * slab
    loads[0].wait()
    positions = kept_ref[...]
    before = jnp.sum((positions < base).astype(jnp.int32))
    start = jnp.minimum(before // 16, (kept - window) // 16)
    local = (positions - base).astype(F32)
    for i in range(0, kept, 128):
        spots[i : i + 128, :] = jnp.broadcast_to(local[:, i : i + 128], (128, 128)).T
    spot = pl.ds(pl.multiple_of(start * 16, 16), window)
    mine = spots[spot, :]
    column = lax.broadcasted_iota(jnp.int32, (window, 128), 1).astype(F32)
    rows = jnp.zeros((window, dims), F32)
    for i in range(steps):
        onehot = jnp.concatenate(
            [jnp.where(mine == column + float(j), 1.0, 0.0).astype(BF16) for j in range(i * chunk, (i + 1) * chunk, 128)],
            axis=1,
        )
        loads[1 + i].wait()
        rows += lax.dot_general(onehot, k_ref[i * chunk : (i + 1) * chunk, :], NN, preferred_element_type=F32)
    picked[...] = jnp.zeros_like(picked)
    picked[spot, :] = rows.astype(BF16)
    loads[-1].wait()
    share, part = q_ref.shape[0] // 4, kept // 4
    is_root = shard_ref[0] == root_ref[0]
    tall = share + part
    for s in range(4):
        out, at = (keep_ref, send_ref)[s % 2], s // 2 * tall
        place = (shard_ref[0] % 4) ^ s
        q = q_ref[aligned(place, share), :]
        out[at : at + share, :] = jnp.where(is_root, q, jnp.zeros_like(q))
        out[at + share : at + tall, :] = picked[aligned(place, part), :]


def sum_kernel(*refs):
    total = refs[0][...]
    for ref in refs[1:-1]:
        total = total + ref[...]
    refs[-1][...] = total


def halve_kernel(a_ref, b_ref, near_ref, far_ref):
    rows = near_ref.shape[0]
    near_ref[...] = a_ref[:rows, :] + b_ref[:rows, :]
    far_ref[...] = a_ref[rows:, :] + b_ref[rows:, :]


def stack_kernel(a_ref, b_ref, out_ref):
    rows = a_ref.shape[0]
    out_ref[:rows, :] = a_ref[...]
    out_ref[rows:, :] = b_ref[...]


def spread(shard, queries, kept, keys, roots, values, attend_to):
    (rows, dims), (slab, _) = queries.shape, keys.shape
    count = kept.shape[1]
    devices = lax.axis_size("ctx")
    quarter = ((rows + count) // 4, dims)
    half = (2 * quarter[0], dims)
    in_hbm = lambda x: pltpu.with_memory_space_constraint(x, pltpu.HBM)
    keep, send, keys = call(
        functools.partial(prepare_kernel, 4 * count // devices + 16),
        (shard, roots, in_hbm(queries), in_hbm(kept), in_hbm(keys)),
        [(half, BF16)] * 2 + [(keys.shape, BF16)],
        scratch=[
            pltpu.VMEM((rows, dims), BF16),
            pltpu.VMEM((1, count), jnp.int32),
            pltpu.VMEM((count, 128), F32),
            pltpu.VMEM((count, dims), BF16),
            pltpu.SemaphoreType.DMA((6,)),
        ],
        name="prepare",
        specs=[SMEM, SMEM, HBM, HBM, HBM],
    )
    near, far = call(halve_kernel, (keep, swap(send, "ctx", 1)), [(quarter, BF16)] * 2, name="halve")
    total = lambda arrays: call(sum_kernel, arrays, [(quarter, BF16)], name="total")[0]
    came = swap(far, "ctx", 2)
    (turned,) = call(turn_kernel, (values,), [((dims + 16, slab), BF16)], 10**7, name="turn")
    came, turned = lax.optimization_barrier((came, turned))
    near = total([near, came])
    step = 4
    while step < devices:
        ways = math.gcd(devices // step, 4)
        near = total([near] + [swap(near, "ctx", t * step) for t in range(1, ways)])
        step *= ways
    far = swap(near, "ctx", 2)
    first = attend_to(near, keys, turned)
    far, first = lax.optimization_barrier((far, first))
    (both,) = call(stack_kernel, (near, far), [(half, BF16)], name="stack")
    other, came = swap(both, "ctx", 1), [swap(first, "ctx", 1)]
    second = attend_to(far, keys, turned)
    other, second = lax.optimization_barrier((other, second))
    came.append(swap(second, "ctx", 3))
    third = attend_to(other, keys, turned, start=quarter[0])
    came.append(swap(third, "ctx", 2))
    other, third = lax.optimization_barrier((other, third))
    return near, far, other, attend_to(other, keys, turned, packed=False), came


def turn_kernel(v_ref, vt_ref):
    dims = v_ref.shape[1]
    vt_ref[:dims, :] = v_ref[...].T
    vt_ref[dims:, :] = jnp.ones((vt_ref.shape[0] - dims, v_ref.shape[0]), BF16)


def attention_kernel(start, block, score_scale, q_ref, k_ref, vt_ref, out_ref):
    dims = k_ref.shape[1]
    lanes = out_ref.shape[1]
    factor = score_scale * math.log2(math.e)
    queries = q_ref[start : start + lanes, :]
    scores = lambda b: dot(k_ref[b : b + block, :], queries, NT)
    slab = k_ref.shape[0]
    ahead = scores(0)
    for b in range(0, slab, block):
        s = ahead
        if b + block < slab:
            ahead = scores(b + block)
        top = jnp.max(s, axis=0, keepdims=True)
        e = jnp.exp2((s - top) * factor).astype(BF16)
        out = dot(vt_ref[:, b : b + block], e, NN)
        top = top * factor
        total = out[dims : dims + 1, :]
        out = out[:dims, :]
        if b:
            joint = jnp.maximum(old_top, top)
            old_scale = jnp.exp2(old_top - joint)
            new_scale = jnp.exp2(top - joint)
            out = old_out * old_scale + out * new_scale
            total = old_total * old_scale + total * new_scale
            top = joint
        old_out, old_top, old_total = out, top, total
    put_partial(out_ref, out, top, total)


def attention(lanes, score_scale, piece, keys, turned, start=0, packed=True):
    slab, dims = keys.shape
    return call(
        functools.partial(attention_kernel, start, min(KBLK, slab), score_scale),
        (piece, keys, turned),
        [partial_shape(dims, lanes, packed)],
        10**6,
        name="attention",
    )[0]


def merged(*refs):
    parts = [partial_of(ref) for ref in refs]
    top = functools.reduce(jnp.maximum, [part[1] for part in parts])
    scales = [jnp.exp2(part[1] - top) for part in parts]
    total = sum(part[2] * scale for part, scale in zip(parts, scales))
    out = sum(part[0] * scale for part, scale in zip(parts, scales))
    return out, top, total


def merge_kernel(*refs):
    put_partial(refs[-1], *merged(*refs[:-1]))


def target_rounds(keep, came):
    dims, lanes = keep.shape[0] - SUB, keep.shape[1]
    shape, kind = partial_shape(dims, lanes, True)
    came = yield came
    (mine,) = call(merge_kernel, (keep, *came), [(shape, kind)], name="merge")
    step = 4
    while step < lax.axis_size("ctx"):
        came = yield [swap(mine, "ctx", step)]
        (mine,) = call(merge_kernel, (mine, *came), [(shape, kind)], name="merge")
        step *= 2
    came = yield [swap(mine, "ctx", 2)]
    (both,) = call(stack_kernel, (mine, *came), [((2 * shape[0], lanes), kind)], name="stack")
    came = yield [swap(both, "ctx", 1)]
    return both, *came


def attend_kernel(score_scale, shard_ref, near_ref, far_ref, other_ref, high_ref, low_ref, square_ref, c_all):
    part, rows = c_all.shape[0] // 4, high_ref.shape[1] // 4
    tall = part + rows
    pieces = [(near_ref, 0), (other_ref, 0), (far_ref, 0), (other_ref, tall)]
    places = [(shard_ref[0] % 4) ^ s for s in range(4)]
    for place, (ref, at) in zip(places, pieces):
        c_all[aligned(place, part), :] = ref[at + rows : at + tall, :]
    for place, (ref, at) in zip(places, pieces):
        scores = lax.dot_general(c_all[...], ref[at : at + rows, :], NT, preferred_element_type=F32) * score_scale
        weights = jnp.exp(scores - jnp.max(scores, axis=0, keepdims=True))
        weights = weights * (1.0 / jnp.sum(weights, axis=0, keepdims=True))
        high_ref[:, aligned(place, rows)], low_ref[:, aligned(place, rows)] = halves(weights)
        square_ref[aligned(place, SUB), :] = jnp.sum((weights * weights).reshape(-1, SUB, rows), axis=0)


def gram_kernel(high_ref, low_ref, square_ref, h_ref, inverse_ref):
    kept = high_ref.shape[0]
    ridge = RIDGE_SHARE * jnp.sum(square_ref[...]) / kept
    row = lax.broadcasted_iota(jnp.int32, (128, kept), 0)
    column = lax.broadcasted_iota(jnp.int32, (128, kept), 1)

    def system(start, rows, columns):
        at = slice(start, start + rows)
        left = jnp.concatenate([high_ref[at, :], low_ref[at, :]], axis=0)
        by_high, by_low = dot(left, high_ref[:columns, :], NT), dot(left, low_ref[:columns, :], NT)
        gram = by_high[:rows] + (by_high[rows:] + by_low[:rows] + by_low[rows:])
        return gram + jnp.where(row[:rows, :columns] + start == column[:rows, :columns], ridge, 0.0)

    def piece(start):
        def fill():
            h_ref[start : start + 128, :] = system(start, 128, kept)

        return fill

    inverse_ref[...] = inverse_beside(system(0, PANEL, PANEL), [piece(i) for i in range(0, kept, 128)])


def invert_block(rows):
    count = len(rows)
    size = count * SUB
    lane = lax.broadcasted_iota(jnp.int32, (SUB, size), 1)
    sub = lax.broadcasted_iota(jnp.int32, (SUB, size), 0)
    spread_lane = lambda array, column: jnp.broadcast_to(array[:, column : column + 1], (SUB, size))
    line = lambda array, row: jnp.broadcast_to(array[row : row + 1, :], (SUB, size))
    def less(old, left, right):
        terms = [x * y for x, y in zip(left, right)]
        while len(terms) > 1:
            terms = [x + y for x, y in zip(terms[::2], terms[1::2])]
        return old - terms[0]

    ahead = []
    for k in range(count):
        base = k * SUB
        inside = (lane >= base) & (lane < base + SUB)
        columns = ahead + [spread_lane(rows[k], base + j) for j in range(len(ahead), SUB)]
        work = jnp.where(inside, jnp.where(lane - base == sub, 1.0, 0.0), rows[k])
        beyond = [spread_lane(rows[k], base + SUB + j) for j in range(2)] if k + 1 < count else []
        full = columns + [work] + beyond
        bare = list(full)
        for j in range(0, SUB, 2):
            first, second = full[j], full[j + 1]
            a, b, c, d = line(bare[j], j), line(bare[j + 1], j), line(bare[j], j + 1), line(bare[j + 1], j + 1)
            inverse = 1.0 / (a * d - b * c)
            for i in range(j + 2, len(full)):
                upper, lower = line(bare[i], j), line(bare[i], j + 1)
                new_upper = (d * upper - b * lower) * inverse
                new_lower = (a * lower - c * upper) * inverse
                bare[i] = full[i] - (first * new_upper + second * new_lower)
                full[i] = jnp.where(sub == j, new_upper, jnp.where(sub == j + 1, new_lower, bare[i]))
        work, beyond = full[SUB], full[SUB + 1 :]
        lines = [line(work, j) for j in range(SUB)]
        updated = list(rows)
        updated[k] = work
        for i in list(range(k + 1, count)) + list(range(k)):
            factors = [spread_lane(rows[i], base + j) for j in range(SUB)]
            if i == k + 1:
                ahead = [
                    less(spread_lane(rows[i], base + SUB + j), factors, [line(array, m) for m in range(SUB)])
                    for j, array in enumerate(beyond)
                ]
            updated[i] = less(jnp.where(inside, 0.0, rows[i]), factors, lines)
        rows = updated
        yield
    return jnp.concatenate(rows, axis=0)


def inverse_beside(block, work=()):
    work = list(work)
    groups = invert_block([block[i : i + SUB, :] for i in range(0, block.shape[0], SUB)])
    while True:
        try:
            next(groups)
        except StopIteration as stop:
            for piece in work:
                piece()
            return stop.value
        if work:
            work.pop(0)()


def sweep_kernel(panel, h_ref, inverse_ref, out_ref, *next_ref):
    size = h_ref.shape[0]
    at = slice(panel * PANEL, (panel + 1) * PANEL)
    wide = slice(panel * PANEL // 128 * 128, panel * PANEL // 128 * 128 + 128)
    offset = at.start - wide.start
    inverse = inverse_ref[...]
    turned = product(halves(inverse), halves(h_ref[at, :]), NN)
    padded = jnp.concatenate(
        [turned if i == offset else jnp.zeros_like(turned) for i in range(0, 128, PANEL)], axis=0
    )
    split = halves(padded)
    columns = padded.T
    lane = lax.broadcasted_iota(jnp.int32, (128, 128), 1)
    inside = (lane >= offset) & (lane < offset + PANEL)

    def rows_update(i):
        def piece():
            rows = slice(i, i + 128)
            old = h_ref[rows, :]
            out_ref[rows, :] = old - product(halves(h_ref[rows, wide]), split, NN)
            out_ref[rows, wide] = jnp.where(inside, columns[rows, :], out_ref[rows, wide])
            if i == wide.start:
                out_ref[at, :] = turned
                out_ref[at, at] = -inverse

        return piece

    work = [rows_update(i) for i in range(0, size, 128)]
    if next_ref:
        after = slice(at.stop, at.stop + PANEL)
        block = h_ref[after, after] - product(
            halves(h_ref[after, wide]), tuple(x[:, after] for x in split), NN
        )
        next_ref[0][...] = inverse_beside(block, work)
    else:
        for piece in work:
            piece()


def fit_kernel(shard_ref, minus_ref, high_ref, low_ref, own_ref, other_ref, x_ref, err_ref, yt):
    rows, lanes = own_ref.shape[0] // 2, own_ref.shape[1]
    place = shard_ref[0] % 4
    for s, ref in ((1, own_ref), (3, own_ref), (0, other_ref), (2, other_ref)):
        half = s // 2
        yt[:, aligned(place ^ s, lanes)] = means(ref[half * rows : (half + 1) * rows, :])
    target = yt[...]
    attend = high_ref[...], low_ref[...]
    cross = product(halves(target), attend, NT)
    fitted = -product(halves(cross), halves(minus_ref[...]), NN)
    x_ref[...] = fitted
    misfit = product(halves(fitted), attend, NN) - target
    error = jnp.sum(misfit * misfit) / jnp.sum(target * target)
    err_ref[...] = jnp.full(err_ref.shape, error, F32)


def flip_kernel(x_ref, out_ref):
    out_ref[...] = x_ref[...].T


def mean_kernel(heads, *refs):
    total = refs[0][:1, :1]
    for ref in refs[1:-1]:
        total = total + ref[:1, :1]
    refs[-1][...] = total / heads


def per_device(queries, keys, values, kept, roots):
    rows, dims = queries.shape[2:]
    slab, count = keys.shape[1], kept.shape[1]
    lanes = rows // 4
    score_scale = 1.0 / math.sqrt(dims)
    shard = lax.axis_index("ctx").astype(jnp.int32).reshape(1)

    attend_to = functools.partial(attention, lanes, score_scale)
    near, far, other, keep, came = spread(shard, queries[0, 0], kept, keys[0], roots, values[0], attend_to)
    rounds = target_rounds(keep, came)
    came = next(rounds)
    ends = None

    def beside(arrays):
        nonlocal came, ends
        if ends is None:
            arrays, came = lax.optimization_barrier((arrays, came))
            try:
                came = rounds.send(came)
            except StopIteration as stop:
                ends = stop.value
        return arrays

    system_shape = ((count, count), F32)
    attend = call(
        functools.partial(attend_kernel, score_scale),
        (shard, near, far, other),
        [((count, rows), BF16)] * 2 + [((4 * SUB, lanes), F32)],
        10**6,
        scratch=[pltpu.VMEM((count, dims), BF16)],
        name="attend",
    )
    attend = beside(attend)
    panels = count // PANEL
    block_shape = ((PANEL, PANEL), F32)
    system, inverse = call(gram_kernel, attend, [system_shape, block_shape], 4 * 10**9, name="gram")
    for panel in range(panels):
        last = panel == panels - 1
        system, *inverse = call(
            functools.partial(sweep_kernel, panel),
            (system, inverse),
            [system_shape] if last else [system_shape, block_shape],
            2 * 10**9,
            name="sweep",
        )
        inverse = None if last else inverse[0]
        if panel in (0, 2, 4, 6):
            system, inverse = beside((system, inverse))
    while ends is None:
        system = beside(system)

    turned_fit, error = call(
        fit_kernel,
        (shard, system, *attend[:2], *ends),
        [((dims, count), F32), ((SUB, 128), F32)],
        10**9,
        scratch=[pltpu.VMEM((dims, rows), F32)],
        name="fit",
    )
    heads = lax.axis_size("head")
    errors, step = [error], 1
    while step < heads:
        if len(errors) > 1:
            errors = list(call(sum_kernel, errors, [((SUB, 128), F32)], name="total"))
        errors.append(swap(errors[0], "head", step))
        step *= 2
    (compact,) = call(flip_kernel, (turned_fit,), [((count, dims), F32)], 10**6, name="flip")
    (error,) = call(functools.partial(mean_kernel, heads), errors, [((1, 1), F32)], name="mean")
    return (compact[None], error.reshape(()))


def solution(mesh):
    placed = (
        P("head", "ctx", None, None),
        P("head", "ctx", None),
        P("head", "ctx", None),
        P("head", None),
        P("head"),
    )
    return jax.shard_map(
        per_device,
        mesh=mesh,
        in_specs=placed,
        out_specs=(P("head", None, None), P()),
        check_vma=False,
    )
```

```python
import functools
import itertools
import math

import jax
import jax.numpy as jnp
from jax import lax
from jax.experimental import pallas as pl
from jax.experimental.pallas import tpu as pltpu
from jax.sharding import PartitionSpec as P

KBLK = 1024
PANEL = 64
SUB = 8
RIDGE_SHARE = 0.01
F32 = jnp.float32
BF16 = jnp.bfloat16
VMEM_LIMIT = 48 * 1024 * 1024
VMEM = pl.BlockSpec(memory_space=pltpu.VMEM)
SMEM = pl.BlockSpec(memory_space=pltpu.SMEM)
HBM = pl.BlockSpec(memory_space=pltpu.HBM)
NT = (((1,), (1,)), ((), ()))
TN = (((0,), (0,)), ((), ()))
NN = (((1,), (0,)), ((), ()))


def swap(array, axis, step):
    size = lax.axis_size(axis)
    return lax.ppermute(array, axis, [(i, i ^ step) for i in range(size)])


def call(kernel, ins, outs, cost=10**5, scratch=(), name=None, specs=None):
    return pl.pallas_call(
        kernel,
        in_specs=specs or [SMEM if x.size == 1 else VMEM for x in ins],
        out_specs=[VMEM] * len(outs),
        out_shape=[jax.ShapeDtypeStruct(shape, kind) for shape, kind in outs],
        scratch_shapes=list(scratch),
        compiler_params=pltpu.CompilerParams(vmem_limit_bytes=VMEM_LIMIT),
        cost_estimate=pl.CostEstimate(flops=cost, bytes_accessed=10**5, transcendentals=0),
        name=name,
    )(*ins)


def aligned(value, unit):
    return pl.ds(pl.multiple_of(value * unit, unit), unit)


def halves(array):
    high = array.astype(BF16)
    return high, (array - high.astype(F32)).astype(BF16)


def dot(left, right, dims):
    return lax.dot_general(left, right, dims, preferred_element_type=F32)


def product(left, right, dims):
    (high, low), (right_high, right_low) = left, right
    rows = high.shape[0]
    both = dot(jnp.concatenate([high, low], axis=0), right_high, dims)
    return both[:rows] + (both[rows:] + dot(high, right_low, dims))


def pack(out, top, total):
    rows = out.shape[0] // 2
    mean = out * (1.0 / total)
    code = (jnp.max(jnp.abs(mean), axis=0, keepdims=True) * 2.0**27).astype(jnp.int32) + 1
    fixed = jnp.round(mean * (32767.0 / (code.astype(F32) * 2.0**-27))).astype(jnp.int32)
    words = (fixed[:rows] << 16) | (fixed[rows:] & 0xFFFF)
    level = jnp.floor(top + jnp.log2(total))
    rest = (total * jnp.exp2(top - level) * 2.0**28).astype(jnp.int32)
    blank = jnp.zeros((SUB - 3, top.shape[1]), jnp.int32)
    return jnp.concatenate([words, code, level.astype(jnp.int32), rest, blank], axis=0)


def means(packed):
    rows = packed.shape[0] - SUB
    words = packed[:rows]
    fixed = jnp.concatenate([words >> 16, (words << 16) >> 16], axis=0)
    return fixed.astype(F32) * (packed[rows : rows + 1].astype(F32) * (2.0**-27 / 32767.0))


def tail(top, total):
    return jnp.concatenate([top, total, jnp.zeros((SUB - 2, top.shape[1]), F32)], axis=0)


def partial_of(ref):
    rows = ref.shape[0] - SUB
    if ref.dtype == F32:
        return ref[:rows, :], ref[rows : rows + 1, :], ref[rows + 1 : rows + 2, :]
    packed = ref[...]
    rest = packed[rows + 2 : rows + 3].astype(F32) * 2.0**-28
    return means(packed) * rest, packed[rows + 1 : rows + 2].astype(F32), rest


def put_partial(ref, out, top, total):
    if ref.dtype == F32:
        ref[: out.shape[0], :] = out
        ref[out.shape[0] :, :] = tail(top, total)
    else:
        ref[...] = pack(out, top, total)


def partial_shape(rows, lanes, packed):
    if packed and rows % 16 == 0:
        return (rows // 2 + SUB, lanes), jnp.int32
    return (rows + SUB, lanes), F32


def prepare_kernel(window, shard_ref, root_ref, q_hbm, kept_hbm, k_hbm, *refs):
    keep_ref, send_ref, k_ref, q_ref, kept_ref, spots, picked, sems = refs
    slab, dims = k_ref.shape
    kept = kept_ref.shape[1]
    steps = sems.shape[0] - 2
    chunk = slab // steps
    loads = [pltpu.make_async_copy(kept_hbm, kept_ref, sems.at[steps])]
    for i in range(steps):
        part = pl.ds(i * chunk, chunk)
        loads.append(pltpu.make_async_copy(k_hbm.at[part], k_ref.at[part], sems.at[i]))
    loads.append(pltpu.make_async_copy(q_hbm, q_ref, sems.at[steps + 1]))
    for load in loads:
        load.start()
    base = shard_ref[0] * slab
    loads[0].wait()
    positions = kept_ref[...]
    before = jnp.sum((positions < base).astype(jnp.int32))
    start = jnp.minimum(before // 16, (kept - window) // 16)
    local = (positions - base).astype(F32)
    for i in range(0, kept, 128):
        spots[i : i + 128, :] = jnp.broadcast_to(local[:, i : i + 128], (128, 128)).T
    spot = pl.ds(pl.multiple_of(start * 16, 16), window)
    mine = spots[spot, :]
    column = lax.broadcasted_iota(jnp.int32, (window, 128), 1).astype(F32)
    rows = jnp.zeros((window, dims), F32)
    for i in range(steps):
        onehot = jnp.concatenate(
            [jnp.where(mine == column + float(j), 1.0, 0.0).astype(BF16) for j in range(i * chunk, (i + 1) * chunk, 128)],
            axis=1,
        )
        loads[1 + i].wait()
        rows += lax.dot_general(onehot, k_ref[i * chunk : (i + 1) * chunk, :], NN, preferred_element_type=F32)
    picked[...] = jnp.zeros_like(picked)
    picked[spot, :] = rows.astype(BF16)
    loads[-1].wait()
    share, part = q_ref.shape[0] // 4, kept // 4
    is_root = shard_ref[0] == root_ref[0]
    tall = share + part
    for s in range(4):
        out, at = (keep_ref, send_ref)[s % 2], s // 2 * tall
        place = (shard_ref[0] % 4) ^ s
        q = q_ref[aligned(place, share), :]
        out[at : at + share, :] = jnp.where(is_root, q, jnp.zeros_like(q))
        out[at + share : at + tall, :] = picked[aligned(place, part), :]


def sum_kernel(*refs):
    total = refs[0][...]
    for ref in refs[1:-1]:
        total = total + ref[...]
    refs[-1][...] = total


def halve_kernel(a_ref, b_ref, near_ref, far_ref):
    rows = near_ref.shape[0]
    near_ref[...] = a_ref[:rows, :] + b_ref[:rows, :]
    far_ref[...] = a_ref[rows:, :] + b_ref[rows:, :]


def stack_kernel(a_ref, b_ref, out_ref):
    rows = a_ref.shape[0]
    out_ref[:rows, :] = a_ref[...]
    out_ref[rows:, :] = b_ref[...]


def spread(shard, queries, kept, keys, roots, values, attend_to):
    (rows, dims), (slab, _) = queries.shape, keys.shape
    count = kept.shape[1]
    devices = lax.axis_size("ctx")
    quarter = ((rows + count) // 4, dims)
    half = (2 * quarter[0], dims)
    in_hbm = lambda x: pltpu.with_memory_space_constraint(x, pltpu.HBM)
    keep, send, keys = call(
        functools.partial(prepare_kernel, 4 * count // devices + 16),
        (shard, roots, in_hbm(queries), in_hbm(kept), in_hbm(keys)),
        [(half, BF16)] * 2 + [(keys.shape, BF16)],
        scratch=[
            pltpu.VMEM((rows, dims), BF16),
            pltpu.VMEM((1, count), jnp.int32),
            pltpu.VMEM((count, 128), F32),
            pltpu.VMEM((count, dims), BF16),
            pltpu.SemaphoreType.DMA((6,)),
        ],
        name="prepare",
        specs=[SMEM, SMEM, HBM, HBM, HBM],
    )
    near, far = call(halve_kernel, (keep, swap(send, "ctx", 1)), [(quarter, BF16)] * 2, name="halve")
    total = lambda arrays: call(sum_kernel, arrays, [(quarter, BF16)], name="total")[0]
    came = swap(far, "ctx", 2)
    (turned,) = call(turn_kernel, (values,), [((dims + 16, slab), BF16)], 10**7, name="turn")
    came, turned = lax.optimization_barrier((came, turned))
    near = total([near, came])
    step = 4
    while step < devices:
        ways = math.gcd(devices // step, 4)
        near = total([near] + [swap(near, "ctx", t * step) for t in range(1, ways)])
        step *= ways
    far = swap(near, "ctx", 2)
    first = attend_to(near, keys, turned)
    far, first = lax.optimization_barrier((far, first))
    (both,) = call(stack_kernel, (near, far), [(half, BF16)], name="stack")
    other, came = swap(both, "ctx", 1), [swap(first, "ctx", 1)]
    second = attend_to(far, keys, turned)
    other, second = lax.optimization_barrier((other, second))
    came.append(swap(second, "ctx", 3))
    return near, far, other, keys, turned, came


def turn_kernel(v_ref, vt_ref):
    dims = v_ref.shape[1]
    vt_ref[:dims, :] = v_ref[...].T
    vt_ref[dims:, :] = jnp.ones((vt_ref.shape[0] - dims, v_ref.shape[0]), BF16)


def attention_pieces(start, block, score_scale, q_ref, k_ref, vt_ref, out_ref):
    dims = k_ref.shape[1]
    slab = k_ref.shape[0]
    lanes = out_ref.shape[1]
    factor = score_scale * math.log2(math.e)
    state = {}

    def scores(b):
        return dot(k_ref[b : b + block, :], q_ref[start : start + lanes, :], NT)

    def step(b):
        s = state["ahead"] if b else scores(0)
        if b + block < slab:
            state["ahead"] = scores(b + block)
        top = jnp.max(s, axis=0, keepdims=True)
        e = jnp.exp2((s - top) * factor).astype(BF16)
        out = dot(vt_ref[:, b : b + block], e, NN)
        part = out[:dims, :], top * factor, out[dims : dims + 1, :]
        state["part"] = join(state["part"], part) if b else part
        if b + block >= slab:
            put_partial(out_ref, *state["part"])

    return [functools.partial(step, b) for b in range(0, slab, block)]


def attention_kernel(start, block, score_scale, *refs):
    for step in attention_pieces(start, block, score_scale, *refs):
        step()


def attention(lanes, score_scale, piece, keys, turned, start=0, packed=True):
    slab, dims = keys.shape
    return call(
        functools.partial(attention_kernel, start, min(KBLK, slab), score_scale),
        (piece, keys, turned),
        [partial_shape(dims, lanes, packed)],
        10**6,
        name="attention",
    )[0]


def join(*parts):
    top = functools.reduce(jnp.maximum, [part[1] for part in parts])
    scales = [jnp.exp2(part[1] - top) for part in parts]
    total = sum(part[2] * scale for part, scale in zip(parts, scales))
    out = sum(part[0] * scale for part, scale in zip(parts, scales))
    return out, top, total


def merged(*refs):
    return join(*[partial_of(ref) for ref in refs])


def merge_kernel(*refs):
    put_partial(refs[-1], *merged(*refs[:-1]))


def target_rounds(keep, came):
    dims, lanes = keep.shape[0] - SUB, keep.shape[1]
    shape, kind = partial_shape(dims, lanes, True)
    came = yield came
    (mine,) = call(merge_kernel, (keep, *came), [(shape, kind)], name="merge")
    step = 4
    while step < lax.axis_size("ctx"):
        came = yield [swap(mine, "ctx", step)]
        (mine,) = call(merge_kernel, (mine, *came), [(shape, kind)], name="merge")
        step *= 2
    came = yield [swap(mine, "ctx", 2)]
    (both,) = call(stack_kernel, (mine, *came), [((2 * shape[0], lanes), kind)], name="stack")
    came = yield [swap(both, "ctx", 1)]
    return both, *came


def attend_kernel(score_scale, shard_ref, near_ref, far_ref, other_ref, high_ref, low_ref, square_ref, c_all):
    part, rows = c_all.shape[0] // 4, high_ref.shape[1] // 4
    tall = part + rows
    pieces = [(near_ref, 0), (other_ref, 0), (far_ref, 0), (other_ref, tall)]
    places = [(shard_ref[0] % 4) ^ s for s in range(4)]
    for place, (ref, at) in zip(places, pieces):
        c_all[aligned(place, part), :] = ref[at + rows : at + tall, :]
    for place, (ref, at) in zip(places, pieces):
        scores = lax.dot_general(c_all[...], ref[at : at + rows, :], NT, preferred_element_type=F32) * score_scale
        weights = jnp.exp(scores - jnp.max(scores, axis=0, keepdims=True))
        weights = weights * (1.0 / jnp.sum(weights, axis=0, keepdims=True))
        high_ref[:, aligned(place, rows)], low_ref[:, aligned(place, rows)] = halves(weights)
        square_ref[aligned(place, SUB), :] = jnp.sum((weights * weights).reshape(-1, SUB, rows), axis=0)


def gram_kernel(start, block, score_scale, high_ref, low_ref, square_ref, q_ref, k_ref, vt_ref, h_ref, inverse_ref, part_ref):
    kept = high_ref.shape[0]
    ridge = RIDGE_SHARE * jnp.sum(square_ref[...]) / kept
    row = lax.broadcasted_iota(jnp.int32, (128, kept), 0)
    column = lax.broadcasted_iota(jnp.int32, (128, kept), 1)

    def system(start, rows, columns):
        at = slice(start, start + rows)
        left = jnp.concatenate([high_ref[at, :], low_ref[at, :]], axis=0)
        by_high, by_low = dot(left, high_ref[:columns, :], NT), dot(left, low_ref[:columns, :], NT)
        gram = by_high[:rows] + (by_high[rows:] + by_low[:rows] + by_low[rows:])
        return gram + jnp.where(row[:rows, :columns] + start == column[:rows, :columns], ridge, 0.0)

    def piece(start):
        def fill():
            h_ref[start : start + 128, :] = system(start, 128, kept)

        return fill

    steps = attention_pieces(start, block, score_scale, q_ref, k_ref, vt_ref, part_ref)
    rows_of = [piece(i) for i in range(0, kept, 128)]
    inverse_ref[...] = inverse_beside(system(0, PANEL, PANEL), alternate(steps, rows_of))


def invert_block(rows):
    count = len(rows)
    size = count * SUB
    lane = lax.broadcasted_iota(jnp.int32, (SUB, size), 1)
    sub = lax.broadcasted_iota(jnp.int32, (SUB, size), 0)
    spread_lane = lambda array, column: jnp.broadcast_to(array[:, column : column + 1], (SUB, size))
    line = lambda array, row: jnp.broadcast_to(array[row : row + 1, :], (SUB, size))
    def less(old, left, right):
        terms = [x * y for x, y in zip(left, right)]
        while len(terms) > 1:
            terms = [x + y for x, y in zip(terms[::2], terms[1::2])]
        return old - terms[0]

    ahead = []
    for k in range(count):
        base = k * SUB
        inside = (lane >= base) & (lane < base + SUB)
        columns = ahead + [spread_lane(rows[k], base + j) for j in range(len(ahead), SUB)]
        work = jnp.where(inside, jnp.where(lane - base == sub, 1.0, 0.0), rows[k])
        beyond = [spread_lane(rows[k], base + SUB + j) for j in range(2)] if k + 1 < count else []
        full = columns + [work] + beyond
        bare = list(full)
        for j in range(0, SUB, 2):
            first, second = full[j], full[j + 1]
            a, b, c, d = line(bare[j], j), line(bare[j + 1], j), line(bare[j], j + 1), line(bare[j + 1], j + 1)
            inverse = 1.0 / (a * d - b * c)
            for i in range(j + 2, len(full)):
                upper, lower = line(bare[i], j), line(bare[i], j + 1)
                new_upper = (d * upper - b * lower) * inverse
                new_lower = (a * lower - c * upper) * inverse
                bare[i] = full[i] - (first * new_upper + second * new_lower)
                full[i] = jnp.where(sub == j, new_upper, jnp.where(sub == j + 1, new_lower, bare[i]))
        work, beyond = full[SUB], full[SUB + 1 :]
        lines = [line(work, j) for j in range(SUB)]
        updated = list(rows)
        updated[k] = work
        for i in list(range(k + 1, count)) + list(range(k)):
            factors = [spread_lane(rows[i], base + j) for j in range(SUB)]
            if i == k + 1:
                ahead = [
                    less(spread_lane(rows[i], base + SUB + j), factors, [line(array, m) for m in range(SUB)])
                    for j, array in enumerate(beyond)
                ]
            updated[i] = less(jnp.where(inside, 0.0, rows[i]), factors, lines)
        rows = updated
        yield
    return jnp.concatenate(rows, axis=0)


def inverse_beside(block, work=()):
    work = list(work)
    groups = invert_block([block[i : i + SUB, :] for i in range(0, block.shape[0], SUB)])
    while True:
        try:
            next(groups)
        except StopIteration as stop:
            for piece in work:
                piece()
            return stop.value
        if work:
            work.pop(0)()


def alternate(*lists):
    return [x for group in itertools.zip_longest(*lists) for x in group if x is not None]


def sweep_kernel(panel, h_ref, inverse_ref, out_ref, *next_ref, steps=()):
    size = h_ref.shape[0]
    at = slice(panel * PANEL, (panel + 1) * PANEL)
    wide = slice(panel * PANEL // 128 * 128, panel * PANEL // 128 * 128 + 128)
    offset = at.start - wide.start
    inverse = inverse_ref[...]
    turned = product(halves(inverse), halves(h_ref[at, :]), NN)
    padded = jnp.concatenate(
        [turned if i == offset else jnp.zeros_like(turned) for i in range(0, 128, PANEL)], axis=0
    )
    split = halves(padded)
    columns = padded.T
    lane = lax.broadcasted_iota(jnp.int32, (128, 128), 1)
    inside = (lane >= offset) & (lane < offset + PANEL)

    def rows_update(i):
        def piece():
            rows = slice(i, i + 128)
            old = h_ref[rows, :]
            out_ref[rows, :] = old - product(halves(h_ref[rows, wide]), split, NN)
            out_ref[rows, wide] = jnp.where(inside, columns[rows, :], out_ref[rows, wide])
            if i == wide.start:
                out_ref[at, :] = turned
                out_ref[at, at] = -inverse

        return piece

    work = alternate(steps, [rows_update(i) for i in range(0, size, 128)])
    if next_ref:
        after = slice(at.stop, at.stop + PANEL)
        block = h_ref[after, after] - product(
            halves(h_ref[after, wide]), tuple(x[:, after] for x in split), NN
        )
        next_ref[0][...] = inverse_beside(block, work)
    else:
        for piece in work:
            piece()


def first_sweep_kernel(start, block, score_scale, h_ref, inverse_ref, q_ref, k_ref, vt_ref, out_ref, next_ref, part_ref):
    steps = attention_pieces(start, block, score_scale, q_ref, k_ref, vt_ref, part_ref)
    sweep_kernel(0, h_ref, inverse_ref, out_ref, next_ref, steps=steps)


def fit_kernel(shard_ref, minus_ref, high_ref, low_ref, own_ref, other_ref, x_ref, err_ref, yt):
    rows, lanes = own_ref.shape[0] // 2, own_ref.shape[1]
    place = shard_ref[0] % 4
    for s, ref in ((1, own_ref), (3, own_ref), (0, other_ref), (2, other_ref)):
        half = s // 2
        yt[:, aligned(place ^ s, lanes)] = means(ref[half * rows : (half + 1) * rows, :])
    target = yt[...]
    attend = high_ref[...], low_ref[...]
    cross = product(halves(target), attend, NT)
    fitted = -product(halves(cross), halves(minus_ref[...]), NN)
    x_ref[...] = fitted
    misfit = product(halves(fitted), attend, NN) - target
    error = jnp.sum(misfit * misfit) / jnp.sum(target * target)
    err_ref[...] = jnp.full(err_ref.shape, error, F32)


def flip_kernel(x_ref, out_ref):
    out_ref[...] = x_ref[...].T


def mean_kernel(heads, *refs):
    total = refs[0][:1, :1]
    for ref in refs[1:-1]:
        total = total + ref[:1, :1]
    refs[-1][...] = total / heads


def per_device(queries, keys, values, kept, roots):
    rows, dims = queries.shape[2:]
    slab, count = keys.shape[1], kept.shape[1]
    lanes = rows // 4
    score_scale = 1.0 / math.sqrt(dims)
    shard = lax.axis_index("ctx").astype(jnp.int32).reshape(1)

    attend_to = functools.partial(attention, lanes, score_scale)
    near, far, other, own_keys, turned, sent = spread(shard, queries[0, 0], kept, keys[0], roots, values[0], attend_to)
    came = ends = rounds = None

    def beside(arrays):
        nonlocal came, ends
        if ends is None:
            arrays, came = lax.optimization_barrier((arrays, came))
            try:
                came = rounds.send(came)
            except StopIteration as stop:
                ends = stop.value
        return arrays

    system_shape = ((count, count), F32)
    attend = call(
        functools.partial(attend_kernel, score_scale),
        (shard, near, far, other),
        [((count, rows), BF16)] * 2 + [((4 * SUB, lanes), F32)],
        10**6,
        scratch=[pltpu.VMEM((count, dims), BF16)],
        name="attend",
    )
    panels = count // PANEL
    block_shape = ((PANEL, PANEL), F32)
    tall = near.shape[0]
    quarter = lambda kernel, s: functools.partial(kernel, s // 2 * tall, min(KBLK, slab), score_scale)
    system, inverse, third = call(
        quarter(gram_kernel, 3),
        (*attend, other, own_keys, turned),
        [system_shape, block_shape, partial_shape(dims, lanes, True)],
        4 * 10**9,
        name="gram",
    )
    sent.append(swap(third, "ctx", 2))
    system, inverse, keep = call(
        quarter(first_sweep_kernel, 1),
        (system, inverse, other, own_keys, turned),
        [system_shape, block_shape, partial_shape(dims, lanes, False)],
        2 * 10**9,
        name="first_sweep",
    )
    rounds = target_rounds(keep, sent)
    came = next(rounds)
    system, inverse = beside((system, inverse))
    for panel in range(1, panels):
        last = panel == panels - 1
        system, *inverse = call(
            functools.partial(sweep_kernel, panel),
            (system, inverse),
            [system_shape] if last else [system_shape, block_shape],
            2 * 10**9,
            name="sweep",
        )
        inverse = None if last else inverse[0]
        if panel in (1, 3, 5, 6):
            system, inverse = beside((system, inverse))
    while ends is None:
        system = beside(system)

    turned_fit, error = call(
        fit_kernel,
        (shard, system, *attend[:2], *ends),
        [((dims, count), F32), ((SUB, 128), F32)],
        10**9,
        scratch=[pltpu.VMEM((dims, rows), F32)],
        name="fit",
    )
    heads = lax.axis_size("head")
    errors, step = [error], 1
    while step < heads:
        if len(errors) > 1:
            errors = list(call(sum_kernel, errors, [((SUB, 128), F32)], name="total"))
        errors.append(swap(errors[0], "head", step))
        step *= 2
    (compact,) = call(flip_kernel, (turned_fit,), [((count, dims), F32)], 10**6, name="flip")
    (error,) = call(functools.partial(mean_kernel, heads), errors, [((1, 1), F32)], name="mean")
    return (compact[None], error.reshape(()))


def solution(mesh):
    placed = (
        P("head", "ctx", None, None),
        P("head", "ctx", None),
        P("head", "ctx", None),
        P("head", None),
        P("head"),
    )
    return jax.shard_map(
        per_device,
        mesh=mesh,
        in_specs=placed,
        out_specs=(P("head", None, None), P()),
        check_vma=False,
    )
```

```python
import functools
import math

import jax
import jax.numpy as jnp
from jax import lax
from jax.experimental import pallas as pl
from jax.experimental.pallas import tpu as pltpu
from jax.sharding import PartitionSpec as P

KBLK = 1024
PANEL = 64
SUB = 8
RIDGE_SHARE = 0.01
F32 = jnp.float32
BF16 = jnp.bfloat16
VMEM_LIMIT = 48 * 1024 * 1024
VMEM = pl.BlockSpec(memory_space=pltpu.VMEM)
SMEM = pl.BlockSpec(memory_space=pltpu.SMEM)
HBM = pl.BlockSpec(memory_space=pltpu.HBM)
NT = (((1,), (1,)), ((), ()))
TN = (((0,), (0,)), ((), ()))
NN = (((1,), (0,)), ((), ()))


def swap(array, axis, step):
    size = lax.axis_size(axis)
    return lax.ppermute(array, axis, [(i, i ^ step) for i in range(size)])


def call(kernel, ins, outs, cost=10**5, scratch=(), name=None, specs=None):
    return pl.pallas_call(
        kernel,
        in_specs=specs or [SMEM if x.size == 1 else VMEM for x in ins],
        out_specs=[VMEM] * len(outs),
        out_shape=[jax.ShapeDtypeStruct(shape, kind) for shape, kind in outs],
        scratch_shapes=list(scratch),
        compiler_params=pltpu.CompilerParams(vmem_limit_bytes=VMEM_LIMIT),
        cost_estimate=pl.CostEstimate(flops=cost, bytes_accessed=10**5, transcendentals=0),
        name=name,
    )(*ins)


def aligned(value, unit):
    return pl.ds(pl.multiple_of(value * unit, unit), unit)


def halves(array):
    high = array.astype(BF16)
    return high, (array - high.astype(F32)).astype(BF16)


def dot(left, right, dims):
    return lax.dot_general(left, right, dims, preferred_element_type=F32)


def product(left, right, dims):
    (high, low), (right_high, right_low) = left, right
    rows = high.shape[0]
    both = dot(jnp.concatenate([high, low], axis=0), right_high, dims)
    return both[:rows] + (both[rows:] + dot(high, right_low, dims))


def pack(out, top, total):
    rows = out.shape[0] // 2
    mean = out * (1.0 / total)
    code = (jnp.max(jnp.abs(mean), axis=0, keepdims=True) * 2.0**27).astype(jnp.int32) + 1
    fixed = jnp.round(mean * (32767.0 / (code.astype(F32) * 2.0**-27))).astype(jnp.int32)
    words = (fixed[:rows] << 16) | (fixed[rows:] & 0xFFFF)
    level = jnp.floor(top + jnp.log2(total))
    rest = (total * jnp.exp2(top - level) * 2.0**28).astype(jnp.int32)
    blank = jnp.zeros((SUB - 3, top.shape[1]), jnp.int32)
    return jnp.concatenate([words, code, level.astype(jnp.int32), rest, blank], axis=0)


def means(packed):
    rows = packed.shape[0] - SUB
    words = packed[:rows]
    fixed = jnp.concatenate([words >> 16, (words << 16) >> 16], axis=0)
    return fixed.astype(F32) * (packed[rows : rows + 1].astype(F32) * (2.0**-27 / 32767.0))


def tail(top, total):
    return jnp.concatenate([top, total, jnp.zeros((SUB - 2, top.shape[1]), F32)], axis=0)


def partial_of(ref):
    rows = ref.shape[0] - SUB
    if ref.dtype == F32:
        return ref[:rows, :], ref[rows : rows + 1, :], ref[rows + 1 : rows + 2, :]
    packed = ref[...]
    rest = packed[rows + 2 : rows + 3].astype(F32) * 2.0**-28
    return means(packed) * rest, packed[rows + 1 : rows + 2].astype(F32), rest


def put_partial(ref, out, top, total):
    if ref.dtype == F32:
        ref[: out.shape[0], :] = out
        ref[out.shape[0] :, :] = tail(top, total)
    else:
        ref[...] = pack(out, top, total)


def partial_shape(rows, lanes, packed):
    if packed and rows % 16 == 0:
        return (rows // 2 + SUB, lanes), jnp.int32
    return (rows + SUB, lanes), F32


def prepare_kernel(window, shard_ref, root_ref, q_hbm, kept_hbm, k_hbm, *refs):
    keep_ref, send_ref, k_ref, q_ref, kept_ref, spots, picked, sems = refs
    slab, dims = k_ref.shape
    kept = kept_ref.shape[1]
    steps = sems.shape[0] - 2
    chunk = slab // steps
    loads = [pltpu.make_async_copy(kept_hbm, kept_ref, sems.at[steps])]
    for i in range(steps):
        part = pl.ds(i * chunk, chunk)
        loads.append(pltpu.make_async_copy(k_hbm.at[part], k_ref.at[part], sems.at[i]))
    loads.append(pltpu.make_async_copy(q_hbm, q_ref, sems.at[steps + 1]))
    for load in loads:
        load.start()
    base = shard_ref[0] * slab
    loads[0].wait()
    positions = kept_ref[...]
    before = jnp.sum((positions < base).astype(jnp.int32))
    start = jnp.minimum(before // 16, (kept - window) // 16)
    local = (positions - base).astype(F32)
    for i in range(0, kept, 128):
        spots[i : i + 128, :] = jnp.broadcast_to(local[:, i : i + 128], (128, 128)).T
    spot = pl.ds(pl.multiple_of(start * 16, 16), window)
    mine = spots[spot, :]
    column = lax.broadcasted_iota(jnp.int32, (window, 128), 1).astype(F32)
    rows = jnp.zeros((window, dims), F32)
    for i in range(steps):
        onehot = jnp.concatenate(
            [jnp.where(mine == column + float(j), 1.0, 0.0).astype(BF16) for j in range(i * chunk, (i + 1) * chunk, 128)],
            axis=1,
        )
        loads[1 + i].wait()
        rows += lax.dot_general(onehot, k_ref[i * chunk : (i + 1) * chunk, :], NN, preferred_element_type=F32)
    picked[...] = jnp.zeros_like(picked)
    picked[spot, :] = rows.astype(BF16)
    loads[-1].wait()
    share, part = q_ref.shape[0] // 4, kept // 4
    is_root = shard_ref[0] == root_ref[0]
    tall = share + part
    for s in range(4):
        out, at = (keep_ref, send_ref)[s % 2], s // 2 * tall
        place = (shard_ref[0] % 4) ^ s
        q = q_ref[aligned(place, share), :]
        out[at : at + share, :] = jnp.where(is_root, q, jnp.zeros_like(q))
        out[at + share : at + tall, :] = picked[aligned(place, part), :]


def sum_kernel(*refs):
    total = refs[0][...]
    for ref in refs[1:-1]:
        total = total + ref[...]
    refs[-1][...] = total


def halve_kernel(a_ref, b_ref, near_ref, far_ref):
    rows = near_ref.shape[0]
    near_ref[...] = a_ref[:rows, :] + b_ref[:rows, :]
    far_ref[...] = a_ref[rows:, :] + b_ref[rows:, :]


def stack_kernel(a_ref, b_ref, out_ref):
    rows = a_ref.shape[0]
    out_ref[:rows, :] = a_ref[...]
    out_ref[rows:, :] = b_ref[...]


def spread(shard, queries, kept, keys, roots, values, attend_to):
    (rows, dims), (slab, _) = queries.shape, keys.shape
    count = kept.shape[1]
    devices = lax.axis_size("ctx")
    quarter = ((rows + count) // 4, dims)
    half = (2 * quarter[0], dims)
    in_hbm = lambda x: pltpu.with_memory_space_constraint(x, pltpu.HBM)
    keep, send, keys = call(
        functools.partial(prepare_kernel, 4 * count // devices + 16),
        (shard, roots, in_hbm(queries), in_hbm(kept), in_hbm(keys)),
        [(half, BF16)] * 2 + [(keys.shape, BF16)],
        scratch=[
            pltpu.VMEM((rows, dims), BF16),
            pltpu.VMEM((1, count), jnp.int32),
            pltpu.VMEM((count, 128), F32),
            pltpu.VMEM((count, dims), BF16),
            pltpu.SemaphoreType.DMA((6,)),
        ],
        name="prepare",
        specs=[SMEM, SMEM, HBM, HBM, HBM],
    )
    near, far = call(halve_kernel, (keep, swap(send, "ctx", 1)), [(quarter, BF16)] * 2, name="halve")
    total = lambda arrays: call(sum_kernel, arrays, [(quarter, BF16)], name="total")[0]
    came = swap(far, "ctx", 2)
    (turned,) = call(turn_kernel, (values,), [((dims + 16, slab), BF16)], 10**7, name="turn")
    came, turned = lax.optimization_barrier((came, turned))
    near = total([near, came])
    step = 4
    while step < devices:
        ways = math.gcd(devices // step, 4)
        near = total([near] + [swap(near, "ctx", t * step) for t in range(1, ways)])
        step *= ways
    far = swap(near, "ctx", 2)
    first = attend_to(near, keys, turned)
    far, first = lax.optimization_barrier((far, first))
    (both,) = call(stack_kernel, (near, far), [(half, BF16)], name="stack")
    other, came = swap(both, "ctx", 1), [swap(first, "ctx", 1)]
    second = attend_to(far, keys, turned)
    other, second = lax.optimization_barrier((other, second))
    came.append(swap(second, "ctx", 3))
    third = attend_to(other, keys, turned, start=quarter[0])
    came.append(swap(third, "ctx", 2))
    other, third = lax.optimization_barrier((other, third))
    return near, far, other, attend_to(other, keys, turned, packed=False), came


def turn_kernel(v_ref, vt_ref):
    dims = v_ref.shape[1]
    vt_ref[:dims, :] = v_ref[...].T
    vt_ref[dims:, :] = jnp.ones((vt_ref.shape[0] - dims, v_ref.shape[0]), BF16)


def attention_kernel(start, block, score_scale, q_ref, k_ref, vt_ref, out_ref):
    dims = k_ref.shape[1]
    lanes = out_ref.shape[1]
    factor = score_scale * math.log2(math.e)
    queries = q_ref[start : start + lanes, :]
    scores = lambda b: dot(k_ref[b : b + block, :], queries, NT)
    slab = k_ref.shape[0]
    ahead, parts = scores(0), []
    for b in range(0, slab, block):
        s = ahead
        if b + block < slab:
            ahead = scores(b + block)
        top = jnp.max(s, axis=0, keepdims=True)
        e = jnp.exp2((s - top) * factor).astype(BF16)
        out = dot(vt_ref[:, b : b + block], e, NN)
        parts.append((out[:dims, :], top * factor, out[dims : dims + 1, :]))
    put_partial(out_ref, *join(*parts))


def attention(lanes, score_scale, piece, keys, turned, start=0, packed=True):
    slab, dims = keys.shape
    return call(
        functools.partial(attention_kernel, start, min(KBLK, slab), score_scale),
        (piece, keys, turned),
        [partial_shape(dims, lanes, packed)],
        10**6,
        name="attention",
    )[0]


def join(*parts):
    top = functools.reduce(jnp.maximum, [part[1] for part in parts])
    scales = [jnp.exp2(part[1] - top) for part in parts]
    total = sum(part[2] * scale for part, scale in zip(parts, scales))
    out = sum(part[0] * scale for part, scale in zip(parts, scales))
    return out, top, total


def merged(*refs):
    return join(*[partial_of(ref) for ref in refs])


def merge_kernel(*refs):
    put_partial(refs[-1], *merged(*refs[:-1]))


def target_rounds(keep, came):
    dims, lanes = keep.shape[0] - SUB, keep.shape[1]
    shape, kind = partial_shape(dims, lanes, True)
    came = yield came
    (mine,) = call(merge_kernel, (keep, *came), [(shape, kind)], name="merge")
    step = 4
    while step < lax.axis_size("ctx"):
        came = yield [swap(mine, "ctx", step)]
        (mine,) = call(merge_kernel, (mine, *came), [(shape, kind)], name="merge")
        step *= 2
    came = yield [swap(mine, "ctx", 2)]
    (both,) = call(stack_kernel, (mine, *came), [((2 * shape[0], lanes), kind)], name="stack")
    came = yield [swap(both, "ctx", 1)]
    return both, *came


def attend_kernel(score_scale, shard_ref, near_ref, far_ref, other_ref, high_ref, low_ref, square_ref, c_all):
    part, rows = c_all.shape[0] // 4, high_ref.shape[1] // 4
    tall = part + rows
    pieces = [(near_ref, 0), (other_ref, 0), (far_ref, 0), (other_ref, tall)]
    places = [(shard_ref[0] % 4) ^ s for s in range(4)]
    for place, (ref, at) in zip(places, pieces):
        c_all[aligned(place, part), :] = ref[at + rows : at + tall, :]
    for place, (ref, at) in zip(places, pieces):
        scores = dot(c_all[...], ref[at : at + rows, :], NT)
        weights = jnp.exp2((scores - jnp.max(scores, axis=0, keepdims=True)) * (score_scale * math.log2(math.e)))
        weights = weights * (1.0 / jnp.sum(weights, axis=0, keepdims=True))
        high_ref[:, aligned(place, rows)], low_ref[:, aligned(place, rows)] = halves(weights)
        square_ref[aligned(place, SUB), :] = jnp.sum((weights * weights).reshape(-1, SUB, rows), axis=0)


def gram_kernel(high_ref, low_ref, square_ref, h_ref, inverse_ref):
    kept = high_ref.shape[0]
    ridge = RIDGE_SHARE * jnp.sum(square_ref[...]) / kept
    row = lax.broadcasted_iota(jnp.int32, (128, kept), 0)
    column = lax.broadcasted_iota(jnp.int32, (128, kept), 1)

    def system(start, rows, columns):
        at = slice(start, start + rows)
        left = jnp.concatenate([high_ref[at, :], low_ref[at, :]], axis=0)
        by_high, by_low = dot(left, high_ref[:columns, :], NT), dot(left, low_ref[:columns, :], NT)
        gram = by_high[:rows] + (by_high[rows:] + by_low[:rows] + by_low[rows:])
        return gram + jnp.where(row[:rows, :columns] + start == column[:rows, :columns], ridge, 0.0)

    def piece(start):
        def fill():
            h_ref[start : start + 128, :] = system(start, 128, kept)

        return fill

    inverse_ref[...] = inverse_beside(system(0, PANEL, PANEL), [piece(i) for i in range(0, kept, 128)])


def invert_block(rows):
    count = len(rows)
    size = count * SUB
    lane = lax.broadcasted_iota(jnp.int32, (SUB, size), 1)
    sub = lax.broadcasted_iota(jnp.int32, (SUB, size), 0)
    spread_lane = lambda array, column: jnp.broadcast_to(array[:, column : column + 1], (SUB, size))
    line = lambda array, row: jnp.broadcast_to(array[row : row + 1, :], (SUB, size))
    def less(old, left, right):
        terms = [x * y for x, y in zip(left, right)]
        while len(terms) > 1:
            terms = [x + y for x, y in zip(terms[::2], terms[1::2])]
        return old - terms[0]

    ahead = []
    for k in range(count):
        base = k * SUB
        inside = (lane >= base) & (lane < base + SUB)
        columns = ahead + [spread_lane(rows[k], base + j) for j in range(len(ahead), SUB)]
        work = jnp.where(inside, jnp.where(lane - base == sub, 1.0, 0.0), rows[k])
        beyond = [spread_lane(rows[k], base + SUB + j) for j in range(2)] if k + 1 < count else []
        full = columns + [work] + beyond
        bare = list(full)
        for j in range(0, SUB, 2):
            first, second = full[j], full[j + 1]
            a, b, c, d = line(bare[j], j), line(bare[j + 1], j), line(bare[j], j + 1), line(bare[j + 1], j + 1)
            inverse = 1.0 / (a * d - b * c)
            for i in range(j + 2, len(full)):
                upper, lower = line(bare[i], j), line(bare[i], j + 1)
                new_upper = (d * upper - b * lower) * inverse
                new_lower = (a * lower - c * upper) * inverse
                bare[i] = full[i] - (first * new_upper + second * new_lower)
                full[i] = jnp.where(sub == j, new_upper, jnp.where(sub == j + 1, new_lower, bare[i]))
        work, beyond = full[SUB], full[SUB + 1 :]
        lines = [line(work, j) for j in range(SUB)]
        updated = list(rows)
        updated[k] = work
        for i in list(range(k + 1, count)) + list(range(k)):
            factors = [spread_lane(rows[i], base + j) for j in range(SUB)]
            if i == k + 1:
                ahead = [
                    less(spread_lane(rows[i], base + SUB + j), factors, [line(array, m) for m in range(SUB)])
                    for j, array in enumerate(beyond)
                ]
            updated[i] = less(jnp.where(inside, 0.0, rows[i]), factors, lines)
        rows = updated
        yield
    return jnp.concatenate(rows, axis=0)


def inverse_beside(block, work=()):
    work = list(work)
    groups = invert_block([block[i : i + SUB, :] for i in range(0, block.shape[0], SUB)])
    while True:
        try:
            next(groups)
        except StopIteration as stop:
            for piece in work:
                piece()
            return stop.value
        if work:
            work.pop(0)()


def sweep_kernel(panel, h_ref, inverse_ref, out_ref, next_ref):
    size = h_ref.shape[0]
    at = slice(panel * PANEL, (panel + 1) * PANEL)
    after = slice(at.stop, at.stop + PANEL)
    wide, after_wide = (slice(x.start // 128 * 128, x.start // 128 * 128 + 128) for x in (at, after))
    offset = at.start - wide.start
    inverse = inverse_ref[...]
    split_inverse = halves(inverse)
    blank = jnp.zeros((PANEL, 1), F32)

    def pad(array):
        zeros = jnp.broadcast_to(blank, array.shape)
        return jnp.concatenate([array if i == offset else zeros for i in range(0, 128, PANEL)], axis=0)

    near = pad(product(split_inverse, halves(h_ref[at, after_wide]), NN))
    block = h_ref[after, after_wide] - product(halves(h_ref[after, wide]), halves(near), NN)
    block = block[:, after.start - after_wide.start :][:, :PANEL]

    turned = product(split_inverse, halves(h_ref[at, :]), NN)
    padded = pad(turned)
    split = halves(padded)
    columns = padded.T
    lane = lax.broadcasted_iota(jnp.int32, (128, 128), 1)
    inside = (lane >= offset) & (lane < offset + PANEL)

    def rows_update(i):
        def piece():
            rows = slice(i, i + 128)
            old = h_ref[rows, :]
            out_ref[rows, :] = old - product(halves(h_ref[rows, wide]), split, NN)
            out_ref[rows, wide] = jnp.where(inside, columns[rows, :], out_ref[rows, wide])
            if i == wide.start:
                out_ref[at, :] = turned
                out_ref[at, at] = -inverse

        return piece

    next_ref[...] = inverse_beside(block, [rows_update(i) for i in range(0, size, 128)])


def fit_kernel(shard_ref, swept_ref, inverse_ref, high_ref, low_ref, own_ref, other_ref, x_ref, err_ref, yt):
    rows, lanes = own_ref.shape[0] // 2, own_ref.shape[1]
    place = shard_ref[0] % 4
    for s, ref in ((1, own_ref), (3, own_ref), (0, other_ref), (2, other_ref)):
        half = s // 2
        yt[:, aligned(place ^ s, lanes)] = means(ref[half * rows : (half + 1) * rows, :])
    target = yt[...]
    attend = high_ref[...], low_ref[...]
    cross = product(halves(target), attend, NT)
    size = swept_ref.shape[0]
    last = slice(size - PANEL, size)
    first = product(halves(jnp.concatenate([cross[:, : last.start], jnp.zeros_like(cross[:, last])], axis=1)), halves(swept_ref[...]), NN)
    rest = product(halves(cross[:, last] - first[:, last]), halves(inverse_ref[...]), NN)
    others = first + product(halves(rest), halves(swept_ref[last, :]), NN)
    fitted = jnp.concatenate([-others[:, : last.start], rest], axis=1)
    x_ref[...] = fitted
    misfit = product(halves(fitted), attend, NN) - target
    error = jnp.sum(misfit * misfit) / jnp.sum(target * target)
    err_ref[...] = jnp.full(err_ref.shape, error, F32)


def flip_kernel(x_ref, out_ref):
    out_ref[...] = x_ref[...].T


def mean_kernel(heads, *refs):
    total = refs[0][:1, :1]
    for ref in refs[1:-1]:
        total = total + ref[:1, :1]
    refs[-1][...] = total / heads


def per_device(queries, keys, values, kept, roots):
    rows, dims = queries.shape[2:]
    slab, count = keys.shape[1], kept.shape[1]
    lanes = rows // 4
    score_scale = 1.0 / math.sqrt(dims)
    shard = lax.axis_index("ctx").astype(jnp.int32).reshape(1)

    attend_to = functools.partial(attention, lanes, score_scale)
    near, far, other, keep, came = spread(shard, queries[0, 0], kept, keys[0], roots, values[0], attend_to)
    rounds = target_rounds(keep, came)
    came = next(rounds)
    ends = None

    def beside(arrays):
        nonlocal came, ends
        if ends is None:
            arrays, came = lax.optimization_barrier((arrays, came))
            try:
                came = rounds.send(came)
            except StopIteration as stop:
                ends = stop.value
        return arrays

    system_shape = ((count, count), F32)
    attend = call(
        functools.partial(attend_kernel, score_scale),
        (shard, near, far, other),
        [((count, rows), BF16)] * 2 + [((4 * SUB, lanes), F32)],
        10**6,
        scratch=[pltpu.VMEM((count, dims), BF16)],
        name="attend",
    )
    attend = beside(attend)
    panels = count // PANEL
    block_shape = ((PANEL, PANEL), F32)
    system, inverse = call(gram_kernel, attend, [system_shape, block_shape], 4 * 10**9, name="gram")
    for panel in range(panels - 1):
        system, inverse = call(
            functools.partial(sweep_kernel, panel),
            (system, inverse),
            [system_shape, block_shape],
            2 * 10**9,
            name="sweep",
        )
        if panel in (0, 2, 4, 6):
            system, inverse = beside((system, inverse))
    while ends is None:
        system = beside(system)

    turned_fit, error = call(
        fit_kernel,
        (shard, system, inverse, *attend[:2], *ends),
        [((dims, count), F32), ((SUB, 128), F32)],
        10**9,
        scratch=[pltpu.VMEM((dims, rows), F32)],
        name="fit",
    )
    heads = lax.axis_size("head")
    errors, step = [error], 1
    while step < heads:
        if len(errors) > 1:
            errors = list(call(sum_kernel, errors, [((SUB, 128), F32)], name="total"))
        errors.append(swap(errors[0], "head", step))
        step *= 2
    (compact,) = call(flip_kernel, (turned_fit,), [((count, dims), F32)], 10**6, name="flip")
    (error,) = call(functools.partial(mean_kernel, heads), errors, [((1, 1), F32)], name="mean")
    return (compact[None], error.reshape(()))


def solution(mesh):
    placed = (
        P("head", "ctx", None, None),
        P("head", "ctx", None),
        P("head", "ctx", None),
        P("head", None),
        P("head"),
    )
    return jax.shard_map(
        per_device,
        mesh=mesh,
        in_specs=placed,
        out_specs=(P("head", None, None), P()),
        check_vma=False,
    )
```

```python
import functools
import math

import jax
import jax.numpy as jnp
from jax import lax
from jax.experimental import pallas as pl
from jax.experimental.pallas import tpu as pltpu
from jax.sharding import PartitionSpec as P

KBLK = 1024
PANEL = 64
SUB = 8
RIDGE_SHARE = 0.01
F32 = jnp.float32
BF16 = jnp.bfloat16
VMEM_LIMIT = 48 * 1024 * 1024
VMEM = pl.BlockSpec(memory_space=pltpu.VMEM)
SMEM = pl.BlockSpec(memory_space=pltpu.SMEM)
HBM = pl.BlockSpec(memory_space=pltpu.HBM)
NT = (((1,), (1,)), ((), ()))
TN = (((0,), (0,)), ((), ()))
NN = (((1,), (0,)), ((), ()))


def swap(array, axis, step):
    size = lax.axis_size(axis)
    return lax.ppermute(array, axis, [(i, i ^ step) for i in range(size)])


def call(kernel, ins, outs, cost=10**5, scratch=(), name=None, specs=None):
    return pl.pallas_call(
        kernel,
        in_specs=specs or [SMEM if x.size == 1 else VMEM for x in ins],
        out_specs=[VMEM] * len(outs),
        out_shape=[jax.ShapeDtypeStruct(shape, kind) for shape, kind in outs],
        scratch_shapes=list(scratch),
        compiler_params=pltpu.CompilerParams(vmem_limit_bytes=VMEM_LIMIT),
        cost_estimate=pl.CostEstimate(flops=cost, bytes_accessed=10**5, transcendentals=0),
        name=name,
    )(*ins)


def aligned(value, unit):
    return pl.ds(pl.multiple_of(value * unit, unit), unit)


def halves(array):
    high = array.astype(BF16)
    return high, (array - high.astype(F32)).astype(BF16)


def dot(left, right, dims):
    return lax.dot_general(left, right, dims, preferred_element_type=F32)


def product(left, right, dims):
    (high, low), (right_high, right_low) = left, right
    rows = high.shape[0]
    both = dot(jnp.concatenate([high, low], axis=0), right_high, dims)
    return both[:rows] + (both[rows:] + dot(high, right_low, dims))


def pack(out, top, total):
    rows = out.shape[0] // 2
    mean = out * (1.0 / total)
    code = (jnp.max(jnp.abs(mean), axis=0, keepdims=True) * 2.0**27).astype(jnp.int32) + 1
    fixed = jnp.round(mean * (32767.0 / (code.astype(F32) * 2.0**-27))).astype(jnp.int32)
    words = (fixed[:rows] << 16) | (fixed[rows:] & 0xFFFF)
    level = jnp.floor(top + jnp.log2(total))
    rest = (total * jnp.exp2(top - level) * 2.0**28).astype(jnp.int32)
    blank = jnp.zeros((SUB - 3, top.shape[1]), jnp.int32)
    return jnp.concatenate([words, code, level.astype(jnp.int32), rest, blank], axis=0)


def means(packed):
    rows = packed.shape[0] - SUB
    words = packed[:rows]
    fixed = jnp.concatenate([words >> 16, (words << 16) >> 16], axis=0)
    return fixed.astype(F32) * (packed[rows : rows + 1].astype(F32) * (2.0**-27 / 32767.0))


def tail(top, total):
    return jnp.concatenate([top, total, jnp.zeros((SUB - 2, top.shape[1]), F32)], axis=0)


def partial_of(ref):
    rows = ref.shape[0] - SUB
    if ref.dtype == F32:
        return ref[:rows, :], ref[rows : rows + 1, :], ref[rows + 1 : rows + 2, :]
    packed = ref[...]
    rest = packed[rows + 2 : rows + 3].astype(F32) * 2.0**-28
    return means(packed) * rest, packed[rows + 1 : rows + 2].astype(F32), rest


def put_partial(ref, out, top, total):
    if ref.dtype == F32:
        ref[: out.shape[0], :] = out
        ref[out.shape[0] :, :] = tail(top, total)
    else:
        ref[...] = pack(out, top, total)


def partial_shape(rows, lanes, packed):
    if packed and rows % 16 == 0:
        return (rows // 2 + SUB, lanes), jnp.int32
    return (rows + SUB, lanes), F32


def prepare_kernel(window, shard_ref, root_ref, q_hbm, kept_hbm, k_hbm, *refs):
    keep_ref, send_ref, k_ref, q_ref, kept_ref, spots, picked, sems = refs
    slab, dims = k_ref.shape
    kept = kept_ref.shape[1]
    steps = sems.shape[0] - 2
    chunk = slab // steps
    loads = [pltpu.make_async_copy(kept_hbm, kept_ref, sems.at[steps])]
    for i in range(steps):
        part = pl.ds(i * chunk, chunk)
        loads.append(pltpu.make_async_copy(k_hbm.at[part], k_ref.at[part], sems.at[i]))
    loads.append(pltpu.make_async_copy(q_hbm, q_ref, sems.at[steps + 1]))
    for load in [loads[0], loads[-1]] + loads[1:-1]:
        load.start()
    base = shard_ref[0] * slab
    loads[0].wait()
    positions = kept_ref[...]
    before = jnp.sum((positions < base).astype(jnp.int32))
    start = jnp.minimum(before // 16, (kept - window) // 16)
    local = (positions - base).astype(F32)
    for i in range(0, kept, 128):
        spots[i : i + 128, :] = jnp.broadcast_to(local[:, i : i + 128], (128, 128)).T
    spot = pl.ds(pl.multiple_of(start * 16, 16), window)
    mine = spots[spot, :]
    column = lax.broadcasted_iota(jnp.int32, (window, 128), 1).astype(F32)
    share, part = q_ref.shape[0] // 4, kept // 4
    tall = share + part
    is_root = shard_ref[0] == root_ref[0]
    targets = [((keep_ref, send_ref)[s % 2], s // 2 * tall, (shard_ref[0] % 4) ^ s) for s in range(4)]
    loads[-1].wait()
    for out, at, place in targets:
        q = q_ref[aligned(place, share), :]
        out[at : at + share, :] = jnp.where(is_root, q, jnp.zeros_like(q))
    rows = jnp.zeros((window, dims), F32)
    for i in range(steps):
        onehot = jnp.concatenate(
            [jnp.where(mine == column + float(j), 1.0, 0.0).astype(BF16) for j in range(i * chunk, (i + 1) * chunk, 128)],
            axis=1,
        )
        loads[1 + i].wait()
        rows += lax.dot_general(onehot, k_ref[i * chunk : (i + 1) * chunk, :], NN, preferred_element_type=F32)
    picked[...] = jnp.zeros_like(picked)
    picked[spot, :] = rows.astype(BF16)
    for out, at, place in targets:
        out[at + share : at + tall, :] = picked[aligned(place, part), :]


def sum_kernel(*refs):
    total = refs[0][...]
    for ref in refs[1:-1]:
        total = total + ref[...]
    refs[-1][...] = total


def halve_kernel(a_ref, b_ref, near_ref, far_ref):
    rows = near_ref.shape[0]
    near_ref[...] = a_ref[:rows, :] + b_ref[:rows, :]
    far_ref[...] = a_ref[rows:, :] + b_ref[rows:, :]


def stack_kernel(a_ref, b_ref, out_ref):
    rows = a_ref.shape[0]
    out_ref[:rows, :] = a_ref[...]
    out_ref[rows:, :] = b_ref[...]


def spread(shard, queries, kept, keys, roots, values, attend_to):
    (rows, dims), (slab, _) = queries.shape, keys.shape
    count = kept.shape[1]
    devices = lax.axis_size("ctx")
    quarter = ((rows + count) // 4, dims)
    half = (2 * quarter[0], dims)
    in_hbm = lambda x: pltpu.with_memory_space_constraint(x, pltpu.HBM)
    keep, send, keys = call(
        functools.partial(prepare_kernel, 4 * count // devices + 16),
        (shard, roots, in_hbm(queries), in_hbm(kept), in_hbm(keys)),
        [(half, BF16)] * 2 + [(keys.shape, BF16)],
        scratch=[
            pltpu.VMEM((rows, dims), BF16),
            pltpu.VMEM((1, count), jnp.int32),
            pltpu.VMEM((count, 128), F32),
            pltpu.VMEM((count, dims), BF16),
            pltpu.SemaphoreType.DMA((6,)),
        ],
        name="prepare",
        specs=[SMEM, SMEM, HBM, HBM, HBM],
    )
    near, far = call(halve_kernel, (keep, swap(send, "ctx", 1)), [(quarter, BF16)] * 2, name="halve")
    total = lambda arrays: call(sum_kernel, arrays, [(quarter, BF16)], name="total")[0]
    came = swap(far, "ctx", 2)
    (turned,) = call(turn_kernel, (values,), [((dims + 16, slab), BF16)], 10**7, name="turn")
    came, turned = lax.optimization_barrier((came, turned))
    near = total([near, came])
    step = 4
    while step < devices:
        ways = math.gcd(devices // step, 4)
        near = total([near] + [swap(near, "ctx", t * step) for t in range(1, ways)])
        step *= ways
    far = swap(near, "ctx", 2)
    first = attend_to(near, keys, turned)
    far, first = lax.optimization_barrier((far, first))
    (both,) = call(stack_kernel, (near, far), [(half, BF16)], name="stack")
    other, came = swap(both, "ctx", 1), [swap(first, "ctx", 1)]
    second = attend_to(far, keys, turned)
    other, second = lax.optimization_barrier((other, second))
    came.append(swap(second, "ctx", 3))
    third = attend_to(other, keys, turned, start=quarter[0])
    came.append(swap(third, "ctx", 2))
    other, third = lax.optimization_barrier((other, third))
    return near, far, other, attend_to(other, keys, turned, packed=False), came


def turn_kernel(v_ref, vt_ref):
    dims = v_ref.shape[1]
    vt_ref[:dims, :] = v_ref[...].T
    vt_ref[dims:, :] = jnp.ones((vt_ref.shape[0] - dims, v_ref.shape[0]), BF16)


def attention_kernel(start, block, score_scale, q_ref, k_ref, vt_ref, out_ref):
    dims = k_ref.shape[1]
    lanes = out_ref.shape[1]
    factor = score_scale * math.log2(math.e)
    queries = q_ref[start : start + lanes, :]
    scores = lambda b: dot(k_ref[b : b + block, :], queries, NT)
    slab = k_ref.shape[0]
    ahead, parts = scores(0), []
    for b in range(0, slab, block):
        s = ahead
        if b + block < slab:
            ahead = scores(b + block)
        top = jnp.max(s, axis=0, keepdims=True)
        e = jnp.exp2((s - top) * factor).astype(BF16)
        out = dot(vt_ref[:, b : b + block], e, NN)
        parts.append((out[:dims, :], top * factor, out[dims : dims + 1, :]))
    put_partial(out_ref, *join(*parts))


def attention(lanes, score_scale, piece, keys, turned, start=0, packed=True):
    slab, dims = keys.shape
    return call(
        functools.partial(attention_kernel, start, min(KBLK, slab), score_scale),
        (piece, keys, turned),
        [partial_shape(dims, lanes, packed)],
        10**6,
        name="attention",
    )[0]


def join(*parts):
    top = functools.reduce(jnp.maximum, [part[1] for part in parts])
    scales = [jnp.exp2(part[1] - top) for part in parts]
    total = sum(part[2] * scale for part, scale in zip(parts, scales))
    out = sum(part[0] * scale for part, scale in zip(parts, scales))
    return out, top, total


def merged(*refs):
    return join(*[partial_of(ref) for ref in refs])


def merge_kernel(*refs):
    put_partial(refs[-1], *merged(*refs[:-1]))


def target_rounds(keep, came):
    dims, lanes = keep.shape[0] - SUB, keep.shape[1]
    shape, kind = partial_shape(dims, lanes, True)
    came = yield came
    (mine,) = call(merge_kernel, (keep, *came), [(shape, kind)], name="merge")
    step = 4
    while step < lax.axis_size("ctx"):
        came = yield [swap(mine, "ctx", step)]
        (mine,) = call(merge_kernel, (mine, *came), [(shape, kind)], name="merge")
        step *= 2
    came = yield [swap(mine, "ctx", 2)]
    (both,) = call(stack_kernel, (mine, *came), [((2 * shape[0], lanes), kind)], name="stack")
    came = yield [swap(both, "ctx", 1)]
    return both, *came


def attend_kernel(score_scale, shard_ref, near_ref, far_ref, other_ref, high_ref, low_ref, square_ref, c_all):
    part, rows = c_all.shape[0] // 4, high_ref.shape[1] // 4
    tall = part + rows
    pieces = [(near_ref, 0), (other_ref, 0), (far_ref, 0), (other_ref, tall)]
    places = [(shard_ref[0] % 4) ^ s for s in range(4)]
    for place, (ref, at) in zip(places, pieces):
        c_all[aligned(place, part), :] = ref[at + rows : at + tall, :]
    for place, (ref, at) in zip(places, pieces):
        scores = dot(c_all[...], ref[at : at + rows, :], NT)
        weights = jnp.exp2((scores - jnp.max(scores, axis=0, keepdims=True)) * (score_scale * math.log2(math.e)))
        weights = weights * (1.0 / jnp.sum(weights, axis=0, keepdims=True))
        high_ref[:, aligned(place, rows)], low_ref[:, aligned(place, rows)] = halves(weights)
        square_ref[aligned(place, SUB), :] = jnp.sum((weights * weights).reshape(-1, SUB, rows), axis=0)


def gram_kernel(high_ref, low_ref, square_ref, h_ref, inverse_ref):
    kept = high_ref.shape[0]
    ridge = RIDGE_SHARE * jnp.sum(square_ref[...]) / kept
    row = lax.broadcasted_iota(jnp.int32, (128, kept), 0)
    column = lax.broadcasted_iota(jnp.int32, (128, kept), 1)

    def system(start, rows, columns):
        at = slice(start, start + rows)
        left = jnp.concatenate([high_ref[at, :], low_ref[at, :]], axis=0)
        by_high, by_low = dot(left, high_ref[:columns, :], NT), dot(left, low_ref[:columns, :], NT)
        gram = by_high[:rows] + (by_high[rows:] + by_low[:rows] + by_low[rows:])
        return gram + jnp.where(row[:rows, :columns] + start == column[:rows, :columns], ridge, 0.0)

    def piece(start):
        def fill():
            h_ref[start : start + 128, :] = system(start, 128, kept)

        return fill

    inverse_ref[...] = inverse_beside(system(0, PANEL, PANEL), [piece(i) for i in range(0, kept, 128)])


def invert_block(rows):
    count = len(rows)
    size = count * SUB
    lane = lax.broadcasted_iota(jnp.int32, (SUB, size), 1)
    sub = lax.broadcasted_iota(jnp.int32, (SUB, size), 0)
    spread_lane = lambda array, column: jnp.broadcast_to(array[:, column : column + 1], (SUB, size))
    line = lambda array, row: jnp.broadcast_to(array[row : row + 1, :], (SUB, size))
    def less(old, left, right):
        terms = [x * y for x, y in zip(left, right)]
        while len(terms) > 1:
            terms = [x + y for x, y in zip(terms[::2], terms[1::2])]
        return old - terms[0]

    ahead = []
    for k in range(count):
        base = k * SUB
        inside = (lane >= base) & (lane < base + SUB)
        columns = ahead + [spread_lane(rows[k], base + j) for j in range(len(ahead), SUB)]
        work = jnp.where(inside, jnp.where(lane - base == sub, 1.0, 0.0), rows[k])
        beyond = [spread_lane(rows[k], base + SUB + j) for j in range(2)] if k + 1 < count else []
        full = columns + [work] + beyond
        bare = list(full)
        for j in range(0, SUB, 2):
            first, second = full[j], full[j + 1]
            a, b, c, d = line(bare[j], j), line(bare[j + 1], j), line(bare[j], j + 1), line(bare[j + 1], j + 1)
            inverse = 1.0 / (a * d - b * c)
            for i in range(j + 2, len(full)):
                upper, lower = line(bare[i], j), line(bare[i], j + 1)
                new_upper = (d * upper - b * lower) * inverse
                new_lower = (a * lower - c * upper) * inverse
                bare[i] = full[i] - (first * new_upper + second * new_lower)
                full[i] = jnp.where(sub == j, new_upper, jnp.where(sub == j + 1, new_lower, bare[i]))
        work, beyond = full[SUB], full[SUB + 1 :]
        lines = [line(work, j) for j in range(SUB)]
        updated = list(rows)
        updated[k] = work
        for i in list(range(k + 1, count)) + list(range(k)):
            factors = [spread_lane(rows[i], base + j) for j in range(SUB)]
            if i == k + 1:
                ahead = [
                    less(spread_lane(rows[i], base + SUB + j), factors, [line(array, m) for m in range(SUB)])
                    for j, array in enumerate(beyond)
                ]
            updated[i] = less(jnp.where(inside, 0.0, rows[i]), factors, lines)
        rows = updated
        yield
    return jnp.concatenate(rows, axis=0)


def inverse_beside(block, work=()):
    work = list(work)
    groups = invert_block([block[i : i + SUB, :] for i in range(0, block.shape[0], SUB)])
    while True:
        try:
            next(groups)
        except StopIteration as stop:
            for piece in work:
                piece()
            return stop.value
        if work:
            work.pop(0)()


def sweep_kernel(panel, h_ref, inverse_ref, out_ref, next_ref, beside=()):
    size = h_ref.shape[0]
    at = slice(panel * PANEL, (panel + 1) * PANEL)
    after = slice(at.stop, at.stop + PANEL)
    wide, after_wide = (slice(x.start // 128 * 128, x.start // 128 * 128 + 128) for x in (at, after))
    offset = at.start - wide.start
    inverse = inverse_ref[...]
    split_inverse = halves(inverse)
    blank = jnp.zeros((PANEL, 1), F32)

    def pad(array):
        zeros = jnp.broadcast_to(blank, array.shape)
        return jnp.concatenate([array if i == offset else zeros for i in range(0, 128, PANEL)], axis=0)

    near = pad(product(split_inverse, halves(h_ref[at, after_wide]), NN))
    block = h_ref[after, after_wide] - product(halves(h_ref[after, wide]), halves(near), NN)
    block = block[:, after.start - after_wide.start :][:, :PANEL]

    turned = product(split_inverse, halves(h_ref[at, :]), NN)
    padded = pad(turned)
    split = halves(padded)
    columns = padded.T
    lane = lax.broadcasted_iota(jnp.int32, (128, 128), 1)
    inside = (lane >= offset) & (lane < offset + PANEL)

    def rows_update(i):
        def piece():
            rows = slice(i, i + 128)
            old = h_ref[rows, :]
            out_ref[rows, :] = old - product(halves(h_ref[rows, wide]), split, NN)
            out_ref[rows, wide] = jnp.where(inside, columns[rows, :], out_ref[rows, wide])
            if i == wide.start:
                out_ref[at, :] = turned
                out_ref[at, at] = -inverse

        return piece

    next_ref[...] = inverse_beside(block, [rows_update(i) for i in range(0, size, 128)] + list(beside))


def last_sweep_kernel(panel, shard_ref, h_ref, inverse_ref, high_ref, low_ref, own_ref, other_ref, out_ref, next_ref, yt_ref, cross_ref):
    def target():
        rows, lanes = own_ref.shape[0] // 2, own_ref.shape[1]
        place = shard_ref[0] % 4
        for s, ref in ((1, own_ref), (3, own_ref), (0, other_ref), (2, other_ref)):
            half = s // 2
            yt_ref[:, aligned(place ^ s, lanes)] = means(ref[half * rows : (half + 1) * rows, :])

    def cross():
        cross_ref[...] = product(halves(yt_ref[...]), (high_ref[...], low_ref[...]), NT)

    sweep_kernel(panel, h_ref, inverse_ref, out_ref, next_ref, (target, cross))


def fit_kernel(swept_ref, inverse_ref, high_ref, low_ref, yt_ref, cross_ref, x_ref, err_ref):
    target, cross = yt_ref[...], cross_ref[...]
    attend = high_ref[...], low_ref[...]
    size = swept_ref.shape[0]
    last = slice(size - PANEL, size)
    first = product(halves(jnp.concatenate([cross[:, : last.start], jnp.zeros_like(cross[:, last])], axis=1)), halves(swept_ref[...]), NN)
    rest = product(halves(cross[:, last] - first[:, last]), halves(inverse_ref[...]), NN)
    others = first + product(halves(rest), halves(swept_ref[last, :]), NN)
    fitted = jnp.concatenate([-others[:, : last.start], rest], axis=1)
    x_ref[...] = fitted
    misfit = product(halves(fitted), attend, NN) - target
    error = jnp.sum(misfit * misfit) / jnp.sum(target * target)
    err_ref[...] = jnp.full(err_ref.shape, error, F32)


def flip_kernel(x_ref, out_ref):
    out_ref[...] = x_ref[...].T


def mean_kernel(heads, *refs):
    total = refs[0][:1, :1]
    for ref in refs[1:-1]:
        total = total + ref[:1, :1]
    refs[-1][...] = total / heads


def per_device(queries, keys, values, kept, roots):
    rows, dims = queries.shape[2:]
    slab, count = keys.shape[1], kept.shape[1]
    lanes = rows // 4
    score_scale = 1.0 / math.sqrt(dims)
    shard = lax.axis_index("ctx").astype(jnp.int32).reshape(1)

    attend_to = functools.partial(attention, lanes, score_scale)
    near, far, other, keep, came = spread(shard, queries[0, 0], kept, keys[0], roots, values[0], attend_to)
    rounds = target_rounds(keep, came)
    came = next(rounds)
    ends = None

    def beside(arrays):
        nonlocal came, ends
        if ends is None:
            arrays, came = lax.optimization_barrier((arrays, came))
            try:
                came = rounds.send(came)
            except StopIteration as stop:
                ends = stop.value
        return arrays

    system_shape = ((count, count), F32)
    attend = call(
        functools.partial(attend_kernel, score_scale),
        (shard, near, far, other),
        [((count, rows), BF16)] * 2 + [((4 * SUB, lanes), F32)],
        10**6,
        scratch=[pltpu.VMEM((count, dims), BF16)],
        name="attend",
    )
    attend = beside(attend)
    panels = count // PANEL
    block_shape = ((PANEL, PANEL), F32)
    system, inverse = call(gram_kernel, attend, [system_shape, block_shape], 4 * 10**9, name="gram")
    for panel in range(panels - 2):
        system, inverse = call(
            functools.partial(sweep_kernel, panel),
            (system, inverse),
            [system_shape, block_shape],
            2 * 10**9,
            name="sweep",
        )
        if panel in (0, 2, 4, 5):
            system, inverse = beside((system, inverse))
    while ends is None:
        system = beside(system)
    system, inverse, target, cross = call(
        functools.partial(last_sweep_kernel, panels - 2),
        (shard, system, inverse, *attend[:2], *ends),
        [system_shape, block_shape, ((dims, rows), F32), ((dims, count), F32)],
        2 * 10**9,
        name="last_sweep",
    )
    turned_fit, error = call(
        fit_kernel,
        (system, inverse, *attend[:2], target, cross),
        [((dims, count), F32), ((SUB, 128), F32)],
        10**9,
        name="fit",
    )
    heads = lax.axis_size("head")
    errors, step = [error], 1
    while step < heads:
        if len(errors) > 1:
            errors = list(call(sum_kernel, errors, [((SUB, 128), F32)], name="total"))
        errors.append(swap(errors[0], "head", step))
        step *= 2
    (compact,) = call(flip_kernel, (turned_fit,), [((count, dims), F32)], 10**6, name="flip")
    (error,) = call(functools.partial(mean_kernel, heads), errors, [((1, 1), F32)], name="mean")
    return (compact[None], error.reshape(()))


def solution(mesh):
    placed = (
        P("head", "ctx", None, None),
        P("head", "ctx", None),
        P("head", "ctx", None),
        P("head", None),
        P("head"),
    )
    return jax.shard_map(
        per_device,
        mesh=mesh,
        in_specs=placed,
        out_specs=(P("head", None, None), P()),
        check_vma=False,
    )
```

```python
import functools
import math

import jax
import jax.numpy as jnp
from jax import lax
from jax.experimental import pallas as pl
from jax.experimental.pallas import tpu as pltpu
from jax.sharding import PartitionSpec as P

KBLK = 1024
PANEL = 64
SUB = 8
RIDGE_SHARE = 0.01
F32 = jnp.float32
BF16 = jnp.bfloat16
VMEM_LIMIT = 48 * 1024 * 1024
VMEM = pl.BlockSpec(memory_space=pltpu.VMEM)
SMEM = pl.BlockSpec(memory_space=pltpu.SMEM)
HBM = pl.BlockSpec(memory_space=pltpu.HBM)
NT = (((1,), (1,)), ((), ()))
TN = (((0,), (0,)), ((), ()))
NN = (((1,), (0,)), ((), ()))


def swap(array, axis, step):
    size = lax.axis_size(axis)
    return lax.ppermute(array, axis, [(i, i ^ step) for i in range(size)])


def call(kernel, ins, outs, cost=10**5, scratch=(), name=None, specs=None):
    return pl.pallas_call(
        kernel,
        in_specs=specs or [SMEM if x.size == 1 else VMEM for x in ins],
        out_specs=[VMEM] * len(outs),
        out_shape=[jax.ShapeDtypeStruct(shape, kind) for shape, kind in outs],
        scratch_shapes=list(scratch),
        compiler_params=pltpu.CompilerParams(vmem_limit_bytes=VMEM_LIMIT),
        cost_estimate=pl.CostEstimate(flops=cost, bytes_accessed=10**5, transcendentals=0),
        name=name,
    )(*ins)


def aligned(value, unit):
    return pl.ds(pl.multiple_of(value * unit, unit), unit)


def halves(array):
    high = array.astype(BF16)
    return high, (array - high.astype(F32)).astype(BF16)


def dot(left, right, dims):
    return lax.dot_general(left, right, dims, preferred_element_type=F32)


def product(left, right, dims):
    (high, low), (right_high, right_low) = left, right
    rows = high.shape[0]
    both = dot(jnp.concatenate([high, low], axis=0), right_high, dims)
    return both[:rows] + (both[rows:] + dot(high, right_low, dims))


def pack(out, top, total):
    rows = out.shape[0] // 2
    mean = out * (1.0 / total)
    code = (jnp.max(jnp.abs(mean), axis=0, keepdims=True) * 2.0**27).astype(jnp.int32) + 1
    fixed = jnp.round(mean * (32767.0 / (code.astype(F32) * 2.0**-27))).astype(jnp.int32)
    words = (fixed[:rows] << 16) | (fixed[rows:] & 0xFFFF)
    level = jnp.floor(top + jnp.log2(total))
    rest = (total * jnp.exp2(top - level) * 2.0**28).astype(jnp.int32)
    blank = jnp.zeros((SUB - 3, top.shape[1]), jnp.int32)
    return jnp.concatenate([words, code, level.astype(jnp.int32), rest, blank], axis=0)


def means(packed):
    rows = packed.shape[0] - SUB
    words = packed[:rows]
    fixed = jnp.concatenate([words >> 16, (words << 16) >> 16], axis=0)
    return fixed.astype(F32) * (packed[rows : rows + 1].astype(F32) * (2.0**-27 / 32767.0))


def tail(top, total):
    return jnp.concatenate([top, total, jnp.zeros((SUB - 2, top.shape[1]), F32)], axis=0)


def partial_of(ref):
    rows = ref.shape[0] - SUB
    if ref.dtype == F32:
        return ref[:rows, :], ref[rows : rows + 1, :], ref[rows + 1 : rows + 2, :]
    packed = ref[...]
    rest = packed[rows + 2 : rows + 3].astype(F32) * 2.0**-28
    return means(packed) * rest, packed[rows + 1 : rows + 2].astype(F32), rest


def put_partial(ref, out, top, total):
    if ref.dtype == F32:
        ref[: out.shape[0], :] = out
        ref[out.shape[0] :, :] = tail(top, total)
    else:
        ref[...] = pack(out, top, total)


def partial_shape(rows, lanes, packed):
    if packed and rows % 16 == 0:
        return (rows // 2 + SUB, lanes), jnp.int32
    return (rows + SUB, lanes), F32


def prepare_kernel(window, shard_ref, root_ref, q_hbm, kept_hbm, k_hbm, *refs):
    keep_ref, send_ref, k_ref, q_ref, kept_ref, spots, picked, sems = refs
    slab, dims = k_ref.shape
    kept = kept_ref.shape[1]
    steps = sems.shape[0] - 2
    chunk = slab // steps
    loads = [pltpu.make_async_copy(kept_hbm, kept_ref, sems.at[steps])]
    for i in range(steps):
        part = pl.ds(i * chunk, chunk)
        loads.append(pltpu.make_async_copy(k_hbm.at[part], k_ref.at[part], sems.at[i]))
    loads.append(pltpu.make_async_copy(q_hbm, q_ref, sems.at[steps + 1]))
    for load in [loads[0], loads[-1]] + loads[1:-1]:
        load.start()
    base = shard_ref[0] * slab
    loads[0].wait()
    positions = kept_ref[...]
    before = jnp.sum((positions < base).astype(jnp.int32))
    start = jnp.minimum(before // 16, (kept - window) // 16)
    local = (positions - base).astype(F32)
    for i in range(0, kept, 128):
        spots[i : i + 128, :] = jnp.broadcast_to(local[:, i : i + 128], (128, 128)).T
    spot = pl.ds(pl.multiple_of(start * 16, 16), window)
    mine = spots[spot, :]
    column = lax.broadcasted_iota(jnp.int32, (window, 128), 1).astype(F32)
    share, part = q_ref.shape[0] // 4, kept // 4
    tall = share + part
    is_root = shard_ref[0] == root_ref[0]
    targets = [((keep_ref, send_ref)[s % 2], s // 2 * tall, (shard_ref[0] % 4) ^ s) for s in range(4)]
    loads[-1].wait()
    for out, at, place in targets:
        q = q_ref[aligned(place, share), :]
        out[at : at + share, :] = jnp.where(is_root, q, jnp.zeros_like(q))
    rows = jnp.zeros((window, dims), F32)
    for i in range(steps):
        onehot = jnp.concatenate(
            [jnp.where(mine == column + float(j), 1.0, 0.0).astype(BF16) for j in range(i * chunk, (i + 1) * chunk, 128)],
            axis=1,
        )
        loads[1 + i].wait()
        rows += lax.dot_general(onehot, k_ref[i * chunk : (i + 1) * chunk, :], NN, preferred_element_type=F32)
    picked[...] = jnp.zeros_like(picked)
    picked[spot, :] = rows.astype(BF16)
    for out, at, place in targets:
        out[at + share : at + tall, :] = picked[aligned(place, part), :]


def sum_kernel(*refs):
    total = refs[0][...]
    for ref in refs[1:-1]:
        total = total + ref[...]
    refs[-1][...] = total


def halve_kernel(a_ref, b_ref, near_ref, far_ref):
    rows = near_ref.shape[0]
    near_ref[...] = a_ref[:rows, :] + b_ref[:rows, :]
    far_ref[...] = a_ref[rows:, :] + b_ref[rows:, :]


def stack_kernel(a_ref, b_ref, out_ref):
    rows = a_ref.shape[0]
    out_ref[:rows, :] = a_ref[...]
    out_ref[rows:, :] = b_ref[...]


def spread(shard, queries, kept, keys, roots, values, attend_to):
    (rows, dims), (slab, _) = queries.shape, keys.shape
    count = kept.shape[1]
    devices = lax.axis_size("ctx")
    quarter = ((rows + count) // 4, dims)
    half = (2 * quarter[0], dims)
    in_hbm = lambda x: pltpu.with_memory_space_constraint(x, pltpu.HBM)
    keep, send, keys = call(
        functools.partial(prepare_kernel, 4 * count // devices + 16),
        (shard, roots, in_hbm(queries), in_hbm(kept), in_hbm(keys)),
        [(half, BF16)] * 2 + [(keys.shape, BF16)],
        scratch=[
            pltpu.VMEM((rows, dims), BF16),
            pltpu.VMEM((1, count), jnp.int32),
            pltpu.VMEM((count, 128), F32),
            pltpu.VMEM((count, dims), BF16),
            pltpu.SemaphoreType.DMA((6,)),
        ],
        name="prepare",
        specs=[SMEM, SMEM, HBM, HBM, HBM],
    )
    near, far = call(halve_kernel, (keep, swap(send, "ctx", 1)), [(quarter, BF16)] * 2, name="halve")
    total = lambda arrays: call(sum_kernel, arrays, [(quarter, BF16)], name="total")[0]
    came = swap(far, "ctx", 2)
    (turned,) = call(turn_kernel, (values,), [((dims + 16, slab), BF16)], 10**7, name="turn")
    came, turned = lax.optimization_barrier((came, turned))
    near = total([near, came])
    step = 4
    while step < devices:
        ways = math.gcd(devices // step, 4)
        near = total([near] + [swap(near, "ctx", t * step) for t in range(1, ways)])
        step *= ways
    far = swap(near, "ctx", 2)
    first = attend_to(near, keys, turned)
    far, first = lax.optimization_barrier((far, first))
    (both,) = call(stack_kernel, (near, far), [(half, BF16)], name="stack")
    other, came = swap(both, "ctx", 1), [swap(first, "ctx", 1)]
    second = attend_to(far, keys, turned)
    other, second = lax.optimization_barrier((other, second))
    came.append(swap(second, "ctx", 3))
    third = attend_to(other, keys, turned, start=quarter[0])
    came.append(swap(third, "ctx", 2))
    other, third = lax.optimization_barrier((other, third))
    return near, far, other, attend_to(other, keys, turned, packed=False), came


def turn_kernel(v_ref, vt_ref):
    dims = v_ref.shape[1]
    vt_ref[:dims, :] = v_ref[...].T
    vt_ref[dims:, :] = jnp.ones((vt_ref.shape[0] - dims, v_ref.shape[0]), BF16)


def attention_kernel(start, block, score_scale, q_ref, k_ref, vt_ref, out_ref):
    dims = k_ref.shape[1]
    lanes = out_ref.shape[1]
    factor = score_scale * math.log2(math.e)
    queries = q_ref[start : start + lanes, :]
    scores = lambda b: dot(k_ref[b : b + block, :], queries, NT)
    slab = k_ref.shape[0]
    ahead, parts = scores(0), []
    for b in range(0, slab, block):
        s = ahead
        if b + block < slab:
            ahead = scores(b + block)
        top = jnp.max(s, axis=0, keepdims=True)
        e = jnp.exp2((s - top) * factor).astype(BF16)
        out = dot(vt_ref[:, b : b + block], e, NN)
        parts.append((out[:dims, :], top * factor, out[dims : dims + 1, :]))
    put_partial(out_ref, *join(*parts))


def attention(lanes, score_scale, piece, keys, turned, start=0, packed=True):
    slab, dims = keys.shape
    return call(
        functools.partial(attention_kernel, start, min(KBLK, slab), score_scale),
        (piece, keys, turned),
        [partial_shape(dims, lanes, packed)],
        10**6,
        name="attention",
    )[0]


def join(*parts):
    top = functools.reduce(jnp.maximum, [part[1] for part in parts])
    scales = [jnp.exp2(part[1] - top) for part in parts]
    total = sum(part[2] * scale for part, scale in zip(parts, scales))
    out = sum(part[0] * scale for part, scale in zip(parts, scales))
    return out, top, total


def merged(*refs):
    return join(*[partial_of(ref) for ref in refs])


def merge_kernel(*refs):
    put_partial(refs[-1], *merged(*refs[:-1]))


def target_rounds(keep, came):
    dims, lanes = keep.shape[0] - SUB, keep.shape[1]
    shape, kind = partial_shape(dims, lanes, True)
    came = yield came
    (mine,) = call(merge_kernel, (keep, *came), [(shape, kind)], name="merge")
    step = 4
    while step < lax.axis_size("ctx"):
        came = yield [swap(mine, "ctx", step)]
        (mine,) = call(merge_kernel, (mine, *came), [(shape, kind)], name="merge")
        step *= 2
    came = yield [swap(mine, "ctx", 2)]
    (both,) = call(stack_kernel, (mine, *came), [((2 * shape[0], lanes), kind)], name="stack")
    came = yield [swap(both, "ctx", 1)]
    return both, *came


def attend_kernel(score_scale, shard_ref, near_ref, far_ref, other_ref, high_ref, low_ref, square_ref, c_all):
    part, rows = c_all.shape[0] // 4, high_ref.shape[1] // 4
    tall = part + rows
    pieces = [(near_ref, 0), (other_ref, 0), (far_ref, 0), (other_ref, tall)]
    places = [(shard_ref[0] % 4) ^ s for s in range(4)]
    for place, (ref, at) in zip(places, pieces):
        c_all[aligned(place, part), :] = ref[at + rows : at + tall, :]
    for place, (ref, at) in zip(places, pieces):
        scores = dot(c_all[...], ref[at : at + rows, :], NT)
        weights = jnp.exp2((scores - jnp.max(scores, axis=0, keepdims=True)) * (score_scale * math.log2(math.e)))
        weights = weights * (1.0 / jnp.sum(weights, axis=0, keepdims=True))
        high_ref[:, aligned(place, rows)], low_ref[:, aligned(place, rows)] = halves(weights)
        square_ref[aligned(place, SUB), :] = jnp.sum((weights * weights).reshape(-1, SUB, rows), axis=0)


def gram_kernel(high_ref, low_ref, square_ref, h_ref, inverse_ref):
    kept = high_ref.shape[0]
    ridge = RIDGE_SHARE * jnp.sum(square_ref[...]) / kept
    row = lax.broadcasted_iota(jnp.int32, (128, kept), 0)
    column = lax.broadcasted_iota(jnp.int32, (128, kept), 1)

    def system(start, rows, columns):
        at = slice(start, start + rows)
        left = jnp.concatenate([high_ref[at, :], low_ref[at, :]], axis=0)
        by_high, by_low = dot(left, high_ref[:columns, :], NT), dot(left, low_ref[:columns, :], NT)
        gram = by_high[:rows] + (by_high[rows:] + by_low[:rows] + by_low[rows:])
        return gram + jnp.where(row[:rows, :columns] + start == column[:rows, :columns], ridge, 0.0)

    def piece(start):
        def fill():
            h_ref[start : start + 128, :] = system(start, 128, kept)

        return fill

    inverse_ref[...] = inverse_beside(system(0, PANEL, PANEL), [piece(i) for i in range(0, kept, 128)])


def invert_block(rows):
    count = len(rows)
    size = count * SUB
    lane = lax.broadcasted_iota(jnp.int32, (SUB, size), 1)
    sub = lax.broadcasted_iota(jnp.int32, (SUB, size), 0)
    spread_lane = lambda array, column: jnp.broadcast_to(array[:, column : column + 1], (SUB, size))
    line = lambda array, row: jnp.broadcast_to(array[row : row + 1, :], (SUB, size))
    def less(old, left, right):
        terms = [x * y for x, y in zip(left, right)]
        while len(terms) > 1:
            terms = [x + y for x, y in zip(terms[::2], terms[1::2])]
        return old - terms[0]

    for k in range(count):
        base = k * SUB
        inside = (lane >= base) & (lane < base + SUB)
        columns = [spread_lane(rows[k], base + j) for j in range(SUB)]
        work = jnp.where(inside, jnp.where(lane - base == sub, 1.0, 0.0), rows[k])
        full = columns + [work]
        bare = list(full)
        for j in range(0, SUB, 2):
            first, second = full[j], full[j + 1]
            a, b, c, d = line(bare[j], j), line(bare[j + 1], j), line(bare[j], j + 1), line(bare[j + 1], j + 1)
            inverse = 1.0 / (a * d - b * c)
            for i in range(j + 2, len(full)):
                upper, lower = line(bare[i], j), line(bare[i], j + 1)
                new_upper = (d * upper - b * lower) * inverse
                new_lower = (a * lower - c * upper) * inverse
                bare[i] = full[i] - (first * new_upper + second * new_lower)
                full[i] = jnp.where(sub == j, new_upper, jnp.where(sub == j + 1, new_lower, bare[i]))
        work = full[SUB]
        lines = [line(work, j) for j in range(SUB)]
        updated = list(rows)
        updated[k] = work
        for i in list(range(k + 1, count)) + list(range(k)):
            factors = [spread_lane(rows[i], base + j) for j in range(SUB)]
            updated[i] = less(jnp.where(inside, 0.0, rows[i]), factors, lines)
        rows = updated
        yield
    return jnp.concatenate(rows, axis=0)


def inverse_beside(block, work=()):
    work = list(work)
    groups = invert_block([block[i : i + SUB, :] for i in range(0, block.shape[0], SUB)])
    while True:
        try:
            next(groups)
        except StopIteration as stop:
            for piece in work:
                piece()
            return stop.value
        if work:
            work.pop(0)()


def sweep_kernel(panel, h_ref, inverse_ref, out_ref, next_ref, beside=()):
    size = h_ref.shape[0]
    at = slice(panel * PANEL, (panel + 1) * PANEL)
    after = slice(at.stop, at.stop + PANEL)
    wide, after_wide = (slice(x.start // 128 * 128, x.start // 128 * 128 + 128) for x in (at, after))
    offset = at.start - wide.start
    inverse = inverse_ref[...]
    split_inverse = halves(inverse)
    blank = jnp.zeros((PANEL, 1), F32)

    def pad(array):
        zeros = jnp.broadcast_to(blank, array.shape)
        return jnp.concatenate([array if i == offset else zeros for i in range(0, 128, PANEL)], axis=0)

    near = pad(product(split_inverse, halves(h_ref[at, after_wide]), NN))
    block = h_ref[after, after_wide] - product(halves(h_ref[after, wide]), halves(near), NN)
    block = block[:, after.start - after_wide.start :][:, :PANEL]

    turned = product(split_inverse, halves(h_ref[at, :]), NN)
    padded = pad(turned)
    split = halves(padded)
    columns = padded.T
    lane = lax.broadcasted_iota(jnp.int32, (128, 128), 1)
    inside = (lane >= offset) & (lane < offset + PANEL)

    def rows_update(i):
        def piece():
            rows = slice(i, i + 128)
            old = h_ref[rows, :]
            out_ref[rows, :] = old - product(halves(h_ref[rows, wide]), split, NN)
            out_ref[rows, wide] = jnp.where(inside, columns[rows, :], out_ref[rows, wide])
            if i == wide.start:
                out_ref[at, :] = turned
                out_ref[at, at] = -inverse

        return piece

    next_ref[...] = inverse_beside(block, [rows_update(i) for i in range(0, size, 128)] + list(beside))


def last_sweep_kernel(panel, shard_ref, h_ref, inverse_ref, high_ref, low_ref, own_ref, other_ref, out_ref, next_ref, yt_ref, cross_ref):
    def target():
        rows, lanes = own_ref.shape[0] // 2, own_ref.shape[1]
        place = shard_ref[0] % 4
        for s, ref in ((1, own_ref), (3, own_ref), (0, other_ref), (2, other_ref)):
            half = s // 2
            yt_ref[:, aligned(place ^ s, lanes)] = means(ref[half * rows : (half + 1) * rows, :])

    def cross():
        cross_ref[...] = product(halves(yt_ref[...]), (high_ref[...], low_ref[...]), NT)

    sweep_kernel(panel, h_ref, inverse_ref, out_ref, next_ref, (target, cross))


def fit_kernel(swept_ref, inverse_ref, high_ref, low_ref, yt_ref, cross_ref, x_ref, err_ref):
    target, cross = yt_ref[...], cross_ref[...]
    attend = high_ref[...], low_ref[...]
    size = swept_ref.shape[0]
    last = slice(size - PANEL, size)
    first = product(halves(jnp.concatenate([cross[:, : last.start], jnp.zeros_like(cross[:, last])], axis=1)), halves(swept_ref[...]), NN)
    rest = product(halves(cross[:, last] - first[:, last]), halves(inverse_ref[...]), NN)
    others = first + product(halves(rest), halves(swept_ref[last, :]), NN)
    fitted = jnp.concatenate([-others[:, : last.start], rest], axis=1)
    x_ref[...] = fitted
    misfit = product(halves(fitted), attend, NN) - target
    error = jnp.sum(misfit * misfit) / jnp.sum(target * target)
    err_ref[...] = jnp.full(err_ref.shape, error, F32)


def flip_kernel(x_ref, out_ref):
    out_ref[...] = x_ref[...].T


def mean_kernel(heads, *refs):
    total = refs[0][:1, :1]
    for ref in refs[1:-1]:
        total = total + ref[:1, :1]
    refs[-1][...] = total / heads


def per_device(queries, keys, values, kept, roots):
    rows, dims = queries.shape[2:]
    slab, count = keys.shape[1], kept.shape[1]
    lanes = rows // 4
    score_scale = 1.0 / math.sqrt(dims)
    shard = lax.axis_index("ctx").astype(jnp.int32).reshape(1)

    attend_to = functools.partial(attention, lanes, score_scale)
    near, far, other, keep, came = spread(shard, queries[0, 0], kept, keys[0], roots, values[0], attend_to)
    rounds = target_rounds(keep, came)
    came = next(rounds)
    ends = None

    def beside(arrays):
        nonlocal came, ends
        if ends is None:
            arrays, came = lax.optimization_barrier((arrays, came))
            try:
                came = rounds.send(came)
            except StopIteration as stop:
                ends = stop.value
        return arrays

    system_shape = ((count, count), F32)
    attend = call(
        functools.partial(attend_kernel, score_scale),
        (shard, near, far, other),
        [((count, rows), BF16)] * 2 + [((4 * SUB, lanes), F32)],
        10**6,
        scratch=[pltpu.VMEM((count, dims), BF16)],
        name="attend",
    )
    attend = beside(attend)
    panels = count // PANEL
    block_shape = ((PANEL, PANEL), F32)
    system, inverse = call(gram_kernel, attend, [system_shape, block_shape], 4 * 10**9, name="gram")
    for panel in range(panels - 2):
        system, inverse = call(
            functools.partial(sweep_kernel, panel),
            (system, inverse),
            [system_shape, block_shape],
            2 * 10**9,
            name="sweep",
        )
        if panel in (0, 2, 4, 5):
            system, inverse = beside((system, inverse))
    while ends is None:
        system = beside(system)
    system, inverse, target, cross = call(
        functools.partial(last_sweep_kernel, panels - 2),
        (shard, system, inverse, *attend[:2], *ends),
        [system_shape, block_shape, ((dims, rows), F32), ((dims, count), F32)],
        2 * 10**9,
        name="last_sweep",
    )
    turned_fit, error = call(
        fit_kernel,
        (system, inverse, *attend[:2], target, cross),
        [((dims, count), F32), ((SUB, 128), F32)],
        10**9,
        name="fit",
    )
    heads = lax.axis_size("head")
    errors, step = [error], 1
    while step < heads:
        if len(errors) > 1:
            errors = list(call(sum_kernel, errors, [((SUB, 128), F32)], name="total"))
        errors.append(swap(errors[0], "head", step))
        step *= 2
    (compact,) = call(flip_kernel, (turned_fit,), [((count, dims), F32)], 10**6, name="flip")
    (error,) = call(functools.partial(mean_kernel, heads), errors, [((1, 1), F32)], name="mean")
    return (compact[None], error.reshape(()))


def solution(mesh):
    placed = (
        P("head", "ctx", None, None),
        P("head", "ctx", None),
        P("head", "ctx", None),
        P("head", None),
        P("head"),
    )
    return jax.shard_map(
        per_device,
        mesh=mesh,
        in_specs=placed,
        out_specs=(P("head", None, None), P()),
        check_vma=False,
    )
```

```python
import functools
import math

import jax
import jax.numpy as jnp
from jax import lax
from jax.experimental import pallas as pl
from jax.experimental.pallas import tpu as pltpu
from jax.sharding import PartitionSpec as P

KBLK = 1024
PANEL = 64
SUB = 8
RIDGE_SHARE = 0.01
F32 = jnp.float32
BF16 = jnp.bfloat16
VMEM_LIMIT = 48 * 1024 * 1024
VMEM = pl.BlockSpec(memory_space=pltpu.VMEM)
SMEM = pl.BlockSpec(memory_space=pltpu.SMEM)
HBM = pl.BlockSpec(memory_space=pltpu.HBM)
NT = (((1,), (1,)), ((), ()))
TN = (((0,), (0,)), ((), ()))
NN = (((1,), (0,)), ((), ()))


def swap(array, axis, step):
    size = lax.axis_size(axis)
    return lax.ppermute(array, axis, [(i, i ^ step) for i in range(size)])


def call(kernel, ins, outs, cost=10**5, scratch=(), name=None, specs=None):
    return pl.pallas_call(
        kernel,
        in_specs=specs or [SMEM if x.size == 1 else VMEM for x in ins],
        out_specs=[VMEM] * len(outs),
        out_shape=[jax.ShapeDtypeStruct(shape, kind) for shape, kind in outs],
        scratch_shapes=list(scratch),
        compiler_params=pltpu.CompilerParams(vmem_limit_bytes=VMEM_LIMIT),
        cost_estimate=pl.CostEstimate(flops=cost, bytes_accessed=10**5, transcendentals=0),
        name=name,
    )(*ins)


def aligned(value, unit):
    return pl.ds(pl.multiple_of(value * unit, unit), unit)


def halves(array):
    high = array.astype(BF16)
    return high, (array - high.astype(F32)).astype(BF16)


def dot(left, right, dims):
    return lax.dot_general(left, right, dims, preferred_element_type=F32)


def product(left, right, dims):
    (high, low), (right_high, right_low) = left, right
    rows = high.shape[0]
    both = dot(jnp.concatenate([high, low], axis=0), right_high, dims)
    return both[:rows] + (both[rows:] + dot(high, right_low, dims))


def pack(out, top, total):
    rows = out.shape[0] // 2
    mean = out * (1.0 / total)
    code = (jnp.max(jnp.abs(mean), axis=0, keepdims=True) * 2.0**27).astype(jnp.int32) + 1
    fixed = jnp.round(mean * (32767.0 / (code.astype(F32) * 2.0**-27))).astype(jnp.int32)
    words = (fixed[:rows] << 16) | (fixed[rows:] & 0xFFFF)
    level = jnp.floor(top + jnp.log2(total))
    rest = (total * jnp.exp2(top - level) * 2.0**28).astype(jnp.int32)
    blank = jnp.zeros((SUB - 3, top.shape[1]), jnp.int32)
    return jnp.concatenate([words, code, level.astype(jnp.int32), rest, blank], axis=0)


def means(packed):
    rows = packed.shape[0] - SUB
    words = packed[:rows]
    fixed = jnp.concatenate([words >> 16, (words << 16) >> 16], axis=0)
    return fixed.astype(F32) * (packed[rows : rows + 1].astype(F32) * (2.0**-27 / 32767.0))


def tail(top, total):
    return jnp.concatenate([top, total, jnp.zeros((SUB - 2, top.shape[1]), F32)], axis=0)


def partial_of(ref):
    rows = ref.shape[0] - SUB
    if ref.dtype == F32:
        return ref[:rows, :], ref[rows : rows + 1, :], ref[rows + 1 : rows + 2, :]
    packed = ref[...]
    rest = packed[rows + 2 : rows + 3].astype(F32) * 2.0**-28
    return means(packed) * rest, packed[rows + 1 : rows + 2].astype(F32), rest


def put_partial(ref, out, top, total):
    if ref.dtype == F32:
        ref[: out.shape[0], :] = out
        ref[out.shape[0] :, :] = tail(top, total)
    else:
        ref[...] = pack(out, top, total)


def partial_shape(rows, lanes, packed):
    if packed and rows % 16 == 0:
        return (rows // 2 + SUB, lanes), jnp.int32
    return (rows + SUB, lanes), F32


def prepare_kernel(window, shard_ref, root_ref, q_hbm, kept_hbm, k_hbm, *refs):
    keep_ref, send_ref, k_ref, q_ref, kept_ref, spots, picked, sems = refs
    slab, dims = k_ref.shape
    kept = kept_ref.shape[1]
    steps = sems.shape[0] - 2
    chunk = slab // steps
    loads = [pltpu.make_async_copy(kept_hbm, kept_ref, sems.at[steps])]
    for i in range(steps):
        part = pl.ds(i * chunk, chunk)
        loads.append(pltpu.make_async_copy(k_hbm.at[part], k_ref.at[part], sems.at[i]))
    loads.append(pltpu.make_async_copy(q_hbm, q_ref, sems.at[steps + 1]))
    for load in [loads[0], loads[-1]] + loads[1:-1]:
        load.start()
    base = shard_ref[0] * slab
    loads[0].wait()
    positions = kept_ref[...]
    before = jnp.sum((positions < base).astype(jnp.int32))
    start = jnp.minimum(before // 16, (kept - window) // 16)
    local = (positions - base).astype(F32)
    for i in range(0, kept, 128):
        spots[i : i + 128, :] = jnp.broadcast_to(local[:, i : i + 128], (128, 128)).T
    spot = pl.ds(pl.multiple_of(start * 16, 16), window)
    mine = spots[spot, :]
    column = lax.broadcasted_iota(jnp.int32, (window, 128), 1).astype(F32)
    share, part = q_ref.shape[0] // 4, kept // 4
    tall = share + part
    is_root = shard_ref[0] == root_ref[0]
    targets = [((keep_ref, send_ref)[s % 2], s // 2 * tall, (shard_ref[0] % 4) ^ s) for s in range(4)]
    loads[-1].wait()
    for out, at, place in targets:
        q = q_ref[aligned(place, share), :]
        out[at : at + share, :] = jnp.where(is_root, q, jnp.zeros_like(q))
    rows = jnp.zeros((window, dims), F32)
    for i in range(steps):
        onehot = jnp.concatenate(
            [jnp.where(mine == column + float(j), 1.0, 0.0).astype(BF16) for j in range(i * chunk, (i + 1) * chunk, 128)],
            axis=1,
        )
        loads[1 + i].wait()
        rows += lax.dot_general(onehot, k_ref[i * chunk : (i + 1) * chunk, :], NN, preferred_element_type=F32)
    picked[...] = jnp.zeros_like(picked)
    picked[spot, :] = rows.astype(BF16)
    for out, at, place in targets:
        out[at + share : at + tall, :] = picked[aligned(place, part), :]


def sum_kernel(*refs):
    total = refs[0][...]
    for ref in refs[1:-1]:
        total = total + ref[...]
    refs[-1][...] = total


def halve_kernel(a_ref, b_ref, near_ref, far_ref):
    rows = near_ref.shape[0]
    near_ref[...] = a_ref[:rows, :] + b_ref[:rows, :]
    far_ref[...] = a_ref[rows:, :] + b_ref[rows:, :]


def stack_kernel(a_ref, b_ref, out_ref):
    rows = a_ref.shape[0]
    out_ref[:rows, :] = a_ref[...]
    out_ref[rows:, :] = b_ref[...]


def spread(shard, queries, kept, keys, roots, values, attend_to):
    (rows, dims), (slab, _) = queries.shape, keys.shape
    count = kept.shape[1]
    devices = lax.axis_size("ctx")
    quarter = ((rows + count) // 4, dims)
    half = (2 * quarter[0], dims)
    in_hbm = lambda x: pltpu.with_memory_space_constraint(x, pltpu.HBM)
    keep, send, keys = call(
        functools.partial(prepare_kernel, 4 * count // devices + 16),
        (shard, roots, in_hbm(queries), in_hbm(kept), in_hbm(keys)),
        [(half, BF16)] * 2 + [(keys.shape, BF16)],
        scratch=[
            pltpu.VMEM((rows, dims), BF16),
            pltpu.VMEM((1, count), jnp.int32),
            pltpu.VMEM((count, 128), F32),
            pltpu.VMEM((count, dims), BF16),
            pltpu.SemaphoreType.DMA((6,)),
        ],
        name="prepare",
        specs=[SMEM, SMEM, HBM, HBM, HBM],
    )
    near, far = call(halve_kernel, (keep, swap(send, "ctx", 1)), [(quarter, BF16)] * 2, name="halve")
    total = lambda arrays: call(sum_kernel, arrays, [(quarter, BF16)], name="total")[0]
    came = swap(far, "ctx", 2)
    (turned,) = call(turn_kernel, (values,), [((dims + 16, slab), BF16)], 10**7, name="turn")
    came, turned = lax.optimization_barrier((came, turned))
    near = total([near, came])
    step = 4
    while step < devices:
        ways = math.gcd(devices // step, 4)
        near = total([near] + [swap(near, "ctx", t * step) for t in range(1, ways)])
        step *= ways
    far = swap(near, "ctx", 2)
    first = attend_to(near, keys, turned)
    far, first = lax.optimization_barrier((far, first))
    (both,) = call(stack_kernel, (near, far), [(half, BF16)], name="stack")
    other, came = swap(both, "ctx", 1), [swap(first, "ctx", 1)]
    second = attend_to(far, keys, turned)
    other, second = lax.optimization_barrier((other, second))
    came.append(swap(second, "ctx", 3))
    third = attend_to(other, keys, turned, start=quarter[0])
    came.append(swap(third, "ctx", 2))
    other, third = lax.optimization_barrier((other, third))
    return near, far, other, attend_to(other, keys, turned, packed=False), came


def turn_kernel(v_ref, vt_ref):
    dims = v_ref.shape[1]
    vt_ref[:dims, :] = v_ref[...].T
    vt_ref[dims:, :] = jnp.ones((vt_ref.shape[0] - dims, v_ref.shape[0]), BF16)


def attention_kernel(start, block, score_scale, q_ref, k_ref, vt_ref, out_ref):
    dims = k_ref.shape[1]
    lanes = out_ref.shape[1]
    factor = score_scale * math.log2(math.e)
    queries = q_ref[start : start + lanes, :]
    scores = lambda b: dot(k_ref[b : b + block, :], queries, NT)
    slab = k_ref.shape[0]
    ahead, parts = scores(0), []
    for b in range(0, slab, block):
        s = ahead
        if b + block < slab:
            ahead = scores(b + block)
        top = jnp.max(s, axis=0, keepdims=True)
        e = jnp.exp2((s - top) * factor).astype(BF16)
        out = dot(vt_ref[:, b : b + block], e, NN)
        parts.append((out[:dims, :], top * factor, out[dims : dims + 1, :]))
    put_partial(out_ref, *join(*parts))


def attention(lanes, score_scale, piece, keys, turned, start=0, packed=True):
    slab, dims = keys.shape
    return call(
        functools.partial(attention_kernel, start, min(KBLK, slab), score_scale),
        (piece, keys, turned),
        [partial_shape(dims, lanes, packed)],
        10**6,
        name="attention",
    )[0]


def join(*parts):
    top = functools.reduce(jnp.maximum, [part[1] for part in parts])
    scales = [jnp.exp2(part[1] - top) for part in parts]
    total = sum(part[2] * scale for part, scale in zip(parts, scales))
    out = sum(part[0] * scale for part, scale in zip(parts, scales))
    return out, top, total


def merged(*refs):
    return join(*[partial_of(ref) for ref in refs])


def merge_kernel(*refs):
    put_partial(refs[-1], *merged(*refs[:-1]))


def target_rounds(keep, came):
    dims, lanes = keep.shape[0] - SUB, keep.shape[1]
    shape, kind = partial_shape(dims, lanes, True)
    came = yield came
    (mine,) = call(merge_kernel, (keep, *came), [(shape, kind)], name="merge")
    step = 4
    while step < lax.axis_size("ctx"):
        came = yield [swap(mine, "ctx", step)]
        (mine,) = call(merge_kernel, (mine, *came), [(shape, kind)], name="merge")
        step *= 2
    came = yield [swap(mine, "ctx", 2)]
    (both,) = call(stack_kernel, (mine, *came), [((2 * shape[0], lanes), kind)], name="stack")
    came = yield [swap(both, "ctx", 1)]
    return both, *came


def attend_kernel(score_scale, shard_ref, near_ref, far_ref, other_ref, high_ref, low_ref, square_ref, c_all):
    part, rows = c_all.shape[0] // 4, high_ref.shape[1] // 4
    tall = part + rows
    pieces = [(near_ref, 0), (other_ref, 0), (far_ref, 0), (other_ref, tall)]
    places = [(shard_ref[0] % 4) ^ s for s in range(4)]
    for place, (ref, at) in zip(places, pieces):
        c_all[aligned(place, part), :] = ref[at + rows : at + tall, :]
    for place, (ref, at) in zip(places, pieces):
        scores = dot(c_all[...], ref[at : at + rows, :], NT)
        weights = jnp.exp2((scores - jnp.max(scores, axis=0, keepdims=True)) * (score_scale * math.log2(math.e)))
        weights = weights * (1.0 / jnp.sum(weights, axis=0, keepdims=True))
        high_ref[:, aligned(place, rows)], low_ref[:, aligned(place, rows)] = halves(weights)
        square_ref[aligned(place, SUB), :] = jnp.sum((weights * weights).reshape(-1, SUB, rows), axis=0)


def gram_kernel(high_ref, low_ref, square_ref, h_ref, inverse_ref):
    kept = high_ref.shape[0]
    ridge = RIDGE_SHARE * jnp.sum(square_ref[...]) / kept
    row = lax.broadcasted_iota(jnp.int32, (128, kept), 0)
    column = lax.broadcasted_iota(jnp.int32, (128, kept), 1)

    def system(start, rows, columns):
        at = slice(start, start + rows)
        left = jnp.concatenate([high_ref[at, :], low_ref[at, :]], axis=0)
        by_high, by_low = dot(left, high_ref[:columns, :], NT), dot(left, low_ref[:columns, :], NT)
        gram = by_high[:rows] + (by_high[rows:] + by_low[:rows] + by_low[rows:])
        return gram + jnp.where(row[:rows, :columns] + start == column[:rows, :columns], ridge, 0.0)

    def piece(start):
        def fill():
            h_ref[start : start + 128, :] = system(start, 128, kept)

        return fill

    inverse_ref[...] = inverse_beside(system(0, PANEL, PANEL), [piece(i) for i in range(0, kept, 128)])


def invert_block(rows):
    count = len(rows)
    size = count * SUB
    lane = lax.broadcasted_iota(jnp.int32, (SUB, size), 1)
    sub = lax.broadcasted_iota(jnp.int32, (SUB, size), 0)
    spread_lane = lambda array, column: jnp.broadcast_to(array[:, column : column + 1], (SUB, size))
    line = lambda array, row: jnp.broadcast_to(array[row : row + 1, :], (SUB, size))
    def less(old, left, right):
        terms = [x * y for x, y in zip(left, right)]
        while len(terms) > 1:
            terms = [x + y for x, y in zip(terms[::2], terms[1::2])]
        return old - terms[0]

    for k in range(count):
        base = k * SUB
        inside = (lane >= base) & (lane < base + SUB)
        columns = [spread_lane(rows[k], base + j) for j in range(SUB)]
        work = jnp.where(inside, jnp.where(lane - base == sub, 1.0, 0.0), rows[k])
        full = columns + [work]
        bare = list(full)
        for j in range(0, SUB, 2):
            first, second = full[j], full[j + 1]
            a, b, c, d = line(bare[j], j), line(bare[j + 1], j), line(bare[j], j + 1), line(bare[j + 1], j + 1)
            inverse = 1.0 / (a * d - b * c)
            for i in range(j + 2, len(full)):
                upper, lower = line(bare[i], j), line(bare[i], j + 1)
                new_upper = (d * upper - b * lower) * inverse
                new_lower = (a * lower - c * upper) * inverse
                bare[i] = full[i] - (first * new_upper + second * new_lower)
                full[i] = jnp.where(sub == j, new_upper, jnp.where(sub == j + 1, new_lower, bare[i]))
        work = full[SUB]
        lines = [line(work, j) for j in range(SUB)]
        updated = list(rows)
        updated[k] = work
        for i in list(range(k + 1, count)) + list(range(k)):
            factors = [spread_lane(rows[i], base + j) for j in range(SUB)]
            updated[i] = less(jnp.where(inside, 0.0, rows[i]), factors, lines)
        rows = updated
        yield
    return jnp.concatenate(rows, axis=0)


def inverse_beside(block, work=()):
    work = list(work)
    groups = invert_block([block[i : i + SUB, :] for i in range(0, block.shape[0], SUB)])
    while True:
        try:
            next(groups)
        except StopIteration as stop:
            for piece in work:
                piece()
            return stop.value
        if work:
            work.pop(0)()


def sweep_kernel(panel, h_ref, inverse_ref, out_ref, next_ref, beside=()):
    size = h_ref.shape[0]
    at = slice(panel * PANEL, (panel + 1) * PANEL)
    after = slice(at.stop, at.stop + PANEL)
    wide, after_wide = (slice(x.start // 128 * 128, x.start // 128 * 128 + 128) for x in (at, after))
    offset = at.start - wide.start
    inverse = inverse_ref[...]
    split_inverse = halves(inverse)
    blank = jnp.zeros((PANEL, 1), F32)

    def pad(array):
        zeros = jnp.broadcast_to(blank, array.shape)
        return jnp.concatenate([array if i == offset else zeros for i in range(0, 128, PANEL)], axis=0)

    near = pad(product(split_inverse, halves(h_ref[at, after_wide]), NN))
    block = h_ref[after, after_wide] - product(halves(h_ref[after, wide]), halves(near), NN)
    block = block[:, after.start - after_wide.start :][:, :PANEL]

    turned = product(split_inverse, halves(h_ref[at, :]), NN)
    padded = pad(turned)
    split = halves(padded)
    columns = padded.T
    lane = lax.broadcasted_iota(jnp.int32, (128, 128), 1)
    inside = (lane >= offset) & (lane < offset + PANEL)

    def rows_update(i):
        def piece():
            rows = slice(i, i + 128)
            old = h_ref[rows, :]
            out_ref[rows, :] = old - product(halves(h_ref[rows, wide]), split, NN)
            out_ref[rows, wide] = jnp.where(inside, columns[rows, :], out_ref[rows, wide])
            if i == wide.start:
                out_ref[at, :] = turned
                out_ref[at, at] = -inverse

        return piece

    next_ref[...] = inverse_beside(block, list(beside) + [rows_update(i) for i in range(0, size, 128)])


def last_sweep_kernel(panel, shard_ref, h_ref, inverse_ref, high_ref, low_ref, own_ref, other_ref, out_ref, next_ref, yt_ref, cross_ref):
    def target():
        rows, lanes = own_ref.shape[0] // 2, own_ref.shape[1]
        place = shard_ref[0] % 4
        for s, ref in ((1, own_ref), (3, own_ref), (0, other_ref), (2, other_ref)):
            half = s // 2
            yt_ref[:, aligned(place ^ s, lanes)] = means(ref[half * rows : (half + 1) * rows, :])

    def cross():
        cross_ref[...] = product(halves(yt_ref[...]), (high_ref[...], low_ref[...]), NT)

    sweep_kernel(panel, h_ref, inverse_ref, out_ref, next_ref, (target, cross))


def fit_kernel(swept_ref, inverse_ref, high_ref, low_ref, yt_ref, cross_ref, x_ref, err_ref):
    target, cross = yt_ref[...], cross_ref[...]
    attend = high_ref[...], low_ref[...]
    size = swept_ref.shape[0]
    last = slice(size - PANEL, size)
    first = product(halves(jnp.concatenate([cross[:, : last.start], jnp.zeros_like(cross[:, last])], axis=1)), halves(swept_ref[...]), NN)
    rest = product(halves(cross[:, last] - first[:, last]), halves(inverse_ref[...]), NN)
    others = first + product(halves(rest), halves(swept_ref[last, :]), NN)
    fitted = jnp.concatenate([-others[:, : last.start], rest], axis=1)
    x_ref[...] = fitted
    misfit = product(halves(fitted), attend, NN) - target
    error = jnp.sum(misfit * misfit) / jnp.sum(target * target)
    err_ref[...] = jnp.full(err_ref.shape, error, F32)


def flip_kernel(x_ref, out_ref):
    out_ref[...] = x_ref[...].T


def mean_kernel(heads, *refs):
    total = refs[0][:1, :1]
    for ref in refs[1:-1]:
        total = total + ref[:1, :1]
    refs[-1][...] = total / heads


def per_device(queries, keys, values, kept, roots):
    rows, dims = queries.shape[2:]
    slab, count = keys.shape[1], kept.shape[1]
    lanes = rows // 4
    score_scale = 1.0 / math.sqrt(dims)
    shard = lax.axis_index("ctx").astype(jnp.int32).reshape(1)

    attend_to = functools.partial(attention, lanes, score_scale)
    near, far, other, keep, came = spread(shard, queries[0, 0], kept, keys[0], roots, values[0], attend_to)
    rounds = target_rounds(keep, came)
    came = next(rounds)
    ends = None

    def beside(arrays):
        nonlocal came, ends
        if ends is None:
            arrays, came = lax.optimization_barrier((arrays, came))
            try:
                came = rounds.send(came)
            except StopIteration as stop:
                ends = stop.value
        return arrays

    system_shape = ((count, count), F32)
    attend = call(
        functools.partial(attend_kernel, score_scale),
        (shard, near, far, other),
        [((count, rows), BF16)] * 2 + [((4 * SUB, lanes), F32)],
        10**6,
        scratch=[pltpu.VMEM((count, dims), BF16)],
        name="attend",
    )
    attend = beside(attend)
    panels = count // PANEL
    block_shape = ((PANEL, PANEL), F32)
    system, inverse = call(gram_kernel, attend, [system_shape, block_shape], 4 * 10**9, name="gram")
    for panel in range(panels - 2):
        system, inverse = call(
            functools.partial(sweep_kernel, panel),
            (system, inverse),
            [system_shape, block_shape],
            2 * 10**9,
            name="sweep",
        )
        if panel in (0, 2, 4, 5):
            system, inverse = beside((system, inverse))
    while ends is None:
        system = beside(system)
    system, inverse, target, cross = call(
        functools.partial(last_sweep_kernel, panels - 2),
        (shard, system, inverse, *attend[:2], *ends),
        [system_shape, block_shape, ((dims, rows), F32), ((dims, count), F32)],
        2 * 10**9,
        name="last_sweep",
    )
    turned_fit, error = call(
        fit_kernel,
        (system, inverse, *attend[:2], target, cross),
        [((dims, count), F32), ((SUB, 128), F32)],
        10**9,
        name="fit",
    )
    heads = lax.axis_size("head")
    errors, step = [error], 1
    while step < heads:
        if len(errors) > 1:
            errors = list(call(sum_kernel, errors, [((SUB, 128), F32)], name="total"))
        errors.append(swap(errors[0], "head", step))
        step *= 2
    (compact,) = call(flip_kernel, (turned_fit,), [((count, dims), F32)], 10**6, name="flip")
    (error,) = call(functools.partial(mean_kernel, heads), errors, [((1, 1), F32)], name="mean")
    return (compact[None], error.reshape(()))


def solution(mesh):
    placed = (
        P("head", "ctx", None, None),
        P("head", "ctx", None),
        P("head", "ctx", None),
        P("head", None),
        P("head"),
    )
    return jax.shard_map(
        per_device,
        mesh=mesh,
        in_specs=placed,
        out_specs=(P("head", None, None), P()),
        check_vma=False,
    )
```
